32 devices in a mesh: fsdp: 16 (over z, y, core), ctx: 2 (over x).
Axes of the slice: x: 2, y: 2, z: 4, core: 2. Of those that a mesh axis runs over, the one named last changes fastest.
Arguments:
- hidden: bfloat16 [16, 512, 5120], P('fsdp', 'ctx'), may hold values from -6 to 6
- queries: bfloat16 [16, 512, 4096], P('fsdp', 'ctx'), may hold values from -300 to 300, as said below
- norm_gain: float32 [5120], replicated, may hold values from 0.1 to 1.9
- key_gain: float32 [128], replicated, may hold values from 0.1 to 1.9
- k_weight: bfloat16 [5120, 512], P('fsdp'), may hold values from -0.078125 to 0.078125
- v_weight: bfloat16 [5120, 512], P('fsdp'), may hold values from -0.078125 to 0.078125
- segment: int32 [16, 512], P('fsdp', 'ctx'), may hold values from 0 to 3, as said below
- position: int32 [16, 512], P('fsdp', 'ctx'), may hold values from 0 to 8191, as said below
Outputs:
- attended: bfloat16 [16, 512, 4096], P('fsdp', 'ctx')
The draws below stay inside these ranges and needn't reach their ends.
Inputs may be any that keep to these rules, and one draw needn't show every extreme that they name: queries keep to the stated range. `segment`: in each stretch, read in the tokens' order, rollout numbers never fall; the tokens of a stretch lie in its slots in an order that keeps 256 slots on each index of ctx, one token of every 2 consecutive ones on each. `position`: within one rollout of a stretch positions rise by one from token to token.
All inputs are finite; a program needn't handle non-finite values.
Results may differ from the reference program's by a relative error of at most 0.0075.
The reference program's roundings to bfloat16 on the way (of `normed`, `values`, `keys` and `rounded`) count: a program that leaves them out, or rounds other values in their place, can miss the bound.
Values may be sent and summed in bfloat16 or wider, within the bound.
No kernel may reach another device: no remote copies, remote signals or barrier semaphores. Data moves between devices by JAX's collectives and lax.ppermute only.
A program may use at most 192 MiB of HBM per device.

```python
import math
import jax
import jax.numpy as jnp
from jax import lax

D = 5120
QH = 32
KVH = 4
HD = 128
TOK_DEV = 256
G = 8
LEN = 512
STRETCHES = 16


def layout(key):

    def one_stretch(sub):
        first, second, third = jax.random.split(sub, 3)
        cuts = jnp.sort(jax.random.randint(first, (3,), 1, LEN)).astype(jnp.int32)
        places = jnp.arange(LEN, dtype=jnp.int32)
        seg_tok = jnp.sum((places[:, None] >= cuts[None, :]).astype(jnp.int32), axis=1).astype(jnp.int32)
        starts = jnp.concatenate([jnp.zeros((1,), jnp.int32), cuts])
        bases = jax.random.randint(second, (4,), 0, 8192 - LEN + 1).astype(jnp.int32)
        bases = bases.at[0].set(0)
        bases = bases.at[3].set(8191 - (LEN - 1 - starts[3]))
        pos_tok = bases[seg_tok] + places - starts[seg_tok]
        groups = LEN // TOK_DEV
        orders = jax.vmap(lambda item: jax.random.permutation(item, groups))(jax.random.split(third, TOK_DEV))
        token_of_slot = (jnp.arange(TOK_DEV, dtype=jnp.int32)[None, :] * groups + orders.T.astype(jnp.int32)).reshape(LEN)
        return (seg_tok[token_of_slot], pos_tok[token_of_slot])
    return jax.vmap(one_stretch)(jax.random.split(key, STRETCHES))


def draw_segment(key, part):
    return layout(key)[0]


def draw_position(key, part):
    return layout(key)[1]


def draw_queries(key, part):
    key = jax.random.fold_in(key, 7)
    first = jax.random.fold_in(key, 0)
    values_out = jnp.clip(jax.random.normal(first, (STRETCHES, LEN, QH, HD), jnp.float32), -6.0, 6.0)
    return values_out.reshape(STRETCHES, LEN, QH * HD).astype(jnp.bfloat16)


def block_levels(key, dims, pieces, low, high):
    level, own = 1.0, jax.random.fold_in(key, 6)
    for axis_at, shards_of in pieces:
        heights = jnp.exp(jax.random.uniform(jax.random.fold_in(own, axis_at), (shards_of,), jnp.float32, low / len(pieces), high / len(pieces)))
        level = level * jnp.repeat(heights, dims[axis_at] // shards_of).reshape([-1 if axis == axis_at else 1 for axis in range(len(dims))])
    return level


def normal_values(key, dims, scale, bound, shards=(), held_as=jnp.bfloat16):
    level = block_levels(key, dims, shards, -0.22, 0.18) if shards else 1.0
    values = jax.random.normal(key, dims, jnp.float32) * scale * level
    return jnp.minimum(jnp.maximum(values, -bound), bound).astype(held_as)


def setup_inputs(seed: int = 0) -> dict:
    arg_keys = jax.random.split(jax.random.key(seed), 9)
    hidden = normal_values(arg_keys[0], (STRETCHES, LEN, D), 1.0, 6.0, ((0, 16), (1, 2)))
    queries = draw_queries(jax.random.fold_in(arg_keys[8], 71), 0)
    norm_gain = jnp.clip(1.0 + 0.18 * jax.random.normal(arg_keys[2], (D,), jnp.float32), 0.1, 1.9)
    key_gain = jnp.clip(1.0 + 0.18 * jax.random.normal(arg_keys[3], (HD,), jnp.float32), 0.1, 1.9)
    k_weight = normal_values(arg_keys[4], (D, KVH * HD), D ** -0.5, 0.078125, ((0, 16),))
    v_weight = normal_values(arg_keys[5], (D, KVH * HD), D ** -0.5, 0.078125, ((0, 16),))
    segment = draw_segment(jax.random.fold_in(arg_keys[8], 71), 0)
    position = draw_position(jax.random.fold_in(arg_keys[8], 71), 0)
    return dict(hidden=hidden, queries=queries, norm_gain=norm_gain, key_gain=key_gain, k_weight=k_weight, v_weight=v_weight, segment=segment, position=position)


EPS = 1e-06
THETA = 1000000.0

def rotate(values_in, where):
    width = values_in.shape[-1]
    half = width // 2
    freq = jnp.exp(jnp.arange(half, dtype=jnp.float32) * (-2.0 * math.log(THETA) / width))
    angle = where.astype(jnp.float32)[:, None] * freq[None, :]
    cosine = jnp.cos(angle)[:, None, :]
    sine = jnp.sin(angle)[:, None, :]
    first = values_in[..., :half]
    second = values_in[..., half:]
    return jnp.concatenate([first * cosine - second * sine, second * cosine + first * sine], axis=-1)

def stretch(args, norm_gain, key_gain, k_weight, v_weight):
    hidden_rows, query_rows, seg_rows, pos_rows = args
    inputs = hidden_rows.astype(jnp.float32)
    normed = (inputs * lax.rsqrt(lax.optimization_barrier(jnp.mean(inputs * inputs, axis=-1, keepdims=True)) + EPS) * norm_gain).astype(jnp.bfloat16)
    key_sums = jnp.dot(normed, k_weight, preferred_element_type=jnp.float32)
    value_sums = jnp.dot(normed, v_weight, preferred_element_type=jnp.float32)
    values = value_sums.reshape(LEN, KVH, HD).astype(jnp.bfloat16)
    raw = key_sums.reshape(LEN, KVH, HD)
    normk = raw * lax.rsqrt(lax.optimization_barrier(jnp.mean(raw * raw, axis=-1, keepdims=True)) + EPS) * key_gain
    keys = rotate(normk, pos_rows).astype(jnp.bfloat16)
    block = math.gcd(LEN, 512)
    count = LEN // block
    grouped = query_rows.reshape(count, block, KVH, G, HD)
    seg_blocks = seg_rows.reshape(count, block)
    pos_blocks = pos_rows.reshape(count, block)
    scale = 1.0 / math.sqrt(HD)
    keys_wide = keys.astype(jnp.float32)
    values_wide = values.astype(jnp.float32)

    def one_block(piece):
        query_block, seg_block, pos_block = piece
        scores = jnp.einsum('tkgd,skd->kgts', query_block.astype(jnp.float32), keys_wide) * scale
        allowed = (seg_rows[None, :] == seg_block[:, None]) & (pos_rows[None, :] <= pos_block[:, None])
        scores = jnp.where(allowed, scores, -1e+30)
        top = lax.optimization_barrier(jnp.max(scores, axis=-1, keepdims=True))
        weights = jnp.where(allowed, jnp.exp(scores - top), 0.0)
        total = lax.optimization_barrier(jnp.sum(weights, axis=-1))
        rounded = weights.astype(jnp.bfloat16)
        summed = jnp.einsum('kgts,skd->kgtd', rounded.astype(jnp.float32), values_wide)
        result = summed / total[..., None]
        return jnp.transpose(result, (2, 0, 1, 3)).reshape(block, QH * HD).astype(jnp.bfloat16)
    return lax.map(one_block, (grouped, seg_blocks, pos_blocks)).reshape(LEN, QH * HD)

def reference(hidden, queries, norm_gain, key_gain, k_weight, v_weight, segment, position):
    return lax.map(lambda args: stretch(args, norm_gain, key_gain, k_weight, v_weight), (hidden, queries, segment, position))
```

```python
import functools
import math

import jax
import jax.numpy as jnp
from jax import lax
from jax.experimental import pallas as pl
from jax.experimental.pallas import tpu as pltpu
from jax.sharding import PartitionSpec as P

KVH = 4
HD = 128
G = 8
EPS = 1e-06
THETA = 1000000.0
MASKED = -1e30
VMEM_LIMIT = 48 * 2**20
AXES = ("fsdp", "ctx")


def project_kernel(chips_z, count, place, own, other, cosine, sine, gain, *rest):
    pieces, (kv_own, kv_other, weight, acc, sems) = rest[: 5 * chips_z], rest[5 * chips_z :]
    z, y, x = place[0], place[1], place[2]
    rows = weight.shape[2]
    copies = []
    for k in range(chips_z):
        p = lax.rem(z - k + chips_z, chips_z)
        near, far = p * 2 + y, p * 2 + 1 - y
        mine, across, beside, top, bottom = pieces[5 * k : 5 * k + 5]
        targets = (
            (mine, weight.at[near, x]),
            (across, weight.at[near, 1 - x]),
            (beside, weight.at[far, x]),
            (top, weight.at[far, 1 - x, pl.ds(0, rows // 2)]),
            (bottom, weight.at[far, 1 - x, pl.ds(rows // 2, rows // 2)]),
        )
        started = []
        for i, (source, target) in enumerate(targets):
            copy = pltpu.make_async_copy(source, target, sems.at[k, i])
            copy.start()
            started.append(copy)
        copies.append((near, started[:2]))
        copies.append((far, started[2:]))
    for step, (chunk, waits) in enumerate(copies):
        for copy in waits:
            copy.wait()
        for half in range(2):
            for part, lhs in enumerate((own, other)):
                term = jnp.dot(
                    lhs[chunk], weight[chunk, half], preferred_element_type=jnp.float32
                )
                at = pl.ds(part * count, count)
                if step == 0:
                    acc[half, at, :] = term
                else:
                    acc[half, at, :] += term
    for half in range(2):
        for part, out in enumerate((kv_own, kv_other)):
            at = pl.ds(part * count, count)
            raw = acc[half, at, :HD]
            normk = raw * lax.rsqrt(jnp.mean(raw * raw, axis=-1, keepdims=True) + EPS) * gain[...]
            turned = normk * cosine[at, :] + pltpu.roll(normk, HD // 2, 1) * sine[at, :]
            out[:, half * 2 * HD : half * 2 * HD + HD] = turned.astype(jnp.bfloat16)
            out[:, half * 2 * HD + HD : (half + 1) * 2 * HD] = acc[half, at, HD:].astype(
                jnp.bfloat16
            )


def attend_kernel(pieces, count, place, queries, seg_q, pos_q, seg_k, pos_k, *rest):
    sources, (out, bias, keys, values) = rest[: 2 * pieces], rest[2 * pieces :]
    step = pl.program_id(0)

    @pl.when(step == 0)
    def _():
        allowed = (seg_k[...] == seg_q[...]) & (pos_k[...] <= pos_q[...])
        bias[...] = jnp.where(allowed, 0.0, MASKED)

    for at in range(KVH):

        @pl.when(step == at)
        def _():
            left = (at % 2) * 2 * HD
            for i in range(pieces):
                source = sources[(at // 2) * pieces + i]
                keys[i * count : (i + 1) * count, :] = source[:, left : left + HD]
                values[i * count : (i + 1) * count, :] = source[:, left + HD : left + 2 * HD]

    factor = math.log2(math.e) / math.sqrt(HD)
    for g in range(G):
        part = slice(g * HD, (g + 1) * HD)
        scores = lax.dot_general(
            queries[:, part], keys[...], (((1,), (1,)), ((), ())),
            preferred_element_type=jnp.float32,
        ) + bias[...]
        top = jnp.max(scores, axis=-1, keepdims=True)
        weights = jnp.exp2((scores - top) * factor)
        total = jnp.sum(weights, axis=-1, keepdims=True)
        summed = jnp.dot(
            weights.astype(jnp.bfloat16), values[...], preferred_element_type=jnp.float32
        )
        out[:, part] = (summed * (1.0 / total)).astype(jnp.bfloat16)


def on_device(
    n, m, hidden, queries, norm_gain, key_gain, k_weight, v_weight, segment, position
):
    count, width = hidden.shape[1:]
    rows = 2 * k_weight.shape[0]
    chips_z = n // 4
    chunks = n // 2
    mine_f, mine_c = lax.axis_index("fsdp"), lax.axis_index("ctx")
    z, y, core, x = mine_f // 4, (mine_f // 2) % 2, mine_f % 2, mine_c % 2

    def send(array, move):
        pairs = []
        for f in range(n):
            for c in range(m):
                g, d = move(f, c)
                pairs.append((f * m + c, (g % n) * m + d % m))
        return lax.ppermute(array, AXES, pairs)

    def to_core(array):
        return send(array, lambda f, c: (f ^ 1, c))

    def to_y(array):
        return send(array, lambda f, c: (f ^ 2, c))

    def to_x(array):
        return send(array, lambda f, c: (f, c ^ 1))

    def to_z(array, k):
        return send(array, lambda f, c: (f + 4 * k, c))

    both = jnp.concatenate(
        [k_weight.reshape(-1, KVH, HD), v_weight.reshape(-1, KVH, HD)], axis=2
    ).reshape(-1, 2, 4 * HD)
    kept = jnp.where(core == 0, both[:, 0], both[:, 1])
    given = jnp.where(core == 0, both[:, 1], both[:, 0])
    taken = to_core(given)
    chip = jnp.where(
        core == 0, jnp.concatenate([kept, taken]), jnp.concatenate([taken, kept])
    )
    first, second = chip[:, : 2 * HD], chip[:, 2 * HD :]
    half_x = jnp.where(x == 0, first, second)
    half_o = jnp.where(x == 0, second, first)

    inputs = hidden[0].astype(jnp.float32)
    normed = (
        inputs * lax.rsqrt(jnp.mean(inputs * inputs, axis=-1, keepdims=True) + EPS) * norm_gain
    ).astype(jnp.bfloat16)
    normed = normed.reshape(count, chunks, rows).transpose(1, 0, 2)
    normed_other = to_core(normed)

    ints = jnp.concatenate([segment, position])
    ints_all = [ints] + [send(ints, lambda f, c, d=d: (f, c + d)) for d in range(1, m)]
    position_other = to_core(position)
    where = jnp.concatenate([position[0], position_other[0]]).astype(jnp.float32)
    half = HD // 2
    freq = jnp.exp(jnp.arange(half, dtype=jnp.float32) * (-2.0 * math.log(THETA) / HD))
    angle = where[:, None] * freq[None, :]
    cosine, sine = jnp.cos(angle), jnp.sin(angle)
    cosine = jnp.concatenate([cosine, cosine], axis=1)
    sine = jnp.concatenate([-sine, sine], axis=1)

    pieces = []
    mine = [half_x] + [to_z(half_x, k) for k in range(1, chips_z)]
    for k in range(chips_z):
        beside = to_y(mine[k])
        if k == 0:
            across = half_o
            top, bottom = to_x(beside[: rows // 2]), to_x(beside[rows // 2 :])
        else:
            across = to_x(mine[k])
            top, bottom = to_x(beside[: rows // 2]), to_y(across[rows // 2 :])
        pieces += [mine[k], across, beside, top, bottom]

    place = jnp.stack([z, y, x]).astype(jnp.int32)
    smem = pl.BlockSpec(memory_space=pltpu.SMEM)
    vmem = pl.BlockSpec(memory_space=pltpu.VMEM)
    anywhere = pl.BlockSpec(memory_space=pl.ANY)
    kv_own, kv_other = pl.pallas_call(
        functools.partial(project_kernel, chips_z, count),
        out_shape=[jax.ShapeDtypeStruct((count, 4 * HD), jnp.bfloat16)] * 2,
        in_specs=[smem] + [vmem] * 5 + [anywhere] * len(pieces),
        out_specs=[vmem] * 2,
        scratch_shapes=[
            pltpu.VMEM((chunks, 2, rows, 2 * HD), jnp.bfloat16),
            pltpu.VMEM((2, 2 * count, 2 * HD), jnp.float32),
            pltpu.SemaphoreType.DMA((chips_z, 5)),
        ],
        compiler_params=pltpu.CompilerParams(vmem_limit_bytes=VMEM_LIMIT),
        cost_estimate=pl.CostEstimate(
            flops=2 * 2 * count * width * 4 * HD,
            bytes_accessed=2 * width * (2 * count + 4 * HD),
            transcendentals=0,
        ),
        name="project",
    )(place, normed, normed_other, cosine, sine, key_gain[None], *pieces)

    sources = [kv_own] + [send(kv_own, lambda f, c, d=d: (f, c + d)) for d in range(1, m)]
    sources += [send(kv_other, lambda f, c, d=d: (f ^ 1, c + d)) for d in range(m)]
    seg_k = jnp.concatenate([piece[:1] for piece in ints_all], axis=1)
    pos_k = jnp.concatenate([piece[1:] for piece in ints_all], axis=1)

    def block(step, place):
        return (0, lax.rem(step + 2 * place[0], KVH))

    whole = pl.BlockSpec(memory_space=pltpu.VMEM)
    result = pl.pallas_call(
        functools.partial(attend_kernel, m, count),
        out_shape=jax.ShapeDtypeStruct((count, KVH * G * HD), jnp.bfloat16),
        grid_spec=pltpu.PrefetchScalarGridSpec(
            num_scalar_prefetch=1,
            grid=(KVH,),
            in_specs=[pl.BlockSpec((count, G * HD), block)] + [whole] * (4 + 2 * m),
            out_specs=pl.BlockSpec((count, G * HD), block),
            scratch_shapes=[
                pltpu.VMEM((count, m * count), jnp.float32),
                pltpu.VMEM((m * count, HD), jnp.bfloat16),
                pltpu.VMEM((m * count, HD), jnp.bfloat16),
            ],
        ),
        compiler_params=pltpu.CompilerParams(vmem_limit_bytes=VMEM_LIMIT),
        cost_estimate=pl.CostEstimate(
            flops=4 * count * m * count * KVH * G * HD,
            bytes_accessed=4 * count * KVH * G * HD,
            transcendentals=count * m * count * KVH * G,
        ),
        name="attend",
    )(
        core.astype(jnp.int32)[None],
        queries[0],
        segment.reshape(count, 1),
        position.reshape(count, 1),
        seg_k,
        pos_k,
        *sources,
    )
    return result[None]


def solution(mesh):
    placed = (
        P("fsdp", "ctx", None),
        P("fsdp", "ctx", None),
        P(),
        P(),
        P("fsdp", None),
        P("fsdp", None),
        P("fsdp", "ctx"),
        P("fsdp", "ctx"),
    )
    return jax.shard_map(
        functools.partial(on_device, mesh.shape["fsdp"], mesh.shape["ctx"]),
        mesh=mesh,
        in_specs=placed,
        out_specs=P("fsdp", "ctx", None),
        check_vma=False,
    )
```

```python
import functools
import math

import jax
import jax.numpy as jnp
import numpy as np
from jax import lax
from jax.experimental import pallas as pl
from jax.experimental.pallas import tpu as pltpu
from jax.sharding import Mesh
from jax.sharding import PartitionSpec as P

KVH = 4
HD = 128
G = 8
EPS = 1e-06
THETA = 1000000.0
MASKED = -1e30
VMEM_LIMIT = 48 * 2**20


def project_kernel(count, own, other, weight, cosine, sine, gain, kv_own, kv_other, acc):
    step = pl.program_id(0)
    for part, lhs in enumerate((own, other)):
        at = pl.ds(part * count, count)
        for half in range(2):
            term = jnp.dot(
                lhs[step], weight[0, half], preferred_element_type=jnp.float32
            )

            @pl.when(step == 0)
            def _():
                acc[half, at, :] = term

            @pl.when(step > 0)
            def _():
                acc[half, at, :] += term

    @pl.when(step == pl.num_programs(0) - 1)
    def _():
        for part, out in enumerate((kv_own, kv_other)):
            at = pl.ds(part * count, count)
            raw = acc[0, at, :]
            normk = raw * lax.rsqrt(jnp.mean(raw * raw, axis=-1, keepdims=True) + EPS) * gain[...]
            turned = normk * cosine[at, :] + pltpu.roll(normk, HD // 2, 1) * sine[at, :]
            out[:, :HD] = turned.astype(jnp.bfloat16)
            out[:, HD:] = acc[1, at, :].astype(jnp.bfloat16)


def attend_kernel(pieces, count, place, queries, seg_q, pos_q, seg_k, pos_k, *rest):
    sources, (out, bias, keys, values) = rest[: 2 * pieces], rest[-4:]
    step = pl.program_id(0)

    @pl.when(step == 0)
    def _():
        allowed = (seg_k[...] == seg_q[...]) & (pos_k[...] <= pos_q[...])
        bias[...] = jnp.where(allowed, 0.0, MASKED)

    for at in range(2):

        @pl.when(step == at)
        def _():
            for i in range(pieces):
                source = sources[at * pieces + i]
                keys[i * count : (i + 1) * count, :] = source[:, :HD]
                values[i * count : (i + 1) * count, :] = source[:, HD:]

    factor = math.log2(math.e) / math.sqrt(HD)
    for g in range(G):
        part = slice(g * HD, (g + 1) * HD)
        scores = lax.dot_general(
            queries[:, part], keys[...], (((1,), (1,)), ((), ())),
            preferred_element_type=jnp.float32,
        ) + bias[...]
        top = jnp.max(scores, axis=-1, keepdims=True)
        weights = jnp.exp2((scores - top) * factor)
        total = jnp.sum(weights, axis=-1, keepdims=True)
        summed = jnp.dot(
            weights.astype(jnp.bfloat16), values[...], preferred_element_type=jnp.float32
        )
        out[:, part] = (summed * (1.0 / total)).astype(jnp.bfloat16)


def swap(array, axis):
    return lax.ppermute(array, axis, [(0, 1), (1, 0)])


def on_device(
    sizes, hidden, queries, norm_gain, key_gain, k_weight, v_weight, segment, position
):
    chips_z, groups = sizes[0], sizes[3]
    count, width = hidden.shape[1:]
    own_rows = k_weight.shape[0]
    rows = 2 * own_rows
    chunks = 2 * chips_z
    m = 2 * groups
    core, x = lax.axis_index("core"), lax.axis_index("x")
    bf16 = jnp.bfloat16

    def along_ctx(array, d, cross=False):
        pairs = []
        for c in range(2):
            for i in range(m):
                pairs.append((c * m + i, (c ^ int(cross)) * m + (i + d) % m))
        return lax.ppermute(array, ("core", "ctx", "x"), pairs)

    def columns(which):
        at = which * 2 * HD
        return jnp.stack(
            [lax.dynamic_slice_in_dim(w, at, 2 * HD, 1) for w in (k_weight, v_weight)]
        )

    taken = swap(columns(1 - core), "core")
    kept = columns(core)
    chip = lax.dynamic_update_slice(
        jnp.zeros((2, rows, 2 * HD), bf16), kept, (0, core * own_rows, 0)
    )
    chip = lax.dynamic_update_slice(chip, taken, (0, (1 - core) * own_rows, 0))
    mine = lax.dynamic_index_in_dim(chip, x, 0, keepdims=False)
    gathered = [
        lax.all_gather(mine[:, s * HD : (s + 1) * HD], ("z", "y", "x")).reshape(
            chunks, 2, rows, HD
        )
        for s in range(2)
    ]

    hidden, taken = lax.optimization_barrier((hidden, taken))
    inputs = hidden[0].astype(jnp.float32)
    normed = (
        inputs * lax.rsqrt(jnp.mean(inputs * inputs, axis=-1, keepdims=True) + EPS) * norm_gain
    ).astype(bf16)
    normed = normed.reshape(count, chunks, rows).transpose(1, 0, 2)
    normed_other = swap(normed, "core")

    ints = jnp.concatenate([segment, position])
    ints_all = [ints] + [along_ctx(ints, d) for d in range(1, m)]
    where = jnp.concatenate([position[0], swap(position, "core")[0]]).astype(jnp.float32)
    half = HD // 2
    freq = np.exp(np.arange(half, dtype=np.float32) * np.float32(-2.0 * math.log(THETA) / HD))
    angle = where[:, None] * freq[None, :]
    cosine, sine = jnp.cos(angle), jnp.sin(angle)
    cosine = jnp.concatenate([cosine, cosine], axis=1)
    sine = jnp.concatenate([-sine, sine], axis=1)
    seg_k = jnp.concatenate([piece[:1] for piece in ints_all], axis=1)
    pos_k = jnp.concatenate([piece[1:] for piece in ints_all], axis=1)

    whole = pl.BlockSpec(memory_space=pltpu.VMEM)
    place = core.astype(jnp.int32)[None]
    params = pltpu.CompilerParams(vmem_limit_bytes=VMEM_LIMIT)
    result = None
    for s in range(2):
        kv_own, kv_other = pl.pallas_call(
            functools.partial(project_kernel, count),
            out_shape=[jax.ShapeDtypeStruct((count, 2 * HD), bf16)] * 2,
            grid=(chunks,),
            in_specs=[
                whole,
                whole,
                pl.BlockSpec((1, 2, rows, HD), lambda i: (i, 0, 0, 0)),
                whole,
                whole,
                whole,
            ],
            out_specs=[whole] * 2,
            scratch_shapes=[pltpu.VMEM((2, 2 * count, HD), jnp.float32)],
            compiler_params=params,
            cost_estimate=pl.CostEstimate(
                flops=2 * 2 * count * width * 2 * HD,
                bytes_accessed=2 * width * (2 * count + 2 * HD),
                transcendentals=0,
            ),
            name="project",
        )(normed, normed_other, gathered[s], cosine, sine, key_gain[None])

        sources = [kv_own] + [along_ctx(kv_own, d) for d in range(1, m)]
        sources += [along_ctx(kv_other, d, True) for d in range(m)]

        def block(step, place, s=s):
            return (0, lax.rem(place[0] + step, 2) * 2 + s)

        earlier = [] if result is None else [result]
        result = pl.pallas_call(
            functools.partial(attend_kernel, m, count),
            out_shape=jax.ShapeDtypeStruct((count, KVH * G * HD), bf16),
            grid_spec=pltpu.PrefetchScalarGridSpec(
                num_scalar_prefetch=1,
                grid=(2,),
                in_specs=[pl.BlockSpec((count, G * HD), block)]
                + [whole] * (4 + 2 * m)
                + [pl.BlockSpec(memory_space=pl.ANY)] * len(earlier),
                out_specs=pl.BlockSpec((count, G * HD), block),
                scratch_shapes=[
                    pltpu.VMEM((count, m * count), jnp.float32),
                    pltpu.VMEM((m * count, HD), bf16),
                    pltpu.VMEM((m * count, HD), bf16),
                ],
            ),
            input_output_aliases={6 + 2 * m: 0} if earlier else {},
            compiler_params=params,
            cost_estimate=pl.CostEstimate(
                flops=2 * count * m * count * KVH * G * HD,
                bytes_accessed=2 * count * KVH * G * HD,
                transcendentals=count * m * count * KVH * G // 2,
            ),
            name="attend",
        )(
            place,
            queries[0],
            segment.reshape(count, 1),
            position.reshape(count, 1),
            seg_k,
            pos_k,
            *sources,
            *earlier,
        )
    return result[None]


def solution(mesh):
    n, m = mesh.shape["fsdp"], mesh.shape["ctx"]
    sizes = (n // 4, 2, 2, m // 2, 2)
    fine = Mesh(mesh.devices.reshape(sizes), ("z", "y", "core", "ctx", "x"))
    fsdp, ctx = ("z", "y", "core"), ("ctx", "x")
    placed = (
        P(fsdp, ctx, None),
        P(fsdp, ctx, None),
        P(),
        P(),
        P(fsdp, None),
        P(fsdp, None),
        P(fsdp, ctx),
        P(fsdp, ctx),
    )
    return jax.shard_map(
        functools.partial(on_device, sizes),
        mesh=fine,
        in_specs=placed,
        out_specs=P(fsdp, ctx, None),
        check_vma=False,
    )
```

```python
import functools
import math

import jax
import jax.numpy as jnp
import numpy as np
from jax import lax
from jax.experimental import pallas as pl
from jax.experimental.pallas import tpu as pltpu
from jax.sharding import Mesh
from jax.sharding import PartitionSpec as P

KVH = 4
HD = 128
G = 8
EPS = 1e-06
THETA = 1000000.0
MASKED = -1e30
VMEM_LIMIT = 48 * 2**20
NORM_ROWS = 64


def norm_kernel(chunks, hidden, gain, out):
    inputs = hidden[...].astype(jnp.float32)
    scale = lax.rsqrt(jnp.mean(inputs * inputs, axis=-1, keepdims=True) + EPS)
    normed = (inputs * scale * gain[...]).astype(jnp.bfloat16)
    rows = normed.shape[1] // chunks
    for j in range(chunks):
        out[j] = normed[:, j * rows : (j + 1) * rows]


def project_kernel(chips_z, items, first, last, count, place, own, other, *rest):
    z, y, x = place[0], place[1], place[2]
    pieces, rest = rest[: len(items)], rest[len(items) :]
    earlier = None if first else rest[0]
    acc = rest[-1]
    for side in ("x", "o"):
        at = x if side == "x" else 1 - x
        term = None if first else earlier[at]
        for (k, kind), piece in zip(items, pieces):
            if (kind in ("mine", "beside")) != (side == "x"):
                continue
            p = lax.rem(z - k + chips_z, chips_z)
            chunk = p * 2 + (y if kind in ("mine", "across") else 1 - y)
            rows = jnp.concatenate([own[chunk], other[chunk]], axis=0)
            part = jnp.dot(rows, piece[...], preferred_element_type=jnp.float32)
            term = part if term is None else term + part
        acc[at] = term
    if not last:
        return
    cosine, sine, gain = rest[1:4]
    outs = rest[4:8]
    for head in range(2):
        columns = slice(head * HD, (head + 1) * HD)
        for part in range(2):
            at = slice(part * count, (part + 1) * count)
            out = outs[2 * head + part]
            raw = acc[0, at, columns]
            normk = raw * lax.rsqrt(jnp.mean(raw * raw, axis=-1, keepdims=True) + EPS) * gain[...]
            turned = normk * cosine[at, :] + pltpu.roll(normk, HD // 2, 1) * sine[at, :]
            out[:, :HD] = turned.astype(jnp.bfloat16)
            out[:, HD:] = acc[1, at, columns].astype(jnp.bfloat16)


def attend_kernel(pieces, count, place, queries, seg_q, pos_q, seg_k, pos_k, *rest):
    sources, (out, bias, keys, values) = rest[: 2 * pieces], rest[-4:]
    step = pl.program_id(0)

    @pl.when(step == 0)
    def _():
        allowed = (seg_k[...] == seg_q[...]) & (pos_k[...] <= pos_q[...])
        bias[...] = jnp.where(allowed, 0.0, MASKED)

    for at in range(2):

        @pl.when(step == at)
        def _():
            for i in range(pieces):
                source = sources[at * pieces + i]
                keys[i * count : (i + 1) * count, :] = source[:, :HD]
                values[i * count : (i + 1) * count, :] = source[:, HD:]

    factor = math.log2(math.e) / math.sqrt(HD)
    for g in range(G):
        part = slice(g * HD, (g + 1) * HD)
        scores = lax.dot_general(
            queries[:, part], keys[...], (((1,), (1,)), ((), ())),
            preferred_element_type=jnp.float32,
        ) + bias[...]
        top = jnp.max(scores, axis=-1, keepdims=True)
        weights = jnp.exp2((scores - top) * factor)
        total = jnp.sum(weights, axis=-1, keepdims=True)
        summed = jnp.dot(
            weights.astype(jnp.bfloat16), values[...], preferred_element_type=jnp.float32
        )
        out[:, part] = (summed * (1.0 / total)).astype(jnp.bfloat16)


def swap(array, axis):
    return lax.ppermute(array, axis, [(0, 1), (1, 0)])


def on_device(
    sizes, hidden, queries, norm_gain, key_gain, k_weight, v_weight, segment, position
):
    chips_z, groups = sizes[0], sizes[3]
    count, width = hidden.shape[1:]
    own_rows = k_weight.shape[0]
    rows = 2 * own_rows
    chunks = 2 * chips_z
    m = 2 * groups
    z, y = lax.axis_index("z"), lax.axis_index("y")
    core, x = lax.axis_index("core"), lax.axis_index("x")
    bf16 = jnp.bfloat16
    whole = pl.BlockSpec(memory_space=pltpu.VMEM)
    params = pltpu.CompilerParams(vmem_limit_bytes=VMEM_LIMIT)

    def along_ctx(array, d, cross=False):
        pairs = []
        for c in range(2):
            for i in range(m):
                pairs.append((c * m + i, (c ^ int(cross)) * m + (i + d) % m))
        return lax.ppermute(array, ("core", "ctx", "x"), pairs)

    def columns(which):
        at = which * 2 * HD
        return jnp.stack(
            [lax.dynamic_slice_in_dim(w, at, 2 * HD, 1) for w in (k_weight, v_weight)]
        )

    taken = swap(columns(1 - core), "core")
    kept = columns(core)
    chip = lax.dynamic_update_slice(
        jnp.zeros((2, rows, 2 * HD), bf16), kept, (0, core * own_rows, 0)
    )
    chip = lax.dynamic_update_slice(chip, taken, (0, (1 - core) * own_rows, 0))
    mine = [lax.dynamic_index_in_dim(chip, x, 0, keepdims=False)]
    across = [lax.dynamic_index_in_dim(chip, 1 - x, 0, keepdims=False)]
    hidden, mine[0], across[0] = lax.optimization_barrier((hidden, mine[0], across[0]))
    normed = pl.pallas_call(
        functools.partial(norm_kernel, chunks),
        out_shape=jax.ShapeDtypeStruct((chunks, count, rows), bf16),
        grid=(count // NORM_ROWS,),
        in_specs=[pl.BlockSpec((NORM_ROWS, width), lambda i: (i, 0)), whole],
        out_specs=pl.BlockSpec((chunks, NORM_ROWS, rows), lambda i: (0, i, 0)),
        compiler_params=params,
        cost_estimate=pl.CostEstimate(
            flops=4 * count * width, bytes_accessed=4 * count * width, transcendentals=0
        ),
        name="norm",
    )(hidden[0], norm_gain[None])
    ring = [(i, (i + 1) % chips_z) for i in range(chips_z)]
    end = chips_z - 1
    beside = [swap(mine[0], "y")]
    for k in range(1, chips_z):
        arrived = lax.ppermute(mine[-1], "z", ring)
        if k == 1:
            normed, arrived, beside[0] = lax.optimization_barrier(
                (normed, arrived, beside[0])
            )
        else:
            arrived, beside[k - 1], across[k - 1] = lax.optimization_barrier(
                (arrived, beside[k - 1], across[k - 1])
            )
        if k == end:
            arrived, beside[0], across[1] = lax.optimization_barrier(
                (arrived, beside[0], across[1])
            )
        mine.append(arrived)
        beside.append(swap(arrived, "y"))
        across.append(swap(arrived, "x"))
    corner = {0: swap(beside[0], "x"), 1: swap(across[1], "y")}
    tied = lax.optimization_barrier((beside[end], *across[2:end]))
    beside[end], across[2:end] = tied[0], list(tied[1:])
    for k in range(2, chips_z):
        corner[k] = swap(beside[k], "x") if k == end or k % 2 else swap(across[k], "y")

    normed_other = swap(normed, "core")

    ints = jnp.concatenate([segment, position])
    ints_all = [ints] + [along_ctx(ints, d) for d in range(1, m)]
    where = jnp.concatenate([position[0], swap(position, "core")[0]]).astype(jnp.float32)
    half = HD // 2
    freq = np.exp(np.arange(half, dtype=np.float32) * np.float32(-2.0 * math.log(THETA) / HD))
    angle = where[:, None] * freq[None, :]
    cosine, sine = jnp.cos(angle), jnp.sin(angle)
    cosine = jnp.concatenate([cosine, cosine], axis=1)
    sine = jnp.concatenate([-sine, sine], axis=1)
    seg_k = jnp.concatenate([piece[:1] for piece in ints_all], axis=1)
    pos_k = jnp.concatenate([piece[1:] for piece in ints_all], axis=1)

    place = jnp.stack([z, y, x]).astype(jnp.int32)
    acc_shape = jax.ShapeDtypeStruct((2, 2 * count, 2 * HD), jnp.float32)
    kv_shape = jax.ShapeDtypeStruct((count, 2 * HD), bf16)
    kinds = dict(mine=mine, across=across, beside=beside, corner=corner)
    every = [(k, kind) for k in range(chips_z) for kind in kinds]
    final = [(k, "corner") for k in range(2, chips_z)]
    late = [(end, "across"), (end, "beside"), (0, "corner"), (1, "corner")]
    early = [item for item in every if item not in final + late]
    acc = []
    for items in (early, late, final):
        first, last = items is early, items is final
        outs = pl.pallas_call(
            functools.partial(project_kernel, chips_z, items, first, last, count),
            out_shape=([kv_shape] * 4 if last else []) + [acc_shape],
            in_specs=[pl.BlockSpec(memory_space=pltpu.SMEM)]
            + [whole] * (2 + len(items) + len(acc) + (3 if last else 0)),
            out_specs=[whole] * (5 if last else 1),
            compiler_params=params,
            cost_estimate=pl.CostEstimate(
                flops=2 * 2 * count * rows * 2 * HD * len(items),
                bytes_accessed=2 * rows * 2 * HD * len(items),
                transcendentals=0,
            ),
            name="project",
        )(
            place, normed, normed_other, *[kinds[kind][k] for k, kind in items], *acc,
            *((cosine, sine, key_gain[None]) if last else ()),
        )
        acc = [outs[-1]]

    result = None
    for s in range(2):
        kv_own, kv_other = outs[2 * s], outs[2 * s + 1]
        sources = [kv_own] + [along_ctx(kv_own, d) for d in range(1, m)]
        sources += [along_ctx(kv_other, d, True) for d in range(m)]

        def block(step, place, s=s):
            return (0, lax.rem(place[0] + step, 2) * 2 + s)

        earlier = [] if result is None else [result]
        result = pl.pallas_call(
            functools.partial(attend_kernel, m, count),
            out_shape=jax.ShapeDtypeStruct((count, KVH * G * HD), bf16),
            grid_spec=pltpu.PrefetchScalarGridSpec(
                num_scalar_prefetch=1,
                grid=(2,),
                in_specs=[pl.BlockSpec((count, G * HD), block)]
                + [whole] * (4 + 2 * m)
                + [pl.BlockSpec(memory_space=pl.ANY)] * len(earlier),
                out_specs=pl.BlockSpec((count, G * HD), block),
                scratch_shapes=[
                    pltpu.VMEM((count, m * count), jnp.float32),
                    pltpu.VMEM((m * count, HD), bf16),
                    pltpu.VMEM((m * count, HD), bf16),
                ],
            ),
            input_output_aliases={6 + 2 * m: 0} if earlier else {},
            compiler_params=params,
            cost_estimate=pl.CostEstimate(
                flops=2 * count * m * count * KVH * G * HD,
                bytes_accessed=2 * count * KVH * G * HD,
                transcendentals=count * m * count * KVH * G // 2,
            ),
            name="attend",
        )(
            core.astype(jnp.int32)[None],
            queries[0],
            segment.reshape(count, 1),
            position.reshape(count, 1),
            seg_k,
            pos_k,
            *sources,
            *earlier,
        )
    return result[None]


def solution(mesh):
    n, m = mesh.shape["fsdp"], mesh.shape["ctx"]
    sizes = (n // 4, 2, 2, m // 2, 2)
    fine = Mesh(mesh.devices.reshape(sizes), ("z", "y", "core", "ctx", "x"))
    fsdp, ctx = ("z", "y", "core"), ("ctx", "x")
    placed = (
        P(fsdp, ctx, None),
        P(fsdp, ctx, None),
        P(),
        P(),
        P(fsdp, None),
        P(fsdp, None),
        P(fsdp, ctx),
        P(fsdp, ctx),
    )
    return jax.shard_map(
        functools.partial(on_device, sizes),
        mesh=fine,
        in_specs=placed,
        out_specs=P(fsdp, ctx, None),
        check_vma=False,
    )
```

```python
import functools
import math

import jax
import jax.numpy as jnp
import numpy as np
from jax import lax
from jax.experimental import pallas as pl
from jax.experimental.pallas import tpu as pltpu
from jax.sharding import Mesh
from jax.sharding import PartitionSpec as P

KVH = 4
HD = 128
G = 8
EPS = 1e-06
THETA = 1000000.0
MASKED = -1e30
VMEM_LIMIT = 24 * 2**20
NORM_ROWS = 64


def norm_kernel(chunks, hidden, gain, out):
    inputs = hidden[...].astype(jnp.float32)
    scale = lax.rsqrt(jnp.mean(inputs * inputs, axis=-1, keepdims=True) + EPS)
    normed = (inputs * scale * gain[...]).astype(jnp.bfloat16)
    rows = normed.shape[1] // chunks
    for j in range(chunks):
        out[j] = normed[:, j * rows : (j + 1) * rows]


def project_kernel(chips_z, items, first, last, count, place, own, other, *rest):
    z, y, x = place[0], place[1], place[2]
    pieces, rest = dict(zip(items, rest)), rest[len(items) :]
    terms = {}
    for k in range(chips_z):
        p = lax.rem(z - k + chips_z, chips_z)
        for chunk, kinds in (
            (p * 2 + y, ("mine", "across")),
            (p * 2 + 1 - y, ("beside", "corner")),
        ):
            rows = None
            for side, kind in enumerate(kinds):
                if (k, kind) not in pieces:
                    continue
                if rows is None:
                    rows = jnp.concatenate([own[chunk], other[chunk]], axis=0)
                part = jnp.dot(rows, pieces[k, kind][...], preferred_element_type=jnp.float32)
                terms[side] = terms[side] + part if side in terms else part
    acc = rest[-1]
    for side, at in ((0, x), (1, 1 - x)):
        if side in terms:
            acc[at] = terms[side] if first else rest[0][at] + terms[side]
        else:
            acc[at] = rest[0][at]
    if not last:
        return
    cosine, sine, gain = rest[1:4]
    outs = rest[4:8]
    for head in range(2):
        columns = slice(head * HD, (head + 1) * HD)
        for part in range(2):
            at = slice(part * count, (part + 1) * count)
            out = outs[2 * head + part]
            raw = acc[0, at, columns]
            normk = raw * lax.rsqrt(jnp.mean(raw * raw, axis=-1, keepdims=True) + EPS) * gain[...]
            turned = normk * cosine[at, :] + pltpu.roll(normk, HD // 2, 1) * sine[at, :]
            out[:, :HD] = turned.astype(jnp.bfloat16)
            out[:, HD:] = acc[1, at, columns].astype(jnp.bfloat16)


def mask_kernel(seg_q, pos_q, seg_k, pos_k, bias, needs):
    allowed = (seg_k[...] == seg_q[...]) & (pos_k[...] <= pos_q[...])
    bias[...] = jnp.where(allowed, 0.0, MASKED)
    rows, columns = bias.shape[0] // 2, bias.shape[1] // 2
    for tile in range(2):
        found = [
            jnp.max(
                bias[tile * rows : (tile + 1) * rows, half * columns : (half + 1) * columns]
            )
            == 0.0
            for half in range(2)
        ]
        needs[tile] = found[0].astype(jnp.int32) + 2 * found[1].astype(jnp.int32)


def attend_kernel(pieces, count, place, needs, queries, bias, *rest):
    sources, (out, keys, values) = rest[: 2 * pieces], rest[-3:]
    step = pl.program_id(0)
    tile_rows = count // 2
    length = pieces * tile_rows

    for at in range(2):

        @pl.when(step == at)
        def _():
            for i in range(pieces):
                source = sources[at * pieces + i]
                for half in range(2):
                    here = slice(half * tile_rows, (half + 1) * tile_rows)
                    there = half * length + i * tile_rows
                    keys[there : there + tile_rows, :] = source[here, :HD]
                    values[there : there + tile_rows, :] = source[here, HD:]

    factor = math.log2(math.e) / math.sqrt(HD)

    def tile_body(tile, low, high):
        rows = slice(tile * tile_rows, (tile + 1) * tile_rows)
        k, v, b = keys[low:high, :], values[low:high, :], bias[rows, low:high]

        def score(pair):
            q = jnp.concatenate(
                [queries[rows, g * HD : (g + 1) * HD] for g in (2 * pair, 2 * pair + 1)], axis=0
            )
            return lax.dot_general(
                q, k, (((1,), (1,)), ((), ())), preferred_element_type=jnp.float32
            )

        ahead = score(0)
        for pair in range(G // 2):
            scores = ahead.reshape(2, tile_rows, high - low) + b[None]
            if pair + 1 < G // 2:
                ahead = score(pair + 1)
            top = jnp.max(scores, axis=-1, keepdims=True)
            weights = jnp.exp2((scores - top) * factor)
            total = jnp.sum(weights, axis=-1, keepdims=True)
            summed = jnp.dot(
                weights.astype(jnp.bfloat16).reshape(2 * tile_rows, high - low),
                v,
                preferred_element_type=jnp.float32,
            ).reshape(2, tile_rows, HD)
            result = (summed * (1.0 / total)).astype(jnp.bfloat16)
            for i in range(2):
                g = 2 * pair + i
                out[rows, g * HD : (g + 1) * HD] = result[i]

    for tile in range(2):
        for need, low, high in ((1, 0, length), (2, length, 2 * length), (3, 0, 2 * length)):

            @pl.when(needs[tile] == need)
            def _():
                tile_body(tile, low, high)


def swap(array, axis):
    return lax.ppermute(array, axis, [(0, 1), (1, 0)])


def on_device(
    sizes, hidden, queries, norm_gain, key_gain, k_weight, v_weight, segment, position
):
    chips_z, groups = sizes[0], sizes[3]
    count, width = hidden.shape[1:]
    own_rows = k_weight.shape[0]
    rows = 2 * own_rows
    chunks = 2 * chips_z
    m = 2 * groups
    z, y = lax.axis_index("z"), lax.axis_index("y")
    core, x = lax.axis_index("core"), lax.axis_index("x")
    bf16 = jnp.bfloat16
    whole = pl.BlockSpec(memory_space=pltpu.VMEM)
    params = pltpu.CompilerParams(vmem_limit_bytes=VMEM_LIMIT)

    def along_ctx(array, d, cross=False):
        pairs = []
        for c in range(2):
            for i in range(m):
                pairs.append((c * m + i, (c ^ int(cross)) * m + (i + d) % m))
        return lax.ppermute(array, ("core", "ctx", "x"), pairs)

    def columns(which):
        at = which * 2 * HD
        return jnp.stack(
            [lax.dynamic_slice_in_dim(w, at, 2 * HD, 1) for w in (k_weight, v_weight)]
        )

    taken = swap(columns(1 - core), "core")
    kept = columns(core)
    chip = lax.dynamic_update_slice(
        jnp.zeros((2, rows, 2 * HD), bf16), kept, (0, core * own_rows, 0)
    )
    chip = lax.dynamic_update_slice(chip, taken, (0, (1 - core) * own_rows, 0))
    mine = [lax.dynamic_index_in_dim(chip, x, 0, keepdims=False)]
    across = [lax.dynamic_index_in_dim(chip, 1 - x, 0, keepdims=False)]
    hidden, mine[0], across[0] = lax.optimization_barrier((hidden, mine[0], across[0]))
    normed = pl.pallas_call(
        functools.partial(norm_kernel, chunks),
        out_shape=jax.ShapeDtypeStruct((chunks, count, rows), bf16),
        grid=(count // NORM_ROWS,),
        in_specs=[pl.BlockSpec((NORM_ROWS, width), lambda i: (i, 0)), whole],
        out_specs=pl.BlockSpec((chunks, NORM_ROWS, rows), lambda i: (0, i, 0)),
        compiler_params=params,
        cost_estimate=pl.CostEstimate(
            flops=4 * count * width, bytes_accessed=4 * count * width, transcendentals=0
        ),
        name="norm",
    )(hidden[0], norm_gain[None])
    ints = jnp.concatenate([segment, position])
    ints_all = [ints] + [along_ctx(ints, d) for d in range(1, m)]
    where = jnp.concatenate([position[0], swap(position, "core")[0]]).astype(jnp.float32)
    half = HD // 2
    freq = np.exp(np.arange(half, dtype=np.float32) * np.float32(-2.0 * math.log(THETA) / HD))
    angle = where[:, None] * freq[None, :]
    cosine, sine = jnp.cos(angle), jnp.sin(angle)
    cosine = jnp.concatenate([cosine, cosine], axis=1)
    sine = jnp.concatenate([-sine, sine], axis=1)
    order = (
        jnp.stack(ints_all).reshape(m, 2, 2, count // 2).transpose(1, 2, 0, 3).reshape(2, m * count)
    )
    bias, needs = pl.pallas_call(
        mask_kernel,
        out_shape=[
            jax.ShapeDtypeStruct((count, m * count), jnp.float32),
            jax.ShapeDtypeStruct((2,), jnp.int32),
        ],
        in_specs=[whole] * 4,
        out_specs=[whole, pl.BlockSpec(memory_space=pltpu.SMEM)],
        compiler_params=params,
        name="mask",
    )(segment.reshape(count, 1), position.reshape(count, 1), order[:1], order[1:])

    ring = [(i, (i + 1) % chips_z) for i in range(chips_z)]
    end = chips_z - 1
    beside = [swap(mine[0], "y")]
    for k in range(1, chips_z):
        arrived = lax.ppermute(mine[-1], "z", ring)
        if k == 1:
            normed, arrived, beside[0] = lax.optimization_barrier(
                (normed, arrived, beside[0])
            )
        else:
            arrived, beside[k - 1], across[k - 1] = lax.optimization_barrier(
                (arrived, beside[k - 1], across[k - 1])
            )
        if k == end:
            arrived, beside[0], across[1], bias, needs = lax.optimization_barrier(
                (arrived, beside[0], across[1], bias, needs)
            )
        mine.append(arrived)
        beside.append(swap(arrived, "y"))
        across.append(swap(arrived, "x"))
    corner = {0: swap(beside[0], "x"), 1: swap(across[1], "y")}
    tied = lax.optimization_barrier((beside[end], *across[2:end]))
    beside[end], across[2:end] = tied[0], list(tied[1:])
    for k in range(2, chips_z):
        corner[k] = swap(beside[k], "x") if k == end or k % 2 else swap(across[k], "y")

    normed_other = swap(normed, "core")

    place = jnp.stack([z, y, x]).astype(jnp.int32)
    acc_shape = jax.ShapeDtypeStruct((2, 2 * count, 2 * HD), jnp.float32)
    kv_shape = jax.ShapeDtypeStruct((count, 2 * HD), bf16)
    kinds = dict(mine=mine, across=across, beside=beside, corner=corner)
    every = [(k, kind) for k in range(chips_z) for kind in kinds]
    final = [(k, "corner") for k in range(2, chips_z)]
    late = [(end, "across"), (end, "beside"), (0, "corner"), (1, "corner")]
    early = [item for item in every if item not in final + late]
    acc = []
    for items in (early, late, final):
        first, last = items is early, items is final
        outs = pl.pallas_call(
            functools.partial(project_kernel, chips_z, items, first, last, count),
            out_shape=[kv_shape] * 4 if last else [acc_shape],
            in_specs=[pl.BlockSpec(memory_space=pltpu.SMEM)]
            + [whole] * (2 + len(items) + len(acc) + (3 if last else 0)),
            out_specs=[whole] * (4 if last else 1),
            scratch_shapes=[pltpu.VMEM(acc_shape.shape, acc_shape.dtype)] * int(last),
            compiler_params=params,
            cost_estimate=pl.CostEstimate(
                flops=2 * 2 * count * rows * 2 * HD * len(items),
                bytes_accessed=2 * rows * 2 * HD * len(items),
                transcendentals=0,
            ),
            name="project",
        )(
            place, normed, normed_other, *[kinds[kind][k] for k, kind in items], *acc,
            *((cosine, sine, key_gain[None]) if last else ()),
        )
        acc = [outs[-1]]

    result = None
    for s in range(2):
        kv_own, kv_other = outs[2 * s], outs[2 * s + 1]
        sources = [kv_own] + [along_ctx(kv_own, d) for d in range(1, m)]
        sources += [along_ctx(kv_other, d, True) for d in range(m)]

        def block(step, place, needs, s=s):
            return (0, lax.rem(place[0] + step, 2) * 2 + s)

        earlier = [] if result is None else [result]
        result = pl.pallas_call(
            functools.partial(attend_kernel, m, count),
            out_shape=jax.ShapeDtypeStruct((count, KVH * G * HD), bf16),
            grid_spec=pltpu.PrefetchScalarGridSpec(
                num_scalar_prefetch=2,
                grid=(2,),
                in_specs=[pl.BlockSpec((count, G * HD), block)]
                + [whole] * (1 + 2 * m)
                + [pl.BlockSpec(memory_space=pl.ANY)] * len(earlier),
                out_specs=pl.BlockSpec((count, G * HD), block),
                scratch_shapes=[
                    pltpu.VMEM((m * count, HD), bf16),
                    pltpu.VMEM((m * count, HD), bf16),
                ],
            ),
            input_output_aliases={4 + 2 * m: 0} if earlier else {},
            compiler_params=params,
            cost_estimate=pl.CostEstimate(
                flops=2 * count * m * count * KVH * G * HD,
                bytes_accessed=2 * count * KVH * G * HD,
                transcendentals=count * m * count * KVH * G // 2,
            ),
            name="attend",
        )(core.astype(jnp.int32)[None], needs, queries[0], bias, *sources, *earlier)
    return result[None]


def solution(mesh):
    n, m = mesh.shape["fsdp"], mesh.shape["ctx"]
    sizes = (n // 4, 2, 2, m // 2, 2)
    fine = Mesh(mesh.devices.reshape(sizes), ("z", "y", "core", "ctx", "x"))
    fsdp, ctx = ("z", "y", "core"), ("ctx", "x")
    placed = (
        P(fsdp, ctx, None),
        P(fsdp, ctx, None),
        P(),
        P(),
        P(fsdp, None),
        P(fsdp, None),
        P(fsdp, ctx),
        P(fsdp, ctx),
    )
    return jax.shard_map(
        functools.partial(on_device, sizes),
        mesh=fine,
        in_specs=placed,
        out_specs=P(fsdp, ctx, None),
        check_vma=False,
    )
```

```python
import functools
import math

import jax
import jax.numpy as jnp
import numpy as np
from jax import lax
from jax.experimental import pallas as pl
from jax.experimental.pallas import tpu as pltpu
from jax.sharding import Mesh
from jax.sharding import PartitionSpec as P

KVH = 4
HD = 128
G = 8
EPS = 1e-06
THETA = 1000000.0
MASKED = -1e30
VMEM_LIMIT = 24 * 2**20
NORM_ROWS = 64


def norm_kernel(chunks, hidden, gain, out):
    inputs = hidden[...].astype(jnp.float32)
    scale = lax.rsqrt(jnp.mean(inputs * inputs, axis=-1, keepdims=True) + EPS)
    normed = (inputs * scale * gain[...]).astype(jnp.bfloat16)
    rows = normed.shape[1] // chunks
    for j in range(chunks):
        out[j] = normed[:, j * rows : (j + 1) * rows]


def project_kernel(chips_z, items, first, last, count, place, own, other, *rest):
    z, y, x = place[0], place[1], place[2]
    pieces, rest = {}, list(rest)
    for item in items:
        halves = 2 if item == (chips_z // 2, "corner") else 1
        pieces[item] = jnp.concatenate([rest.pop(0)[...] for _ in range(halves)], axis=0)
    terms = {}
    for k in range(chips_z):
        p = lax.rem(z - k + chips_z, chips_z)
        for chunk, kinds in (
            (p * 2 + y, ("mine", "across")),
            (p * 2 + 1 - y, ("beside", "corner")),
        ):
            rows = None
            for side, kind in enumerate(kinds):
                if (k, kind) not in pieces:
                    continue
                if rows is None:
                    rows = jnp.concatenate([own[chunk], other[chunk]], axis=0)
                part = jnp.dot(rows, pieces[k, kind], preferred_element_type=jnp.float32)
                terms[side] = terms[side] + part if side in terms else part
    acc = rest[-1]
    for side, at in ((0, x), (1, 1 - x)):
        if side in terms:
            acc[at] = terms[side] if first else rest[0][at] + terms[side]
        else:
            acc[at] = rest[0][at]
    if not last:
        return
    cosine, sine, gain = rest[1:4]
    outs = rest[4:8]
    for head in range(2):
        columns = slice(head * HD, (head + 1) * HD)
        for part in range(2):
            at = slice(part * count, (part + 1) * count)
            out = outs[2 * head + part]
            raw = acc[0, at, columns]
            normk = raw * lax.rsqrt(jnp.mean(raw * raw, axis=-1, keepdims=True) + EPS) * gain[...]
            turned = normk * cosine[at, :] + pltpu.roll(normk, HD // 2, 1) * sine[at, :]
            out[:, :HD] = turned.astype(jnp.bfloat16)
            out[:, HD:] = acc[1, at, columns].astype(jnp.bfloat16)


def mask_kernel(seg_q, pos_q, seg_k, pos_k, bias, needs):
    allowed = (seg_k[...] == seg_q[...]) & (pos_k[...] <= pos_q[...])
    bias[...] = jnp.where(allowed, 0.0, MASKED)
    rows, columns = bias.shape[0] // 2, bias.shape[1] // 2
    for tile in range(2):
        found = [
            jnp.max(
                bias[tile * rows : (tile + 1) * rows, half * columns : (half + 1) * columns]
            )
            == 0.0
            for half in range(2)
        ]
        needs[tile] = found[0].astype(jnp.int32) + 2 * found[1].astype(jnp.int32)


def attend_kernel(lefts, count, place, needs, queries, bias, *rest):
    pieces = len(lefts)
    sources, (out, keys, values) = rest[:pieces], rest[-3:]
    tile_rows = count // 2
    length = pieces * tile_rows
    for i, (left, source) in enumerate(zip(lefts, sources)):
        for half in range(2):
            here = slice(half * tile_rows, (half + 1) * tile_rows)
            there = half * length + i * tile_rows
            keys[there : there + tile_rows, :] = source[here, left : left + HD]
            values[there : there + tile_rows, :] = source[here, left + HD : left + 2 * HD]

    factor = math.log2(math.e) / math.sqrt(HD)

    def tile_body(tile, low, high):
        rows = slice(tile * tile_rows, (tile + 1) * tile_rows)
        k, v, b = keys[low:high, :], values[low:high, :], bias[rows, low:high]

        def score(pair):
            q = jnp.concatenate(
                [queries[rows, g * HD : (g + 1) * HD] for g in (2 * pair, 2 * pair + 1)], axis=0
            )
            return lax.dot_general(
                q, k, (((1,), (1,)), ((), ())), preferred_element_type=jnp.float32
            )

        ahead = score(0)
        for pair in range(G // 2):
            scores = ahead.reshape(2, tile_rows, high - low) + b[None]
            if pair + 1 < G // 2:
                ahead = score(pair + 1)
            top = jnp.max(scores, axis=-1, keepdims=True)
            weights = jnp.exp2((scores - top) * factor)
            total = jnp.sum(weights, axis=-1, keepdims=True)
            summed = jnp.dot(
                weights.astype(jnp.bfloat16).reshape(2 * tile_rows, high - low),
                v,
                preferred_element_type=jnp.float32,
            ).reshape(2, tile_rows, HD)
            result = (summed * (1.0 / total)).astype(jnp.bfloat16)
            for i in range(2):
                g = 2 * pair + i
                out[rows, g * HD : (g + 1) * HD] = result[i]

    for tile in range(2):
        for need, low, high in ((1, 0, length), (2, length, 2 * length), (3, 0, 2 * length)):

            @pl.when(needs[tile] == need)
            def _():
                tile_body(tile, low, high)


def swap(array, axis):
    return lax.ppermute(array, axis, [(0, 1), (1, 0)])


def on_device(
    sizes, hidden, queries, norm_gain, key_gain, k_weight, v_weight, segment, position
):
    chips_z, groups = sizes[0], sizes[3]
    count, width = hidden.shape[1:]
    own_rows = k_weight.shape[0]
    rows = 2 * own_rows
    chunks = 2 * chips_z
    m = 2 * groups
    z, y = lax.axis_index("z"), lax.axis_index("y")
    core, x = lax.axis_index("core"), lax.axis_index("x")
    bf16 = jnp.bfloat16
    whole = pl.BlockSpec(memory_space=pltpu.VMEM)
    params = pltpu.CompilerParams(vmem_limit_bytes=VMEM_LIMIT)

    def along_ctx(array, d, cross=False):
        pairs = []
        for c in range(2):
            for i in range(m):
                pairs.append((c * m + i, (c ^ int(cross)) * m + (i + d) % m))
        return lax.ppermute(array, ("core", "ctx", "x"), pairs)

    def columns(which):
        at = which * 2 * HD
        return jnp.stack(
            [lax.dynamic_slice_in_dim(w, at, 2 * HD, 1) for w in (k_weight, v_weight)]
        )

    taken = swap(columns(1 - core), "core")
    kept = columns(core)
    chip = lax.dynamic_update_slice(
        jnp.zeros((2, rows, 2 * HD), bf16), kept, (0, core * own_rows, 0)
    )
    chip = lax.dynamic_update_slice(chip, taken, (0, (1 - core) * own_rows, 0))
    half_x = lax.dynamic_index_in_dim(chip, x, 0, keepdims=False)
    half_o = lax.dynamic_index_in_dim(chip, 1 - x, 0, keepdims=False)
    hidden, half_x, half_o = lax.optimization_barrier((hidden, half_x, half_o))
    normed = pl.pallas_call(
        functools.partial(norm_kernel, chunks),
        out_shape=jax.ShapeDtypeStruct((chunks, count, rows), bf16),
        grid=(count // NORM_ROWS,),
        in_specs=[pl.BlockSpec((NORM_ROWS, width), lambda i: (i, 0)), whole],
        out_specs=pl.BlockSpec((chunks, NORM_ROWS, rows), lambda i: (0, i, 0)),
        compiler_params=params,
        cost_estimate=pl.CostEstimate(
            flops=4 * count * width, bytes_accessed=4 * count * width, transcendentals=0
        ),
        name="norm",
    )(hidden[0], norm_gain[None])
    def ring(array, step):
        return lax.ppermute(array, "z", [(i, (i + step) % chips_z) for i in range(chips_z)])

    middle = chips_z // 2
    mine, across, beside, corner = {0: half_x}, {0: half_o}, {}, {}
    beside[0] = swap(mine[0], "y")
    for r in range(1, middle + 1):
        arrived = [r] if r == middle else [r, chips_z - r]
        for k in arrived:
            mine[k] = ring(mine[k - 1], 1) if k == r else ring(mine[(k + 1) % chips_z], -1)
        if r == 1:
            tied = (beside[0], segment, position)
            beside[0], segment, position = lax.optimization_barrier(tied)
            corner[0] = swap(beside[0], "x")
            ints = jnp.concatenate([segment, position])
            ints_all = [ints] + [along_ctx(ints, d) for d in range(1, m)]
            position_other = swap(position, "core")
            tied = (mine[1], mine[chips_z - 1], corner[0], normed, position_other, ints_all)
            tied = lax.optimization_barrier(tied)
            mine[1], mine[chips_z - 1], corner[0], normed, position_other, ints_all = tied
        elif r == middle:
            tied = (mine[r], across[r - 1], beside[chips_z - r + 1])
            mine[r], across[r - 1], beside[chips_z - r + 1] = lax.optimization_barrier(tied)
        for k in arrived:
            beside[k], across[k] = swap(mine[k], "y"), swap(mine[k], "x")
    for k in range(1, chips_z):
        if k < middle:
            corner[k] = swap(across[k], "y")
        elif k > middle:
            corner[k] = swap(beside[k], "x")
    normed_other = swap(normed, "core")
    where = jnp.concatenate([position[0], position_other[0]]).astype(jnp.float32)
    half = HD // 2
    freq = np.exp(np.arange(half, dtype=np.float32) * np.float32(-2.0 * math.log(THETA) / HD))
    angle = where[:, None] * freq[None, :]
    cosine, sine = jnp.cos(angle), jnp.sin(angle)
    cosine = jnp.concatenate([cosine, cosine], axis=1)
    sine = jnp.concatenate([-sine, sine], axis=1)
    order = (
        jnp.stack(ints_all).reshape(m, 2, 2, count // 2).transpose(1, 2, 0, 3).reshape(2, m * count)
    )
    bias, needs = pl.pallas_call(
        mask_kernel,
        out_shape=[
            jax.ShapeDtypeStruct((count, m * count), jnp.float32),
            jax.ShapeDtypeStruct((2,), jnp.int32),
        ],
        in_specs=[whole] * 4,
        out_specs=[whole, pl.BlockSpec(memory_space=pltpu.SMEM)],
        compiler_params=params,
        name="mask",
    )(segment.reshape(count, 1), position.reshape(count, 1), order[:1], order[1:])


    place = jnp.stack([z, y, x]).astype(jnp.int32)
    acc_shape = jax.ShapeDtypeStruct((2, 2 * count, 2 * HD), jnp.float32)
    kv_shape = jax.ShapeDtypeStruct((count, 2 * HD), bf16)
    kinds = dict(mine=mine, across=across, beside=beside, corner=corner)
    every = [(k, kind) for k in range(chips_z) for kind in kinds]
    final = [(middle, "corner")]
    late = [(middle, "beside"), (middle, "across")]
    late += [(k, "corner") for k in range(1, chips_z) if k != middle]
    early = [item for item in every if item not in final + late]
    acc = []
    for items in (early, late, final):
        first, last = items is early, items is final
        if items is late:
            tied = (beside[middle], across[middle], acc[0], bias, needs)
            tied = lax.optimization_barrier(tied)
            beside[middle], across[middle], acc[0], bias, needs = tied
            corner[middle] = (
                swap(beside[middle][: rows // 2], "x"), swap(across[middle][rows // 2 :], "y")
            )
        arrays = jax.tree.leaves([kinds[kind][k] for k, kind in items])
        outs = pl.pallas_call(
            functools.partial(project_kernel, chips_z, items, first, last, count),
            out_shape=[kv_shape] * 4 if last else [acc_shape],
            in_specs=[pl.BlockSpec(memory_space=pltpu.SMEM)]
            + [whole] * (2 + len(arrays) + len(acc) + (3 if last else 0)),
            out_specs=[whole] * (4 if last else 1),
            scratch_shapes=[pltpu.VMEM(acc_shape.shape, acc_shape.dtype)] * int(last),
            compiler_params=params,
            cost_estimate=pl.CostEstimate(
                flops=2 * 2 * count * rows * 2 * HD * len(items),
                bytes_accessed=2 * rows * 2 * HD * len(items),
                transcendentals=0,
            ),
            name="project",
        )(
            place, normed, normed_other, *arrays, *acc,
            *((cosine, sine, key_gain[None]) if last else ()),
        )
        acc = [outs[-1]]

    beyond = [[kv] + [along_ctx(kv, d) for d in range(1, m)] for kv in (outs[0], outs[2])]
    joined = jnp.concatenate([outs[1], outs[3]], axis=1)
    local = along_ctx(joined, 0, True)
    beyond += [[local] + [along_ctx(kv, d, True) for d in range(1, m)] for kv in (outs[1], outs[3])]
    result = None
    for step, sources in enumerate(beyond):

        def block(i, place, needs, step=step):
            return (0, lax.rem(place[0] + step // 2, 2) * 2 + step % 2)

        earlier = [] if result is None else [result]
        result = pl.pallas_call(
            functools.partial(
                attend_kernel, [2 * HD * (step % 2) if a is local else 0 for a in sources], count
            ),
            out_shape=jax.ShapeDtypeStruct((count, KVH * G * HD), bf16),
            grid_spec=pltpu.PrefetchScalarGridSpec(
                num_scalar_prefetch=2,
                grid=(1,),
                in_specs=[pl.BlockSpec((count, G * HD), block)]
                + [whole] * (1 + m)
                + [pl.BlockSpec(memory_space=pl.ANY)] * len(earlier),
                out_specs=pl.BlockSpec((count, G * HD), block),
                scratch_shapes=[
                    pltpu.VMEM((m * count, HD), bf16),
                    pltpu.VMEM((m * count, HD), bf16),
                ],
            ),
            input_output_aliases={4 + m: 0} if earlier else {},
            compiler_params=params,
            cost_estimate=pl.CostEstimate(
                flops=count * m * count * KVH * G * HD,
                bytes_accessed=count * KVH * G * HD,
                transcendentals=count * m * count * KVH * G // 4,
            ),
            name="attend",
        )(core.astype(jnp.int32)[None], needs, queries[0], bias, *sources, *earlier)
    return result[None]


def solution(mesh):
    n, m = mesh.shape["fsdp"], mesh.shape["ctx"]
    sizes = (n // 4, 2, 2, m // 2, 2)
    fine = Mesh(mesh.devices.reshape(sizes), ("z", "y", "core", "ctx", "x"))
    fsdp, ctx = ("z", "y", "core"), ("ctx", "x")
    placed = (
        P(fsdp, ctx, None),
        P(fsdp, ctx, None),
        P(),
        P(),
        P(fsdp, None),
        P(fsdp, None),
        P(fsdp, ctx),
        P(fsdp, ctx),
    )
    return jax.shard_map(
        functools.partial(on_device, sizes),
        mesh=fine,
        in_specs=placed,
        out_specs=P(fsdp, ctx, None),
        check_vma=False,
    )
```

```python
import functools
import math

import jax
import jax.numpy as jnp
import numpy as np
from jax import lax
from jax.experimental import pallas as pl
from jax.experimental.pallas import tpu as pltpu
from jax.sharding import Mesh
from jax.sharding import PartitionSpec as P

KVH = 4
HD = 128
G = 8
EPS = 1e-06
THETA = 1000000.0
MASKED = -1e30
VMEM_LIMIT = 24 * 2**20
NORM_ROWS = 64


def norm_kernel(chunks, hidden, gain, out):
    inputs = hidden[...].astype(jnp.float32)
    scale = lax.rsqrt(jnp.mean(inputs * inputs, axis=-1, keepdims=True) + EPS)
    normed = (inputs * scale * gain[...]).astype(jnp.bfloat16)
    rows = normed.shape[1] // chunks
    for j in range(chunks):
        out[j] = normed[:, j * rows : (j + 1) * rows]


def project_kernel(chips_z, groups, first, last, count, tokens, place, own, other, *rest):
    z, y, x = place[0], place[1], place[2]
    rest = list(rest)
    weight, lhs, sems = rest[-3:]
    rows = weight.shape[2]
    waits = []
    for g, (k, near) in enumerate(groups):
        p = lax.rem(z - k + chips_z, chips_z)
        chunk = p * 2 + (y if near else 1 - y)
        pairs = [
            (own.at[chunk], lhs.at[g, pl.ds(0, count)]),
            (other.at[chunk], lhs.at[g, pl.ds(count, count)]),
        ]
        if k == 0:
            pairs.append((rest.pop(0), weight.at[g]))
        elif near or k != chips_z // 2:
            pairs.append((rest.pop(0), weight.at[g, x]))
            pairs.append((rest.pop(0), weight.at[g, 1 - x]))
        else:
            pairs.append((rest.pop(0), weight.at[g, x]))
            for part in range(2):
                at = pl.ds(part * (rows // 2), rows // 2)
                pairs.append((rest.pop(0), weight.at[g, 1 - x, at]))
        copies = [
            pltpu.make_async_copy(source, target, sems.at[g, i])
            for i, (source, target) in enumerate(pairs)
        ]
        for copy in copies:
            copy.start()
        waits.append(copies)
    if last:
        rest = rest[tokens:]
    earlier = None if first else rest.pop(0)
    terms = [None, None]
    for g, copies in enumerate(waits):
        for copy in copies:
            copy.wait()
        for half in range(2):
            part = jnp.dot(lhs[g], weight[g, half], preferred_element_type=jnp.float32)
            terms[half] = part if terms[half] is None else terms[half] + part
    for half in range(2):
        if not first:
            terms[half] += earlier[half]
        if not last:
            rest[0][half] = terms[half]
    if not last:
        return
    cosine, sine, gain = rest[:3]
    outs = rest[3:5]
    for head in range(2):
        columns = slice(head * HD, (head + 1) * HD)
        for part, out in enumerate(outs):
            at = slice(part * count, (part + 1) * count)
            raw = terms[0][at, columns]
            normk = raw * lax.rsqrt(jnp.mean(raw * raw, axis=-1, keepdims=True) + EPS) * gain[...]
            turned = normk * cosine[at, :] + pltpu.roll(normk, HD // 2, 1) * sine[at, :]
            out[:, 2 * head * HD : (2 * head + 1) * HD] = turned.astype(jnp.bfloat16)
            out[:, (2 * head + 1) * HD : (2 * head + 2) * HD] = terms[1][at, columns].astype(
                jnp.bfloat16
            )


def mask_kernel(seg_q, pos_q, seg_k, pos_k, bias, needs):
    allowed = (seg_k[...] == seg_q[...]) & (pos_k[...] <= pos_q[...])
    bias[...] = jnp.where(allowed, 0.0, MASKED)
    rows, columns = bias.shape[0] // 2, bias.shape[1] // 2
    for tile in range(2):
        found = [
            jnp.max(
                bias[tile * rows : (tile + 1) * rows, half * columns : (half + 1) * columns]
            )
            == 0.0
            for half in range(2)
        ]
        needs[tile] = found[0].astype(jnp.int32) + 2 * found[1].astype(jnp.int32)


def attend_kernel(pieces, count, place, needs, queries, bias, *rest):
    sources, (out, keys, values) = rest[:pieces], rest[-3:]
    step = pl.program_id(0)
    tile_rows = count // 2
    length = pieces * tile_rows

    for head in range(2):

        @pl.when(step == head)
        def _():
            left = 2 * head * HD
            for i, source in enumerate(sources):
                for half in range(2):
                    here = slice(half * tile_rows, (half + 1) * tile_rows)
                    there = half * length + i * tile_rows
                    keys[there : there + tile_rows, :] = source[here, left : left + HD]
                    values[there : there + tile_rows, :] = source[here, left + HD : left + 2 * HD]

    factor = math.log2(math.e) / math.sqrt(HD)

    def tile_body(tile, low, high):
        rows = slice(tile * tile_rows, (tile + 1) * tile_rows)
        k, v, b = keys[low:high, :], values[low:high, :], bias[rows, low:high]

        def score(pair):
            q = jnp.concatenate(
                [queries[rows, g * HD : (g + 1) * HD] for g in (2 * pair, 2 * pair + 1)], axis=0
            )
            return lax.dot_general(
                q, k, (((1,), (1,)), ((), ())), preferred_element_type=jnp.float32
            )

        ahead = score(0)
        for pair in range(G // 2):
            scores = ahead.reshape(2, tile_rows, high - low) + b[None]
            if pair + 1 < G // 2:
                ahead = score(pair + 1)
            top = jnp.max(scores, axis=-1, keepdims=True)
            weights = jnp.exp2((scores - top) * factor)
            total = jnp.sum(weights, axis=-1, keepdims=True)
            summed = jnp.dot(
                weights.astype(jnp.bfloat16).reshape(2 * tile_rows, high - low),
                v,
                preferred_element_type=jnp.float32,
            ).reshape(2, tile_rows, HD)
            result = (summed * (1.0 / total)).astype(jnp.bfloat16)
            for i in range(2):
                g = 2 * pair + i
                out[rows, g * HD : (g + 1) * HD] = result[i]

    for tile in range(2):
        for need, low, high in ((1, 0, length), (2, length, 2 * length), (3, 0, 2 * length)):

            @pl.when(needs[tile] == need)
            def _():
                tile_body(tile, low, high)


def swap(array, axis):
    return lax.ppermute(array, axis, [(0, 1), (1, 0)])


def on_device(
    sizes, hidden, queries, norm_gain, key_gain, k_weight, v_weight, segment, position
):
    chips_z, groups = sizes[0], sizes[3]
    count, width = hidden.shape[1:]
    own_rows = k_weight.shape[0]
    rows = 2 * own_rows
    chunks = 2 * chips_z
    m = 2 * groups
    z, y = lax.axis_index("z"), lax.axis_index("y")
    core, x = lax.axis_index("core"), lax.axis_index("x")
    bf16 = jnp.bfloat16
    whole = pl.BlockSpec(memory_space=pltpu.VMEM)
    params = pltpu.CompilerParams(vmem_limit_bytes=VMEM_LIMIT)

    def along_ctx(array, d, cross=False):
        pairs = []
        for c in range(2):
            for i in range(m):
                pairs.append((c * m + i, (c ^ int(cross)) * m + (i + d) % m))
        return lax.ppermute(array, ("core", "ctx", "x"), pairs)

    def columns(which):
        at = which * 2 * HD
        return jnp.stack(
            [lax.dynamic_slice_in_dim(w, at, 2 * HD, 1) for w in (k_weight, v_weight)]
        )

    tokens = []

    def after(array, *others):
        corners = [
            other[tuple(slice(0, size) for size in (1, 16, 128)[-other.ndim :])]
            for other in others
        ]
        array, corners = lax.optimization_barrier((array, corners))
        tokens.extend(corners)
        return array

    def norm(array):
        return pl.pallas_call(
            functools.partial(norm_kernel, chunks),
            out_shape=jax.ShapeDtypeStruct((chunks, count, rows), bf16),
            grid=(count // NORM_ROWS,),
            in_specs=[pl.BlockSpec((NORM_ROWS, width), lambda i: (i, 0)), whole],
            out_specs=pl.BlockSpec((chunks, NORM_ROWS, rows), lambda i: (0, i, 0)),
            compiler_params=params,
            cost_estimate=pl.CostEstimate(
                flops=4 * count * width, bytes_accessed=4 * count * width, transcendentals=0
            ),
            name="norm",
        )(array[0], norm_gain[None])

    taken = swap(columns(1 - core), "core")
    kept = columns(core)
    hidden_other = swap(hidden, "core")
    chip = lax.dynamic_update_slice(
        jnp.zeros((2, rows, 2 * HD), bf16), kept, (0, core * own_rows, 0)
    )
    chip = lax.dynamic_update_slice(chip, taken, (0, (1 - core) * own_rows, 0))
    normed = norm(after(hidden, chip))
    segment, position = after(segment, normed), after(position, normed)
    normed_other = norm(hidden_other)
    position_other = swap(position, "core")
    ints = jnp.concatenate([segment, position])
    ints_all = [ints] + [along_ctx(ints, d) for d in range(1, m)]

    def ring(array, step):
        return lax.ppermute(array, "z", [(i, (i + step) % chips_z) for i in range(chips_z)])

    middle = chips_z // 2
    mine = {0: lax.dynamic_index_in_dim(chip, x, 0, keepdims=False)}
    across, beside, corner = {}, {}, {}
    chip_beside = swap(chip, "y")
    for r in range(1, middle + 1):
        arrived = [r] if r == middle else [r, chips_z - r]
        for k in arrived:
            mine[k] = ring(mine[k - 1], 1) if k == r else ring(mine[(k + 1) % chips_z], -1)
        if r == 1:
            tied = (mine[1], mine[chips_z - 1])
            others = (chip_beside, normed_other, position_other, *ints_all[1:])
            mine[1], mine[chips_z - 1] = after(tied, *others)
        elif r == middle:
            mine[r] = after(mine[r], beside[r - 1], across[chips_z - r + 1])
        for k in arrived:
            beside[k], across[k] = swap(mine[k], "y"), swap(mine[k], "x")
    for k in range(1, chips_z):
        if k < middle:
            corner[k] = swap(across[k], "y")
        elif k > middle:
            corner[k] = swap(beside[k], "x")

    where = jnp.concatenate([position[0], position_other[0]]).astype(jnp.float32)
    half = HD // 2
    freq = np.exp(np.arange(half, dtype=np.float32) * np.float32(-2.0 * math.log(THETA) / HD))
    angle = where[:, None] * freq[None, :]
    cosine, sine = jnp.cos(angle), jnp.sin(angle)
    cosine = jnp.concatenate([cosine, cosine], axis=1)
    sine = jnp.concatenate([-sine, sine], axis=1)
    order = (
        jnp.stack(ints_all).reshape(m, 2, 2, count // 2).transpose(1, 2, 0, 3).reshape(2, m * count)
    )
    bias, needs = pl.pallas_call(
        mask_kernel,
        out_shape=[
            jax.ShapeDtypeStruct((count, m * count), jnp.float32),
            jax.ShapeDtypeStruct((2,), jnp.int32),
        ],
        in_specs=[whole] * 4,
        out_specs=[whole, pl.BlockSpec(memory_space=pltpu.SMEM)],
        compiler_params=params,
        name="mask",
    )(segment.reshape(count, 1), position.reshape(count, 1), order[:1], order[1:])


    place = jnp.stack([z, y, x]).astype(jnp.int32)
    acc_shape = jax.ShapeDtypeStruct((2, 2 * count, 2 * HD), jnp.float32)
    kv_shape = jax.ShapeDtypeStruct((count, 4 * HD), bf16)
    early = [(0, True), (0, False)]
    early += [(k, True) for k in range(1, chips_z) if k != middle]
    late = [(middle, True)] + [(k, False) for k in range(1, chips_z) if k != middle]
    final = [(middle, False)]
    acc = []
    for groups in (early, late, final):
        first, last = groups is early, groups is final
        if groups is late:
            top, bottom = beside[middle][: rows // 2], across[middle][rows // 2 :]
            corner[middle] = (
                swap(after(top, acc[0]), "x"), swap(after(bottom, bias), "y")
            )
        arrays = []
        for k, near in groups:
            if k == 0:
                arrays.append(chip if near else chip_beside)
            else:
                arrays += [mine[k], across[k]] if near else [beside[k], corner[k]]
        arrays = jax.tree.leaves(arrays)
        anywhere = pl.BlockSpec(memory_space=pl.ANY)
        outs = pl.pallas_call(
            functools.partial(
                project_kernel, chips_z, groups, first, last, count, len(tokens)
            ),
            out_shape=[kv_shape] * 2 if last else [acc_shape],
            in_specs=[pl.BlockSpec(memory_space=pltpu.SMEM)]
            + [anywhere] * (2 + len(arrays) + (len(tokens) if last else 0))
            + [whole] * (len(acc) + (3 if last else 0)),
            out_specs=[whole] * (2 if last else 1),
            scratch_shapes=[
                pltpu.VMEM((len(groups), 2, rows, 2 * HD), bf16),
                pltpu.VMEM((len(groups), 2 * count, rows), bf16),
                pltpu.SemaphoreType.DMA((len(groups), 5)),
            ],
            compiler_params=params,
            cost_estimate=pl.CostEstimate(
                flops=2 * 2 * count * rows * 4 * HD * len(groups),
                bytes_accessed=2 * rows * (4 * HD + 2 * count) * len(groups),
                transcendentals=0,
            ),
            name="project",
        )(
            place, normed, normed_other, *arrays, *(tokens if last else []), *acc,
            *((cosine, sine, key_gain[None]) if last else ()),
        )
        acc = [outs[-1]]

    kv_own, kv_other = outs
    result = None
    for cross, kv in enumerate((kv_own, kv_other)):
        sources = [kv if d == 0 and not cross else along_ctx(kv, d, cross) for d in range(m)]

        def block(step, place, needs, cross=cross):
            return (0, lax.rem(place[0] + cross, 2) * 2 + step)

        earlier = [] if result is None else [result]
        result = pl.pallas_call(
            functools.partial(attend_kernel, m, count),
            out_shape=jax.ShapeDtypeStruct((count, KVH * G * HD), bf16),
            grid_spec=pltpu.PrefetchScalarGridSpec(
                num_scalar_prefetch=2,
                grid=(2,),
                in_specs=[pl.BlockSpec((count, G * HD), block)]
                + [whole] * (1 + m)
                + [pl.BlockSpec(memory_space=pl.ANY)] * len(earlier),
                out_specs=pl.BlockSpec((count, G * HD), block),
                scratch_shapes=[
                    pltpu.VMEM((m * count, HD), bf16),
                    pltpu.VMEM((m * count, HD), bf16),
                ],
            ),
            input_output_aliases={4 + m: 0} if earlier else {},
            compiler_params=params,
            cost_estimate=pl.CostEstimate(
                flops=2 * count * m * count * KVH * G * HD,
                bytes_accessed=2 * count * KVH * G * HD,
                transcendentals=count * m * count * KVH * G // 2,
            ),
            name="attend",
        )(core.astype(jnp.int32)[None], needs, queries[0], bias, *sources, *earlier)
    return result[None]


def solution(mesh):
    n, m = mesh.shape["fsdp"], mesh.shape["ctx"]
    sizes = (n // 4, 2, 2, m // 2, 2)
    fine = Mesh(mesh.devices.reshape(sizes), ("z", "y", "core", "ctx", "x"))
    fsdp, ctx = ("z", "y", "core"), ("ctx", "x")
    placed = (
        P(fsdp, ctx, None),
        P(fsdp, ctx, None),
        P(),
        P(),
        P(fsdp, None),
        P(fsdp, None),
        P(fsdp, ctx),
        P(fsdp, ctx),
    )
    return jax.shard_map(
        functools.partial(on_device, sizes),
        mesh=fine,
        in_specs=placed,
        out_specs=P(fsdp, ctx, None),
        check_vma=False,
    )
```

```python
import functools
import math

import jax
import jax.numpy as jnp
import numpy as np
from jax import lax
from jax.experimental import pallas as pl
from jax.experimental.pallas import tpu as pltpu
from jax.sharding import Mesh
from jax.sharding import PartitionSpec as P

KVH = 4
HD = 128
G = 8
EPS = 1e-06
THETA = 1000000.0
MASKED = -1e30
VMEM_LIMIT = 24 * 2**20
NORM_ROWS = 64


def norm_kernel(chunks, hidden, gain, out, held, sems):
    steps = held.shape[0] // NORM_ROWS
    copies = []
    for i in range(steps):
        at = pl.ds(i * NORM_ROWS, NORM_ROWS)
        copies.append(pltpu.make_async_copy(hidden.at[at], held.at[at], sems.at[i]))
        copies[-1].start()
    for i, copy in enumerate(copies):
        copy.wait()
        at = pl.ds(i * NORM_ROWS, NORM_ROWS)
        inputs = held[at, :].astype(jnp.float32)
        scale = lax.rsqrt(jnp.mean(inputs * inputs, axis=-1, keepdims=True) + EPS)
        normed = (inputs * scale * gain[...]).astype(jnp.bfloat16)
        rows = normed.shape[1] // chunks
        for j in range(chunks):
            out[j, at, :] = normed[:, j * rows : (j + 1) * rows]


def project_kernel(chips_z, groups, first, last, count, place, own, other, *rest):
    z, y, x = place[0], place[1], place[2]
    rest = list(rest)
    weight, lhs, sems = rest[-3:]
    waits = []
    for g, (k, near) in enumerate(groups):
        p = lax.rem(z - k + chips_z, chips_z)
        chunk = p * 2 + (y if near else 1 - y)
        pairs = [
            (own.at[chunk], lhs.at[g, pl.ds(0, count)]),
            (other.at[chunk], lhs.at[g, pl.ds(count, count)]),
        ]
        if k == 0:
            pairs.append((rest.pop(0), weight.at[g]))
        else:
            pairs.append((rest.pop(0), weight.at[g, x]))
            pairs.append((rest.pop(0), weight.at[g, 1 - x]))
        copies = [
            pltpu.make_async_copy(source, target, sems.at[g, i])
            for i, (source, target) in enumerate(pairs)
        ]
        for copy in copies:
            copy.start()
        waits.append(copies)
    earlier = None if first else rest.pop(0)
    terms = [None, None]
    for g, copies in enumerate(waits):
        for copy in copies:
            copy.wait()
        for half in range(2):
            part = jnp.dot(lhs[g], weight[g, half], preferred_element_type=jnp.float32)
            terms[half] = part if terms[half] is None else terms[half] + part
    for half in range(2):
        if not first:
            terms[half] += earlier[half]
        if not last:
            rest[0][half] = terms[half]
    if not last:
        return
    cosine, sine, gain = rest[:3]
    outs = rest[3:5]
    for head in range(2):
        columns = slice(head * HD, (head + 1) * HD)
        for part, out in enumerate(outs):
            at = slice(part * count, (part + 1) * count)
            raw = terms[0][at, columns]
            normk = raw * lax.rsqrt(jnp.mean(raw * raw, axis=-1, keepdims=True) + EPS) * gain[...]
            turned = normk * cosine[at, :] + pltpu.roll(normk, HD // 2, 1) * sine[at, :]
            out[:, 2 * head * HD : (2 * head + 1) * HD] = turned.astype(jnp.bfloat16)
            out[:, (2 * head + 1) * HD : (2 * head + 2) * HD] = terms[1][at, columns].astype(
                jnp.bfloat16
            )


def mask_kernel(*refs):
    pieces, (bias, needs) = refs[:-2], refs[-2:]
    count = bias.shape[0]
    half_rows = count // 2
    seg_q, pos_q = (
        jnp.transpose(jnp.broadcast_to(pieces[0][i : i + 1, :], (half_rows, count)))
        for i in range(2)
    )
    half_width = len(pieces) * half_rows
    for half in range(2):
        for i, piece in enumerate(pieces):
            at = slice(half * half_rows, (half + 1) * half_rows)
            allowed = (piece[:1, at] == seg_q) & (piece[1:, at] <= pos_q)
            there = half * half_width + i * half_rows
            bias[:, there : there + half_rows] = jnp.where(allowed, 0.0, MASKED)
    for tile in range(2):
        rows = slice(tile * half_rows, (tile + 1) * half_rows)
        found = [
            jnp.max(bias[rows, half * half_width : (half + 1) * half_width]) == 0.0
            for half in range(2)
        ]
        needs[tile] = found[0].astype(jnp.int32) + 2 * found[1].astype(jnp.int32)


def attend_kernel(pieces, count, place, needs, queries, bias, *rest):
    sources, (out, keys, values) = rest[:pieces], rest[-3:]
    step = pl.program_id(0)
    tile_rows = count // 2
    length = pieces * tile_rows

    for head in range(2):

        @pl.when(step == head)
        def _():
            left = 2 * head * HD
            for i, source in enumerate(sources):
                for half in range(2):
                    here = slice(half * tile_rows, (half + 1) * tile_rows)
                    there = half * length + i * tile_rows
                    keys[there : there + tile_rows, :] = source[here, left : left + HD]
                    values[there : there + tile_rows, :] = source[here, left + HD : left + 2 * HD]

    factor = math.log2(math.e) / math.sqrt(HD)

    def tile_body(tile, low, high):
        rows = slice(tile * tile_rows, (tile + 1) * tile_rows)
        k, v, b = keys[low:high, :], values[low:high, :], bias[rows, low:high]

        def score(pair):
            q = jnp.concatenate(
                [queries[rows, g * HD : (g + 1) * HD] for g in (2 * pair, 2 * pair + 1)], axis=0
            )
            return lax.dot_general(
                q, k, (((1,), (1,)), ((), ())), preferred_element_type=jnp.float32
            )

        ahead = score(0)
        for pair in range(G // 2):
            scores = ahead.reshape(2, tile_rows, high - low) + b[None]
            if pair + 1 < G // 2:
                ahead = score(pair + 1)
            top = jnp.max(scores, axis=-1, keepdims=True)
            weights = jnp.exp2((scores - top) * factor)
            total = jnp.sum(weights, axis=-1, keepdims=True)
            summed = jnp.dot(
                weights.astype(jnp.bfloat16).reshape(2 * tile_rows, high - low),
                v,
                preferred_element_type=jnp.float32,
            ).reshape(2, tile_rows, HD)
            result = (summed * (1.0 / total)).astype(jnp.bfloat16)
            for i in range(2):
                g = 2 * pair + i
                out[rows, g * HD : (g + 1) * HD] = result[i]

    for tile in range(2):
        for need, low, high in ((1, 0, length), (2, length, 2 * length), (3, 0, 2 * length)):

            @pl.when(needs[tile] == need)
            def _():
                tile_body(tile, low, high)


def swap(array, axis):
    return lax.ppermute(array, axis, [(0, 1), (1, 0)])


def on_device(
    sizes, hidden, queries, norm_gain, key_gain, k_weight, v_weight, segment, position
):
    chips_z, groups = sizes[0], sizes[3]
    count, width = hidden.shape[1:]
    own_rows = k_weight.shape[0]
    rows = 2 * own_rows
    chunks = 2 * chips_z
    m = 2 * groups
    z, y = lax.axis_index("z"), lax.axis_index("y")
    core, x = lax.axis_index("core"), lax.axis_index("x")
    bf16 = jnp.bfloat16
    whole = pl.BlockSpec(memory_space=pltpu.VMEM)
    params = pltpu.CompilerParams(vmem_limit_bytes=VMEM_LIMIT)

    def along_ctx(array, d, cross=False):
        pairs = []
        for c in range(2):
            for i in range(m):
                pairs.append((c * m + i, (c ^ int(cross)) * m + (i + d) % m))
        return lax.ppermute(array, ("core", "ctx", "x"), pairs)

    def columns(which):
        at = which * 2 * HD
        return jnp.stack(
            [lax.dynamic_slice_in_dim(w, at, 2 * HD, 1) for w in (k_weight, v_weight)]
        )

    taken = swap(columns(1 - core), "core")
    kept = columns(core)
    chip = lax.dynamic_update_slice(
        jnp.zeros((2, rows, 2 * HD), bf16), kept, (0, core * own_rows, 0)
    )
    chip = lax.dynamic_update_slice(chip, taken, (0, (1 - core) * own_rows, 0))
    hidden, segment, position, chip = lax.optimization_barrier((hidden, segment, position, chip))
    normed = pl.pallas_call(
        functools.partial(norm_kernel, chunks),
        out_shape=jax.ShapeDtypeStruct((chunks, count, rows), bf16),
        in_specs=[pl.BlockSpec(memory_space=pltpu.HBM), whole],
        out_specs=whole,
        scratch_shapes=[
            pltpu.VMEM((count, width), bf16),
            pltpu.SemaphoreType.DMA((count // NORM_ROWS,)),
        ],
        compiler_params=params,
        cost_estimate=pl.CostEstimate(
            flops=4 * count * width, bytes_accessed=4 * count * width, transcendentals=0
        ),
        name="norm",
    )(hidden[0], norm_gain[None])
    ints = jnp.concatenate([segment, position])
    ints_all = [ints] + [along_ctx(ints, d) for d in range(1, m)]
    ints_other = swap(ints, "core")

    def ring(array, step):
        return lax.ppermute(array, "z", [(i, (i + step) % chips_z) for i in range(chips_z)])

    tie = lax.optimization_barrier
    middle = chips_z // 2
    mine = {0: lax.dynamic_index_in_dim(chip, x, 0, keepdims=False)}
    across, beside, corner = {}, {}, {}
    chip_beside = swap(chip, "y")
    mine[1], mine[chips_z - 1] = ring(mine[0], 1), ring(mine[0], -1)
    mine[1], normed, ints_all, ints_other = tie((mine[1], normed, ints_all, ints_other))
    for r in range(1, middle + 1):
        if r > 1:
            mine[r], beside[r - 1], across[chips_z - r + 1] = tie(
                (mine[r], beside[r - 1], across[chips_z - r + 1])
            )
        if r < middle:
            mine[r + 1] = ring(mine[r], 1)
        beside[r], across[r] = swap(mine[r], "y"), swap(mine[r], "x")
        if r == 1:
            mine[chips_z - 1], across[1], chip_beside, normed = tie(
                (mine[chips_z - 1], across[1], chip_beside, normed)
            )
            normed_other = swap(normed, "core")
        if r < middle:
            k = chips_z - r
            if k - 1 > middle:
                mine[k - 1] = ring(mine[k], -1)
            beside[k], across[k] = swap(mine[k], "y"), swap(mine[k], "x")
        if r == 1:
            across[chips_z - 1], normed_other = tie((across[chips_z - 1], normed_other))
    for k in range(1, chips_z):
        corner[k] = swap(beside[k], "x") if k <= middle else swap(across[k], "y")

    where = jnp.concatenate([position[0], ints_other[1]]).astype(jnp.float32)
    half = HD // 2
    freq = np.exp(np.arange(half, dtype=np.float32) * np.float32(-2.0 * math.log(THETA) / HD))
    angle = where[:, None] * freq[None, :]
    cosine, sine = jnp.cos(angle), jnp.sin(angle)
    cosine = jnp.concatenate([cosine, cosine], axis=1)
    sine = jnp.concatenate([-sine, sine], axis=1)
    bias, needs = pl.pallas_call(
        mask_kernel,
        out_shape=[
            jax.ShapeDtypeStruct((count, m * count), jnp.float32),
            jax.ShapeDtypeStruct((2,), jnp.int32),
        ],
        in_specs=[whole] * m,
        out_specs=[whole, pl.BlockSpec(memory_space=pltpu.SMEM)],
        compiler_params=params,
        name="mask",
    )(*ints_all)

    place = jnp.stack([z, y, x]).astype(jnp.int32)
    acc_shape = jax.ShapeDtypeStruct((2, 2 * count, 2 * HD), jnp.float32)
    kv_shape = jax.ShapeDtypeStruct((count, 4 * HD), bf16)
    early = [(0, True), (0, False)]
    early += [(k, True) for k in range(1, chips_z) if k != middle]
    late = [(middle, True)] + [(k, False) for k in range(1, chips_z) if k != middle]
    final = [(middle, False)]
    acc = []
    for groups in (early, late, final):
        first, last = groups is early, groups is final
        arrays = []
        for k, near in groups:
            if k == 0:
                arrays.append(chip if near else chip_beside)
            else:
                arrays += [mine[k], across[k]] if near else [beside[k], corner[k]]
        anywhere = pl.BlockSpec(memory_space=pl.ANY)
        outs = pl.pallas_call(
            functools.partial(project_kernel, chips_z, groups, first, last, count),
            out_shape=[kv_shape] * 2 if last else [acc_shape],
            in_specs=[pl.BlockSpec(memory_space=pltpu.SMEM)]
            + [anywhere] * (2 + len(arrays))
            + [whole] * (len(acc) + (3 if last else 0)),
            out_specs=[whole] * (2 if last else 1),
            scratch_shapes=[
                pltpu.VMEM((len(groups), 2, rows, 2 * HD), bf16),
                pltpu.VMEM((len(groups), 2 * count, rows), bf16),
                pltpu.SemaphoreType.DMA((len(groups), 4)),
            ],
            compiler_params=params,
            cost_estimate=pl.CostEstimate(
                flops=2 * 2 * count * rows * 4 * HD * len(groups),
                bytes_accessed=2 * rows * (4 * HD + 2 * count) * len(groups),
                transcendentals=0,
            ),
            name="project",
        )(
            place, normed, normed_other, *arrays, *acc,
            *((cosine, sine, key_gain[None]) if last else ()),
        )
        acc = [outs[-1]]

    kv_own, kv_other = outs
    result = None
    for cross, kv in enumerate((kv_own, kv_other)):
        sources = [kv if d == 0 and not cross else along_ctx(kv, d, cross) for d in range(m)]

        def block(step, place, needs, cross=cross):
            return (0, lax.rem(place[0] + cross, 2) * 2 + step)

        earlier = [] if result is None else [result]
        result = pl.pallas_call(
            functools.partial(attend_kernel, m, count),
            out_shape=jax.ShapeDtypeStruct((count, KVH * G * HD), bf16),
            grid_spec=pltpu.PrefetchScalarGridSpec(
                num_scalar_prefetch=2,
                grid=(2,),
                in_specs=[pl.BlockSpec((count, G * HD), block)]
                + [whole] * (1 + m)
                + [pl.BlockSpec(memory_space=pl.ANY)] * len(earlier),
                out_specs=pl.BlockSpec((count, G * HD), block),
                scratch_shapes=[
                    pltpu.VMEM((m * count, HD), bf16),
                    pltpu.VMEM((m * count, HD), bf16),
                ],
            ),
            input_output_aliases={4 + m: 0} if earlier else {},
            compiler_params=params,
            cost_estimate=pl.CostEstimate(
                flops=2 * count * m * count * KVH * G * HD,
                bytes_accessed=2 * count * KVH * G * HD,
                transcendentals=count * m * count * KVH * G // 2,
            ),
            name="attend",
        )(core.astype(jnp.int32)[None], needs, queries[0], bias, *sources, *earlier)
    return result[None]


def solution(mesh):
    n, m = mesh.shape["fsdp"], mesh.shape["ctx"]
    sizes = (n // 4, 2, 2, m // 2, 2)
    fine = Mesh(mesh.devices.reshape(sizes), ("z", "y", "core", "ctx", "x"))
    fsdp, ctx = ("z", "y", "core"), ("ctx", "x")
    placed = (
        P(fsdp, ctx, None),
        P(fsdp, ctx, None),
        P(),
        P(),
        P(fsdp, None),
        P(fsdp, None),
        P(fsdp, ctx),
        P(fsdp, ctx),
    )
    return jax.shard_map(
        functools.partial(on_device, sizes),
        mesh=fine,
        in_specs=placed,
        out_specs=P(fsdp, ctx, None),
        check_vma=False,
    )
```

```python
import functools
import math

import jax
import jax.numpy as jnp
import numpy as np
from jax import lax
from jax.experimental import pallas as pl
from jax.experimental.pallas import tpu as pltpu
from jax.sharding import Mesh
from jax.sharding import PartitionSpec as P

KVH = 4
HD = 128
G = 8
EPS = 1e-06
THETA = 1000000.0
MASKED = -1e30
VMEM_LIMIT = 24 * 2**20
NORM_ROWS = 64


def norm_kernel(chunks, hidden, gain, out, held, sems):
    steps = held.shape[0] // NORM_ROWS
    copies = []
    for i in range(steps):
        at = pl.ds(i * NORM_ROWS, NORM_ROWS)
        copies.append(pltpu.make_async_copy(hidden.at[at], held.at[at], sems.at[i]))
        copies[-1].start()
    for i, copy in enumerate(copies):
        copy.wait()
        at = pl.ds(i * NORM_ROWS, NORM_ROWS)
        inputs = held[at, :].astype(jnp.float32)
        scale = lax.rsqrt(jnp.mean(inputs * inputs, axis=-1, keepdims=True) + EPS)
        normed = (inputs * scale * gain[...]).astype(jnp.bfloat16)
        rows = normed.shape[1] // chunks
        for j in range(chunks):
            out[j, at, :] = normed[:, j * rows : (j + 1) * rows]


def project_kernel(groups, first, last, count, place, own, other, *rest):
    z, y, x = place[0], place[1], place[2]
    rest = list(rest)
    weight, lhs, sems = rest[-3:]
    waits = []
    for g, (k, near) in enumerate(groups):
        p = z ^ k
        chunk = p * 2 + (y if near else 1 - y)
        pairs = [
            (own.at[chunk], lhs.at[g, pl.ds(0, count)]),
            (other.at[chunk], lhs.at[g, pl.ds(count, count)]),
        ]
        if k == 0:
            pairs.append((rest.pop(0), weight.at[g]))
        else:
            pairs.append((rest.pop(0), weight.at[g, x]))
            pairs.append((rest.pop(0), weight.at[g, 1 - x]))
        copies = [
            pltpu.make_async_copy(source, target, sems.at[g, i])
            for i, (source, target) in enumerate(pairs)
        ]
        for copy in copies:
            copy.start()
        waits.append(copies)
    earlier = None if first else rest.pop(0)
    terms = [None, None]
    for g, copies in enumerate(waits):
        for copy in copies:
            copy.wait()
        for half in range(2):
            part = jnp.dot(lhs[g], weight[g, half], preferred_element_type=jnp.float32)
            terms[half] = part if terms[half] is None else terms[half] + part
    for half in range(2):
        if not first:
            terms[half] += earlier[half]
        if not last:
            rest[0][half] = terms[half]
    if not last:
        return
    cosine, sine, gain = rest[:3]
    outs = rest[3:5]
    for head in range(2):
        columns = slice(head * HD, (head + 1) * HD)
        for part, out in enumerate(outs):
            at = slice(part * count, (part + 1) * count)
            raw = terms[0][at, columns]
            normk = raw * lax.rsqrt(jnp.mean(raw * raw, axis=-1, keepdims=True) + EPS) * gain[...]
            turned = normk * cosine[at, :] + pltpu.roll(normk, HD // 2, 1) * sine[at, :]
            out[:, 2 * head * HD : (2 * head + 1) * HD] = turned.astype(jnp.bfloat16)
            out[:, (2 * head + 1) * HD : (2 * head + 2) * HD] = terms[1][at, columns].astype(
                jnp.bfloat16
            )


def mask_kernel(*refs):
    pieces, (bias, needs) = refs[:-2], refs[-2:]
    count = bias.shape[0]
    half_rows = count // 2
    seg_q, pos_q = (
        jnp.transpose(jnp.broadcast_to(pieces[0][i : i + 1, :], (half_rows, count)))
        for i in range(2)
    )
    half_width = len(pieces) * half_rows
    for half in range(2):
        for i, piece in enumerate(pieces):
            at = slice(half * half_rows, (half + 1) * half_rows)
            allowed = (piece[:1, at] == seg_q) & (piece[1:, at] <= pos_q)
            there = half * half_width + i * half_rows
            bias[:, there : there + half_rows] = jnp.where(allowed, 0.0, MASKED)
    for tile in range(2):
        rows = slice(tile * half_rows, (tile + 1) * half_rows)
        found = [
            jnp.max(bias[rows, half * half_width : (half + 1) * half_width]) == 0.0
            for half in range(2)
        ]
        needs[tile] = found[0].astype(jnp.int32) + 2 * found[1].astype(jnp.int32)


def attend_kernel(pieces, count, place, needs, queries, bias, *rest):
    sources, (out, keys, values) = rest[:pieces], rest[-3:]
    step = pl.program_id(0)
    tile_rows = count // 2
    length = pieces * tile_rows

    for head in range(2):

        @pl.when(step == head)
        def _():
            left = 2 * head * HD
            for i, source in enumerate(sources):
                for half in range(2):
                    here = slice(half * tile_rows, (half + 1) * tile_rows)
                    there = half * length + i * tile_rows
                    keys[there : there + tile_rows, :] = source[here, left : left + HD]
                    values[there : there + tile_rows, :] = source[here, left + HD : left + 2 * HD]

    factor = math.log2(math.e) / math.sqrt(HD)

    def tile_body(tile, low, high):
        rows = slice(tile * tile_rows, (tile + 1) * tile_rows)
        k, v, b = keys[low:high, :], values[low:high, :], bias[rows, low:high]

        def score(pair):
            q = jnp.concatenate(
                [queries[rows, g * HD : (g + 1) * HD] for g in (2 * pair, 2 * pair + 1)], axis=0
            )
            return lax.dot_general(
                q, k, (((1,), (1,)), ((), ())), preferred_element_type=jnp.float32
            )

        ahead = score(0)
        for pair in range(G // 2):
            scores = ahead.reshape(2, tile_rows, high - low) + b[None]
            if pair + 1 < G // 2:
                ahead = score(pair + 1)
            top = jnp.max(scores, axis=-1, keepdims=True)
            weights = jnp.exp2((scores - top) * factor)
            total = jnp.sum(weights, axis=-1, keepdims=True)
            summed = jnp.dot(
                weights.astype(jnp.bfloat16).reshape(2 * tile_rows, high - low),
                v,
                preferred_element_type=jnp.float32,
            ).reshape(2, tile_rows, HD)
            result = (summed * (1.0 / total)).astype(jnp.bfloat16)
            for i in range(2):
                g = 2 * pair + i
                out[rows, g * HD : (g + 1) * HD] = result[i]

    for tile in range(2):
        for need, low, high in ((1, 0, length), (2, length, 2 * length), (3, 0, 2 * length)):

            @pl.when(needs[tile] == need)
            def _():
                tile_body(tile, low, high)


def swap(array, axis):
    return lax.ppermute(array, axis, [(0, 1), (1, 0)])


def on_device(
    sizes, hidden, queries, norm_gain, key_gain, k_weight, v_weight, segment, position
):
    chips_z, groups = sizes[0], sizes[3]
    count, width = hidden.shape[1:]
    own_rows = k_weight.shape[0]
    rows = 2 * own_rows
    chunks = 2 * chips_z
    m = 2 * groups
    z, y = lax.axis_index("z"), lax.axis_index("y")
    core, x = lax.axis_index("core"), lax.axis_index("x")
    bf16 = jnp.bfloat16
    whole = pl.BlockSpec(memory_space=pltpu.VMEM)
    params = pltpu.CompilerParams(vmem_limit_bytes=VMEM_LIMIT)

    def along_ctx(array, d, cross=False):
        pairs = []
        for c in range(2):
            for i in range(m):
                pairs.append((c * m + i, (c ^ int(cross)) * m + (i + d) % m))
        return lax.ppermute(array, ("core", "ctx", "x"), pairs)

    def columns(which):
        at = which * 2 * HD
        return jnp.stack(
            [lax.dynamic_slice_in_dim(w, at, 2 * HD, 1) for w in (k_weight, v_weight)]
        )

    taken = swap(columns(1 - core), "core")
    kept = columns(core)
    chip = lax.dynamic_update_slice(
        jnp.zeros((2, rows, 2 * HD), bf16), kept, (0, core * own_rows, 0)
    )
    chip = lax.dynamic_update_slice(chip, taken, (0, (1 - core) * own_rows, 0))
    hidden, segment, position, chip = lax.optimization_barrier((hidden, segment, position, chip))
    normed = pl.pallas_call(
        functools.partial(norm_kernel, chunks),
        out_shape=jax.ShapeDtypeStruct((chunks, count, rows), bf16),
        in_specs=[pl.BlockSpec(memory_space=pltpu.HBM), whole],
        out_specs=whole,
        scratch_shapes=[
            pltpu.VMEM((count, width), bf16),
            pltpu.SemaphoreType.DMA((count // NORM_ROWS,)),
        ],
        compiler_params=params,
        cost_estimate=pl.CostEstimate(
            flops=4 * count * width, bytes_accessed=4 * count * width, transcendentals=0
        ),
        name="norm",
    )(hidden[0], norm_gain[None])
    ints = jnp.concatenate([segment, position])
    ints_all = [ints] + [along_ctx(ints, d) for d in range(1, m)]
    ints_other = swap(ints, "core")

    def along_z(array, k):
        return lax.ppermute(array, "z", [(i, i ^ k) for i in range(chips_z)])

    tie = lax.optimization_barrier
    mine = {0: lax.dynamic_index_in_dim(chip, x, 0, keepdims=False)}
    across, beside, corner = {}, {}, {}
    chip_beside = swap(chip, "y")
    for k in range(1, chips_z):
        low = k & -k
        mine[k] = along_z(mine[k - low], low)
        if k == 2:
            tied = (mine[k], across[1], chip_beside, normed, ints_all, ints_other)
            mine[k], across[1], chip_beside, normed, ints_all, ints_other = tie(tied)
            normed_other = swap(normed, "core")
        elif k == 3:
            tied = (mine[k], across[2], beside[1], normed_other)
            mine[k], across[2], beside[1], normed_other = tie(tied)
        elif k > 3:
            tied = (mine[k], across[k - 1], beside[k - 2])
            mine[k], across[k - 1], beside[k - 2] = tie(tied)
        across[k], beside[k] = swap(mine[k], "x"), swap(mine[k], "y")
    end = chips_z - 1
    for k in range(1, chips_z):
        corner[k] = swap(across[k], "y") if k == end else swap(beside[k], "x")

    where = jnp.concatenate([position[0], ints_other[1]]).astype(jnp.float32)
    half = HD // 2
    freq = np.exp(np.arange(half, dtype=np.float32) * np.float32(-2.0 * math.log(THETA) / HD))
    angle = where[:, None] * freq[None, :]
    cosine, sine = jnp.cos(angle), jnp.sin(angle)
    cosine = jnp.concatenate([cosine, cosine], axis=1)
    sine = jnp.concatenate([-sine, sine], axis=1)
    bias, needs = pl.pallas_call(
        mask_kernel,
        out_shape=[
            jax.ShapeDtypeStruct((count, m * count), jnp.float32),
            jax.ShapeDtypeStruct((2,), jnp.int32),
        ],
        in_specs=[whole] * m,
        out_specs=[whole, pl.BlockSpec(memory_space=pltpu.SMEM)],
        compiler_params=params,
        name="mask",
    )(*ints_all)

    place = jnp.stack([z, y, x]).astype(jnp.int32)
    acc_shape = jax.ShapeDtypeStruct((2, 2 * count, 2 * HD), jnp.float32)
    kv_shape = jax.ShapeDtypeStruct((count, 4 * HD), bf16)
    final = [(end - 1, False)]
    late = [(end, True)] + [(k, False) for k in range(1, chips_z) if k != end - 1]
    early = [(0, True), (0, False)] + [(k, True) for k in range(1, end)]
    acc = []
    for groups in (early, late, final):
        first, last = groups is early, groups is final
        arrays = []
        for k, near in groups:
            if k == 0:
                arrays.append(chip if near else chip_beside)
            else:
                arrays += [mine[k], across[k]] if near else [beside[k], corner[k]]
        anywhere = pl.BlockSpec(memory_space=pl.ANY)
        outs = pl.pallas_call(
            functools.partial(project_kernel, groups, first, last, count),
            out_shape=[kv_shape] * 2 if last else [acc_shape],
            in_specs=[pl.BlockSpec(memory_space=pltpu.SMEM)]
            + [anywhere] * (2 + len(arrays))
            + [whole] * (len(acc) + (3 if last else 0)),
            out_specs=[whole] * (2 if last else 1),
            scratch_shapes=[
                pltpu.VMEM((len(groups), 2, rows, 2 * HD), bf16),
                pltpu.VMEM((len(groups), 2 * count, rows), bf16),
                pltpu.SemaphoreType.DMA((len(groups), 4)),
            ],
            compiler_params=params,
            cost_estimate=pl.CostEstimate(
                flops=2 * 2 * count * rows * 4 * HD * len(groups),
                bytes_accessed=2 * rows * (4 * HD + 2 * count) * len(groups),
                transcendentals=0,
            ),
            name="project",
        )(
            place, normed, normed_other, *arrays, *acc,
            *((cosine, sine, key_gain[None]) if last else ()),
        )
        acc = [outs[-1]]

    kv_own, kv_other = outs
    result = None
    for cross, kv in enumerate((kv_own, kv_other)):
        sources = [kv if d == 0 and not cross else along_ctx(kv, d, cross) for d in range(m)]

        def block(step, place, needs, cross=cross):
            return (0, lax.rem(place[0] + cross, 2) * 2 + step)

        earlier = [] if result is None else [result]
        result = pl.pallas_call(
            functools.partial(attend_kernel, m, count),
            out_shape=jax.ShapeDtypeStruct((count, KVH * G * HD), bf16),
            grid_spec=pltpu.PrefetchScalarGridSpec(
                num_scalar_prefetch=2,
                grid=(2,),
                in_specs=[pl.BlockSpec((count, G * HD), block)]
                + [whole] * (1 + m)
                + [pl.BlockSpec(memory_space=pl.ANY)] * len(earlier),
                out_specs=pl.BlockSpec((count, G * HD), block),
                scratch_shapes=[
                    pltpu.VMEM((m * count, HD), bf16),
                    pltpu.VMEM((m * count, HD), bf16),
                ],
            ),
            input_output_aliases={4 + m: 0} if earlier else {},
            compiler_params=params,
            cost_estimate=pl.CostEstimate(
                flops=2 * count * m * count * KVH * G * HD,
                bytes_accessed=2 * count * KVH * G * HD,
                transcendentals=count * m * count * KVH * G // 2,
            ),
            name="attend",
        )(core.astype(jnp.int32)[None], needs, queries[0], bias, *sources, *earlier)
    return result[None]


def solution(mesh):
    n, m = mesh.shape["fsdp"], mesh.shape["ctx"]
    sizes = (n // 4, 2, 2, m // 2, 2)
    fine = Mesh(mesh.devices.reshape(sizes), ("z", "y", "core", "ctx", "x"))
    fsdp, ctx = ("z", "y", "core"), ("ctx", "x")
    placed = (
        P(fsdp, ctx, None),
        P(fsdp, ctx, None),
        P(),
        P(),
        P(fsdp, None),
        P(fsdp, None),
        P(fsdp, ctx),
        P(fsdp, ctx),
    )
    return jax.shard_map(
        functools.partial(on_device, sizes),
        mesh=fine,
        in_specs=placed,
        out_specs=P(fsdp, ctx, None),
        check_vma=False,
    )
```

```python
import functools
import math

import jax
import jax.numpy as jnp
import numpy as np
from jax import lax
from jax.experimental import pallas as pl
from jax.experimental.pallas import tpu as pltpu
from jax.sharding import Mesh
from jax.sharding import PartitionSpec as P

KVH = 4
HD = 128
G = 8
EPS = 1e-06
THETA = 1000000.0
MASKED = -1e30
VMEM_LIMIT = 24 * 2**20
NORM_ROWS = 64
WIDE = 4


def norm_kernel(chunks, hidden, gain, out, held, sems):
    steps = held.shape[0] // NORM_ROWS
    copies = []
    for i in range(steps):
        at = pl.ds(i * NORM_ROWS, NORM_ROWS)
        copies.append(pltpu.make_async_copy(hidden.at[at], held.at[at], sems.at[i]))
        copies[-1].start()
    for i, copy in enumerate(copies):
        copy.wait()
        at = pl.ds(i * NORM_ROWS, NORM_ROWS)
        inputs = held[at, :].astype(jnp.float32)
        scale = lax.rsqrt(jnp.mean(inputs * inputs, axis=-1, keepdims=True) + EPS)
        normed = (inputs * scale * gain[...]).astype(jnp.bfloat16)
        rows = normed.shape[1] // chunks
        for j in range(chunks):
            out[j, at, :] = normed[:, j * rows : (j + 1) * rows]


def project_kernel(groups, first, last, count, place, own, other, *rest):
    z, y, x = place[0], place[1], place[2]
    rest = list(rest)
    weight, lhs, sems = rest[-3:]
    waits = []
    for g, (k, near) in enumerate(groups):
        p = z ^ k
        chunk = p * 2 + (y if near else 1 - y)
        pairs = [
            (own.at[chunk], lhs.at[g, pl.ds(0, count)]),
            (other.at[chunk], lhs.at[g, pl.ds(count, count)]),
        ]
        if k == 0:
            pairs.append((rest.pop(0), weight.at[g]))
        else:
            pairs.append((rest.pop(0), weight.at[g, x]))
            pairs.append((rest.pop(0), weight.at[g, 1 - x]))
        copies = [
            pltpu.make_async_copy(source, target, sems.at[g, i])
            for i, (source, target) in enumerate(pairs)
        ]
        for copy in copies:
            copy.start()
        waits.append(copies)
    earlier = None if first else rest.pop(0)
    terms = [None, None]
    for g, copies in enumerate(waits):
        for copy in copies:
            copy.wait()
        for half in range(2):
            part = jnp.dot(lhs[g], weight[g, half], preferred_element_type=jnp.float32)
            terms[half] = part if terms[half] is None else terms[half] + part
    for half in range(2):
        if not first:
            terms[half] += earlier[half]
        if not last:
            rest[0][half] = terms[half]
    if not last:
        return
    cosine, sine, gain = rest[:3]
    outs = rest[3:5]
    for head in range(2):
        columns = slice(head * HD, (head + 1) * HD)
        for part, out in enumerate(outs):
            at = slice(part * count, (part + 1) * count)
            raw = terms[0][at, columns]
            normk = raw * lax.rsqrt(jnp.mean(raw * raw, axis=-1, keepdims=True) + EPS) * gain[...]
            turned = normk * cosine[at, :] + pltpu.roll(normk, HD // 2, 1) * sine[at, :]
            out[:, 2 * head * HD : (2 * head + 1) * HD] = turned.astype(jnp.bfloat16)
            out[:, (2 * head + 1) * HD : (2 * head + 2) * HD] = terms[1][at, columns].astype(
                jnp.bfloat16
            )


def mask_kernel(*refs):
    pieces, (bias, needs) = refs[:-2], refs[-2:]
    count = bias.shape[0]
    half_rows = count // 2
    seg_q, pos_q = (
        jnp.transpose(jnp.broadcast_to(pieces[0][i : i + 1, :], (half_rows, count)))
        for i in range(2)
    )
    half_width = len(pieces) * half_rows
    for half in range(2):
        for i, piece in enumerate(pieces):
            at = slice(half * half_rows, (half + 1) * half_rows)
            allowed = (piece[:1, at] == seg_q) & (piece[1:, at] <= pos_q)
            there = half * half_width + i * half_rows
            bias[:, there : there + half_rows] = jnp.where(allowed, 0.0, MASKED)
    for tile in range(2):
        rows = slice(tile * half_rows, (tile + 1) * half_rows)
        found = [
            jnp.max(bias[rows, half * half_width : (half + 1) * half_width]) == 0.0
            for half in range(2)
        ]
        needs[tile] = found[0].astype(jnp.int32) + 2 * found[1].astype(jnp.int32)


def attend_kernel(pieces, count, place, needs, queries, bias, *rest):
    sources, (out, keys, values) = rest[:pieces], rest[-3:]
    step = pl.program_id(0)
    tile_rows = count // 2
    length = pieces * tile_rows

    for head in range(2):

        @pl.when(step == head)
        def _():
            left = 2 * head * HD
            for i, source in enumerate(sources):
                for half in range(2):
                    here = slice(half * tile_rows, (half + 1) * tile_rows)
                    there = half * length + i * tile_rows
                    keys[there : there + tile_rows, :] = source[here, left : left + HD]
                    values[there : there + tile_rows, :] = source[here, left + HD : left + 2 * HD]

    factor = math.log2(math.e) / math.sqrt(HD)

    def tile_body(tile, low, high):
        rows = slice(tile * tile_rows, (tile + 1) * tile_rows)
        k, v, b = keys[low:high, :], values[low:high, :], bias[rows, low:high]

        def score(step):
            heads = range(step * WIDE, (step + 1) * WIDE)
            q = jnp.concatenate([queries[rows, g * HD : (g + 1) * HD] for g in heads], axis=0)
            return lax.dot_general(
                q, k, (((1,), (1,)), ((), ())), preferred_element_type=jnp.float32
            )

        ahead = score(0)
        for step in range(G // WIDE):
            scores = ahead.reshape(WIDE, tile_rows, high - low) + b[None]
            if step + 1 < G // WIDE:
                ahead = score(step + 1)
            top = jnp.max(scores, axis=-1, keepdims=True)
            weights = jnp.exp2((scores - top) * factor)
            total = jnp.sum(weights, axis=-1, keepdims=True)
            summed = jnp.dot(
                weights.astype(jnp.bfloat16).reshape(WIDE * tile_rows, high - low),
                v,
                preferred_element_type=jnp.float32,
            ).reshape(WIDE, tile_rows, HD)
            result = (summed * (1.0 / total)).astype(jnp.bfloat16)
            for i in range(WIDE):
                g = step * WIDE + i
                out[rows, g * HD : (g + 1) * HD] = result[i]

    for tile in range(2):
        for need, low, high in ((1, 0, length), (2, length, 2 * length), (3, 0, 2 * length)):

            @pl.when(needs[tile] == need)
            def _():
                tile_body(tile, low, high)


def swap(array, axis):
    return lax.ppermute(array, axis, [(0, 1), (1, 0)])


def on_device(
    sizes, hidden, queries, norm_gain, key_gain, k_weight, v_weight, segment, position
):
    chips_z, groups = sizes[0], sizes[3]
    count, width = hidden.shape[1:]
    own_rows = k_weight.shape[0]
    rows = 2 * own_rows
    chunks = 2 * chips_z
    m = 2 * groups
    z, y = lax.axis_index("z"), lax.axis_index("y")
    core, x = lax.axis_index("core"), lax.axis_index("x")
    bf16 = jnp.bfloat16
    whole = pl.BlockSpec(memory_space=pltpu.VMEM)
    params = pltpu.CompilerParams(vmem_limit_bytes=VMEM_LIMIT)

    def along_ctx(array, d, cross=False):
        pairs = []
        for c in range(2):
            for i in range(m):
                pairs.append((c * m + i, (c ^ int(cross)) * m + (i + d) % m))
        return lax.ppermute(array, ("core", "ctx", "x"), pairs)

    def columns(which):
        at = which * 2 * HD
        return jnp.stack(
            [lax.dynamic_slice_in_dim(w, at, 2 * HD, 1) for w in (k_weight, v_weight)]
        )

    taken = swap(columns(1 - core), "core")
    kept = columns(core)
    chip = lax.dynamic_update_slice(
        jnp.zeros((2, rows, 2 * HD), bf16), kept, (0, core * own_rows, 0)
    )
    chip = lax.dynamic_update_slice(chip, taken, (0, (1 - core) * own_rows, 0))
    hidden, segment, position, chip = lax.optimization_barrier((hidden, segment, position, chip))
    normed = pl.pallas_call(
        functools.partial(norm_kernel, chunks),
        out_shape=jax.ShapeDtypeStruct((chunks, count, rows), bf16),
        in_specs=[pl.BlockSpec(memory_space=pltpu.HBM), whole],
        out_specs=whole,
        scratch_shapes=[
            pltpu.VMEM((count, width), bf16),
            pltpu.SemaphoreType.DMA((count // NORM_ROWS,)),
        ],
        compiler_params=params,
        cost_estimate=pl.CostEstimate(
            flops=4 * count * width, bytes_accessed=4 * count * width, transcendentals=0
        ),
        name="norm",
    )(hidden[0], norm_gain[None])
    ints = jnp.concatenate([segment, position])
    ints_all = [ints] + [along_ctx(ints, d) for d in range(1, m)]
    ints_other = swap(ints, "core")

    def along_z(array, k):
        return lax.ppermute(array, "z", [(i, i ^ k) for i in range(chips_z)])

    tie = lax.optimization_barrier
    mine = {0: lax.dynamic_index_in_dim(chip, x, 0, keepdims=False)}
    across, beside, corner = {}, {}, {}
    chip_beside = swap(chip, "y")
    for k in range(1, chips_z):
        low = k & -k
        if k == 2:
            mine[0], normed = tie((mine[0], normed))
        mine[k] = along_z(mine[k - low], low)
        if k == 2:
            tied = (mine[k], across[1], beside[1], chip_beside, normed, ints_all, ints_other)
            tied = tie(tied)
            mine[k], across[1], beside[1], chip_beside, normed, ints_all, ints_other = tied
            normed_other = swap(normed, "core")
        elif k == 3:
            mine[k], beside[2], normed_other = tie((mine[k], beside[2], normed_other))
        elif k > 3:
            mine[k], beside[k - 1] = tie((mine[k], beside[k - 1]))
        across[k], beside[k] = swap(mine[k], "x"), swap(mine[k], "y")
    end = chips_z - 1
    for k in range(1, chips_z):
        corner[k] = swap(across[k], "y") if k == end else swap(beside[k], "x")

    where = jnp.concatenate([position[0], ints_other[1]]).astype(jnp.float32)
    half = HD // 2
    freq = np.exp(np.arange(half, dtype=np.float32) * np.float32(-2.0 * math.log(THETA) / HD))
    angle = where[:, None] * freq[None, :]
    cosine, sine = jnp.cos(angle), jnp.sin(angle)
    cosine = jnp.concatenate([cosine, cosine], axis=1)
    sine = jnp.concatenate([-sine, sine], axis=1)
    bias, needs = pl.pallas_call(
        mask_kernel,
        out_shape=[
            jax.ShapeDtypeStruct((count, m * count), jnp.float32),
            jax.ShapeDtypeStruct((2,), jnp.int32),
        ],
        in_specs=[whole] * m,
        out_specs=[whole, pl.BlockSpec(memory_space=pltpu.SMEM)],
        compiler_params=params,
        name="mask",
    )(*ints_all)

    place = jnp.stack([z, y, x]).astype(jnp.int32)
    acc_shape = jax.ShapeDtypeStruct((2, 2 * count, 2 * HD), jnp.float32)
    kv_shape = jax.ShapeDtypeStruct((count, 4 * HD), bf16)
    final = [(end - 1, False)]
    late = [(end, True)] + [(k, False) for k in range(1, chips_z) if k != end - 1]
    early = [(0, True), (0, False)] + [(k, True) for k in range(1, end)]
    acc = []
    for groups in (early, late, final):
        first, last = groups is early, groups is final
        arrays = []
        for k, near in groups:
            if k == 0:
                arrays.append(chip if near else chip_beside)
            else:
                arrays += [mine[k], across[k]] if near else [beside[k], corner[k]]
        anywhere = pl.BlockSpec(memory_space=pl.ANY)
        outs = pl.pallas_call(
            functools.partial(project_kernel, groups, first, last, count),
            out_shape=[kv_shape] * 2 if last else [acc_shape],
            in_specs=[pl.BlockSpec(memory_space=pltpu.SMEM)]
            + [anywhere] * (2 + len(arrays))
            + [whole] * (len(acc) + (3 if last else 0)),
            out_specs=[whole] * (2 if last else 1),
            scratch_shapes=[
                pltpu.VMEM((len(groups), 2, rows, 2 * HD), bf16),
                pltpu.VMEM((len(groups), 2 * count, rows), bf16),
                pltpu.SemaphoreType.DMA((len(groups), 4)),
            ],
            compiler_params=params,
            cost_estimate=pl.CostEstimate(
                flops=2 * 2 * count * rows * 4 * HD * len(groups),
                bytes_accessed=2 * rows * (4 * HD + 2 * count) * len(groups),
                transcendentals=0,
            ),
            name="project",
        )(
            place, normed, normed_other, *arrays, *acc,
            *((cosine, sine, key_gain[None]) if last else ()),
        )
        acc = [outs[-1]]

    kv_own, kv_other = outs
    result = None
    for cross, kv in enumerate((kv_own, kv_other)):
        sources = [kv if d == 0 and not cross else along_ctx(kv, d, cross) for d in range(m)]

        def block(step, place, needs, cross=cross):
            return (0, lax.rem(place[0] + cross, 2) * 2 + step)

        earlier = [] if result is None else [result]
        result = pl.pallas_call(
            functools.partial(attend_kernel, m, count),
            out_shape=jax.ShapeDtypeStruct((count, KVH * G * HD), bf16),
            grid_spec=pltpu.PrefetchScalarGridSpec(
                num_scalar_prefetch=2,
                grid=(2,),
                in_specs=[pl.BlockSpec((count, G * HD), block)]
                + [whole] * (1 + m)
                + [pl.BlockSpec(memory_space=pl.ANY)] * len(earlier),
                out_specs=pl.BlockSpec((count, G * HD), block),
                scratch_shapes=[
                    pltpu.VMEM((m * count, HD), bf16),
                    pltpu.VMEM((m * count, HD), bf16),
                ],
            ),
            input_output_aliases={4 + m: 0} if earlier else {},
            compiler_params=params,
            cost_estimate=pl.CostEstimate(
                flops=2 * count * m * count * KVH * G * HD,
                bytes_accessed=2 * count * KVH * G * HD,
                transcendentals=count * m * count * KVH * G // 2,
            ),
            name="attend",
        )(core.astype(jnp.int32)[None], needs, queries[0], bias, *sources, *earlier)
    return result[None]


def solution(mesh):
    n, m = mesh.shape["fsdp"], mesh.shape["ctx"]
    sizes = (n // 4, 2, 2, m // 2, 2)
    fine = Mesh(mesh.devices.reshape(sizes), ("z", "y", "core", "ctx", "x"))
    fsdp, ctx = ("z", "y", "core"), ("ctx", "x")
    placed = (
        P(fsdp, ctx, None),
        P(fsdp, ctx, None),
        P(),
        P(),
        P(fsdp, None),
        P(fsdp, None),
        P(fsdp, ctx),
        P(fsdp, ctx),
    )
    return jax.shard_map(
        functools.partial(on_device, sizes),
        mesh=fine,
        in_specs=placed,
        out_specs=P(fsdp, ctx, None),
        check_vma=False,
    )
```

```python
import functools
import math

import jax
import jax.numpy as jnp
import numpy as np
from jax import lax
from jax.experimental import pallas as pl
from jax.experimental.pallas import tpu as pltpu
from jax.sharding import Mesh
from jax.sharding import PartitionSpec as P

KVH = 4
HD = 128
G = 8
EPS = 1e-06
THETA = 1000000.0
MASKED = -1e30
VMEM_LIMIT = 24 * 2**20
NORM_ROWS = 64
WIDE = 4


def norm_kernel(chunks, hidden, gain, out, held, sems):
    steps = held.shape[0] // NORM_ROWS
    copies = []
    for i in range(steps):
        at = pl.ds(i * NORM_ROWS, NORM_ROWS)
        copies.append(pltpu.make_async_copy(hidden.at[at], held.at[at], sems.at[i]))
        copies[-1].start()
    for i, copy in enumerate(copies):
        copy.wait()
        at = pl.ds(i * NORM_ROWS, NORM_ROWS)
        inputs = held[at, :].astype(jnp.float32)
        scale = lax.rsqrt(jnp.mean(inputs * inputs, axis=-1, keepdims=True) + EPS)
        normed = (inputs * scale * gain[...]).astype(jnp.bfloat16)
        rows = normed.shape[1] // chunks
        for j in range(chunks):
            out[j, at, :] = normed[:, j * rows : (j + 1) * rows]


def project_kernel(groups, first, last, count, place, own, other, *rest):
    chips_z = own.shape[0] // 2
    y, x, spot = place[0], place[1], place[2]
    rest = list(rest)
    weight, lhs, sems = rest[-3:]
    waits = []
    for g, (k, near) in enumerate(groups):
        i = lax.rem(spot - k + chips_z, chips_z)
        chunk = (i ^ (i >> 1)) * 2 + (y if near else 1 - y)
        pairs = [
            (own.at[chunk], lhs.at[g, pl.ds(0, count)]),
            (other.at[chunk], lhs.at[g, pl.ds(count, count)]),
        ]
        if k == 0:
            both = rest.pop(0)
            pairs += [(both.at[h], weight.at[g, :, pl.ds(h * HD, HD)]) for h in range(2)]
        else:
            for h in (x, 1 - x):
                at = pl.ds(pl.multiple_of(h * HD, HD), HD)
                pairs.append((rest.pop(0), weight.at[g, :, at]))
        copies = [
            pltpu.make_async_copy(source, target, sems.at[g, i])
            for i, (source, target) in enumerate(pairs)
        ]
        for copy in copies:
            copy.start()
        waits.append(copies)
    total = None if first else rest.pop(0)[...]
    for g, copies in enumerate(waits):
        for copy in copies:
            copy.wait()
        part = jnp.dot(lhs[g], weight[g], preferred_element_type=jnp.float32)
        total = part if total is None else total + part
    if not last:
        rest[0][...] = total
        return
    cosine, sine, gain = rest[:3]
    for part, out in enumerate(rest[3:5]):
        at = slice(part * count, (part + 1) * count)
        raw = total[at, :HD]
        normk = raw * lax.rsqrt(jnp.mean(raw * raw, axis=-1, keepdims=True) + EPS) * gain[...]
        turned = normk * cosine[at, :] + pltpu.roll(normk, HD // 2, 1) * sine[at, :]
        out[:, :HD] = turned.astype(jnp.bfloat16)
        out[:, HD:] = total[at, HD:].astype(jnp.bfloat16)


def mask_kernel(*refs):
    pieces, (bias, needs) = refs[:-2], refs[-2:]
    count = bias.shape[0]
    half_rows = count // 2
    seg_q, pos_q = (
        jnp.transpose(jnp.broadcast_to(pieces[0][i : i + 1, :], (half_rows, count)))
        for i in range(2)
    )
    half_width = len(pieces) * half_rows
    for half in range(2):
        for i, piece in enumerate(pieces):
            at = slice(half * half_rows, (half + 1) * half_rows)
            allowed = (piece[:1, at] == seg_q) & (piece[1:, at] <= pos_q)
            there = half * half_width + i * half_rows
            bias[:, there : there + half_rows] = jnp.where(allowed, 0.0, MASKED)
    for tile in range(2):
        rows = slice(tile * half_rows, (tile + 1) * half_rows)
        found = [
            jnp.max(bias[rows, half * half_width : (half + 1) * half_width]) == 0.0
            for half in range(2)
        ]
        needs[tile] = found[0].astype(jnp.int32) + 2 * found[1].astype(jnp.int32)


def attend_kernel(pieces, count, place, needs, queries, bias, *rest):
    sources, (out, keys, values) = rest[: 2 * pieces], rest[-3:]
    step = pl.program_id(0)
    tile_rows = count // 2
    length = pieces * tile_rows

    for head in range(2):

        @pl.when(step == head)
        def _():
            for i in range(pieces):
                source = sources[head * pieces + i]
                for half in range(2):
                    here = slice(half * tile_rows, (half + 1) * tile_rows)
                    there = half * length + i * tile_rows
                    keys[there : there + tile_rows, :] = source[here, :HD]
                    values[there : there + tile_rows, :] = source[here, HD:]

    factor = math.log2(math.e) / math.sqrt(HD)

    def tile_body(tile, low, high):
        rows = slice(tile * tile_rows, (tile + 1) * tile_rows)
        k, v, b = keys[low:high, :], values[low:high, :], bias[rows, low:high]

        def score(step):
            heads = range(step * WIDE, (step + 1) * WIDE)
            q = jnp.concatenate([queries[rows, g * HD : (g + 1) * HD] for g in heads], axis=0)
            return lax.dot_general(
                q, k, (((1,), (1,)), ((), ())), preferred_element_type=jnp.float32
            )

        ahead = score(0)
        for step in range(G // WIDE):
            scores = ahead.reshape(WIDE, tile_rows, high - low) + b[None]
            if step + 1 < G // WIDE:
                ahead = score(step + 1)
            top = jnp.max(scores, axis=-1, keepdims=True)
            weights = jnp.exp2((scores - top) * factor)
            total = jnp.sum(weights, axis=-1, keepdims=True)
            summed = jnp.dot(
                weights.astype(jnp.bfloat16).reshape(WIDE * tile_rows, high - low),
                v,
                preferred_element_type=jnp.float32,
            ).reshape(WIDE, tile_rows, HD)
            result = (summed * (1.0 / total)).astype(jnp.bfloat16)
            for i in range(WIDE):
                g = step * WIDE + i
                out[rows, g * HD : (g + 1) * HD] = result[i]

    for tile in range(2):
        for need, low, high in ((1, 0, length), (2, length, 2 * length), (3, 0, 2 * length)):

            @pl.when(needs[tile] == need)
            def _():
                tile_body(tile, low, high)


def swap(array, axis):
    return lax.ppermute(array, axis, [(0, 1), (1, 0)])


def on_device(
    sizes, hidden, queries, norm_gain, key_gain, k_weight, v_weight, segment, position
):
    chips_z, groups = sizes[0], sizes[3]
    count, width = hidden.shape[1:]
    own_rows = k_weight.shape[0]
    rows = 2 * own_rows
    chunks = 2 * chips_z
    m = 2 * groups
    z, y = lax.axis_index("z"), lax.axis_index("y")
    core, x = lax.axis_index("core"), lax.axis_index("x")
    bf16 = jnp.bfloat16
    whole = pl.BlockSpec(memory_space=pltpu.VMEM)
    params = pltpu.CompilerParams(vmem_limit_bytes=VMEM_LIMIT)

    def along_ctx(array, d, cross=False):
        pairs = []
        for c in range(2):
            for i in range(m):
                pairs.append((c * m + i, (c ^ int(cross)) * m + (i + d) % m))
        return lax.ppermute(array, ("core", "ctx", "x"), pairs)

    def columns(which):
        at = which * 2 * HD
        return jnp.stack(
            [lax.dynamic_slice_in_dim(w, at, 2 * HD, 1) for w in (k_weight, v_weight)]
        )

    taken = swap(columns(1 - core), "core")
    kept = columns(core)
    chip = lax.dynamic_update_slice(
        jnp.zeros((2, rows, 2 * HD), bf16), kept, (0, core * own_rows, 0)
    )
    chip = lax.dynamic_update_slice(chip, taken, (0, (1 - core) * own_rows, 0))
    hidden, segment, position, chip = lax.optimization_barrier((hidden, segment, position, chip))
    normed = pl.pallas_call(
        functools.partial(norm_kernel, chunks),
        out_shape=jax.ShapeDtypeStruct((chunks, count, rows), bf16),
        in_specs=[pl.BlockSpec(memory_space=pltpu.HBM), whole],
        out_specs=whole,
        scratch_shapes=[
            pltpu.VMEM((count, width), bf16),
            pltpu.SemaphoreType.DMA((count // NORM_ROWS,)),
        ],
        compiler_params=params,
        cost_estimate=pl.CostEstimate(
            flops=4 * count * width, bytes_accessed=4 * count * width, transcendentals=0
        ),
        name="norm",
    )(hidden[0], norm_gain[None])
    ints = jnp.concatenate([segment, position])
    ints_all = [ints] + [along_ctx(ints, d) for d in range(1, m)]
    ints_other = swap(ints, "core")

    order = [i ^ (i >> 1) for i in range(chips_z)]
    ring = [(order[i], order[(i + 1) % chips_z]) for i in range(chips_z)]
    tie = lax.optimization_barrier
    end = chips_z - 1
    streams = []
    for s in range(2):
        both = chip[:, :, s * HD : (s + 1) * HD]
        streams.append(dict(both=both, mine={}, across={}, beside={}, corner={}))
    for k in range(1, chips_z):
        for s, stream in enumerate(streams):
            mine, across, beside = stream["mine"], stream["across"], stream["beside"]
            if k == 1:
                if s == 1:
                    tied = (stream["both"], streams[0]["mine"][1])
                    stream["both"], streams[0]["mine"][1] = tie(tied)
                mine[0] = lax.dynamic_index_in_dim(stream["both"], x, 0, keepdims=False)
                stream["far"] = swap(stream["both"], "y")
            mine[k] = lax.ppermute(mine[k - 1], "z", ring)
            if k == 2:
                mine[k], across[1], stream["far"], first = tie(
                    (mine[k], across[1], stream["far"], streams[1]["mine"][1])
                )
                if s == 0:
                    tied = (mine[k], first, normed, ints_all, ints_other)
                    mine[k], first, normed, ints_all, ints_other = tie(tied)
                    normed_other = swap(normed, "core")
                    streams[1]["mine"][1] = first
            elif k > 2:
                tied = (mine[k], across[k - 1], beside[k - 1], beside[k - 2])
                mine[k], across[k - 1], beside[k - 1], beside[k - 2] = tie(tied)
            across[k], beside[k] = swap(mine[k], "x"), swap(mine[k], "y")
    for stream in streams:
        for k in range(1, chips_z):
            stream["corner"][k] = (
                swap(stream["beside"][k], "x") if k % 2 else swap(stream["across"][k], "y")
            )

    where = jnp.concatenate([position[0], ints_other[1]]).astype(jnp.float32)
    half = HD // 2
    freq = np.exp(np.arange(half, dtype=np.float32) * np.float32(-2.0 * math.log(THETA) / HD))
    angle = where[:, None] * freq[None, :]
    cosine, sine = jnp.cos(angle), jnp.sin(angle)
    cosine = jnp.concatenate([cosine, cosine], axis=1)
    sine = jnp.concatenate([-sine, sine], axis=1)
    bias, needs = pl.pallas_call(
        mask_kernel,
        out_shape=[
            jax.ShapeDtypeStruct((count, m * count), jnp.float32),
            jax.ShapeDtypeStruct((2,), jnp.int32),
        ],
        in_specs=[whole] * m,
        out_specs=[whole, pl.BlockSpec(memory_space=pltpu.SMEM)],
        compiler_params=params,
        name="mask",
    )(*ints_all)

    spot = sum(jnp.where(z == order[i], i, 0) for i in range(chips_z))
    place = jnp.stack([y, x, spot]).astype(jnp.int32)
    acc_shape = jax.ShapeDtypeStruct((2 * count, 2 * HD), jnp.float32)
    kv_shape = jax.ShapeDtypeStruct((count, 2 * HD), bf16)
    final = [(end, False)]
    late = [(end, True)] + [(k, False) for k in range(1, end)]
    early = [(0, True), (0, False)] + [(k, True) for k in range(1, end)]
    in_hbm = pl.BlockSpec(memory_space=pltpu.HBM)
    result = None
    for s, stream in enumerate(streams):
        acc = []
        for groups in (early, late, final):
            first, last = groups is early, groups is final
            arrays = []
            for k, near in groups:
                if k == 0:
                    arrays.append(stream["both" if near else "far"])
                else:
                    kinds = ("mine", "across") if near else ("beside", "corner")
                    arrays += [stream[kind][k] for kind in kinds]
            outs = pl.pallas_call(
                functools.partial(project_kernel, groups, first, last, count),
                out_shape=[kv_shape] * 2 if last else [acc_shape],
                in_specs=[pl.BlockSpec(memory_space=pltpu.SMEM)]
                + [in_hbm] * (2 + len(arrays))
                + [whole] * (len(acc) + (3 if last else 0)),
                out_specs=[whole] * (2 if last else 1),
                scratch_shapes=[
                    pltpu.VMEM((len(groups), rows, 2 * HD), bf16),
                    pltpu.VMEM((len(groups), 2 * count, rows), bf16),
                    pltpu.SemaphoreType.DMA((len(groups), 4)),
                ],
                compiler_params=params,
                cost_estimate=pl.CostEstimate(
                    flops=2 * 2 * count * rows * 2 * HD * len(groups),
                    bytes_accessed=2 * rows * (2 * HD + 2 * count) * len(groups),
                    transcendentals=0,
                ),
                name="project",
            )(
                place, normed, normed_other, *arrays, *acc,
                *((cosine, sine, key_gain[None]) if last else ()),
            )
            acc = [outs[-1]]

        kv_own, kv_other = outs
        sources = [kv_own] + [along_ctx(kv_own, d) for d in range(1, m)]
        sources += [along_ctx(kv_other, d, True) for d in range(m)]

        def block(step, place, needs, s=s):
            return (0, lax.rem(place[0] + step, 2) * 2 + s)

        earlier = [] if result is None else [result]
        result = pl.pallas_call(
            functools.partial(attend_kernel, m, count),
            out_shape=jax.ShapeDtypeStruct((count, KVH * G * HD), bf16),
            grid_spec=pltpu.PrefetchScalarGridSpec(
                num_scalar_prefetch=2,
                grid=(2,),
                in_specs=[pl.BlockSpec((count, G * HD), block)]
                + [whole] * (1 + 2 * m)
                + [pl.BlockSpec(memory_space=pl.ANY)] * len(earlier),
                out_specs=pl.BlockSpec((count, G * HD), block),
                scratch_shapes=[
                    pltpu.VMEM((m * count, HD), bf16),
                    pltpu.VMEM((m * count, HD), bf16),
                ],
            ),
            input_output_aliases={4 + 2 * m: 0} if earlier else {},
            compiler_params=params,
            cost_estimate=pl.CostEstimate(
                flops=2 * count * m * count * KVH * G * HD,
                bytes_accessed=2 * count * KVH * G * HD,
                transcendentals=count * m * count * KVH * G // 2,
            ),
            name="attend",
        )(core.astype(jnp.int32)[None], needs, queries[0], bias, *sources, *earlier)
    return result[None]


def solution(mesh):
    n, m = mesh.shape["fsdp"], mesh.shape["ctx"]
    sizes = (n // 4, 2, 2, m // 2, 2)
    fine = Mesh(mesh.devices.reshape(sizes), ("z", "y", "core", "ctx", "x"))
    fsdp, ctx = ("z", "y", "core"), ("ctx", "x")
    placed = (
        P(fsdp, ctx, None),
        P(fsdp, ctx, None),
        P(),
        P(),
        P(fsdp, None),
        P(fsdp, None),
        P(fsdp, ctx),
        P(fsdp, ctx),
    )
    return jax.shard_map(
        functools.partial(on_device, sizes),
        mesh=fine,
        in_specs=placed,
        out_specs=P(fsdp, ctx, None),
        check_vma=False,
    )
```

```python
import functools
import math

import jax
import jax.numpy as jnp
import numpy as np
from jax import lax
from jax.experimental import pallas as pl
from jax.experimental.pallas import tpu as pltpu
from jax.sharding import Mesh
from jax.sharding import PartitionSpec as P

KVH = 4
HD = 128
G = 8
EPS = 1e-06
THETA = 1000000.0
MASKED = -1e30
VMEM_LIMIT = 24 * 2**20
NORM_ROWS = 64
WIDE = 4
TILES = 4
SLOW = 2
MASK_COST = 30*10**9


def norm_kernel(chunks, hidden, gain, out, held, sems):
    steps = held.shape[0] // NORM_ROWS
    copies = []
    for i in range(steps):
        at = pl.ds(i * NORM_ROWS, NORM_ROWS)
        copies.append(pltpu.make_async_copy(hidden.at[at], held.at[at], sems.at[i]))
        copies[-1].start()
    for i, copy in enumerate(copies):
        copy.wait()
        at = pl.ds(i * NORM_ROWS, NORM_ROWS)
        inputs = held[at, :].astype(jnp.float32)
        scale = lax.rsqrt(jnp.mean(inputs * inputs, axis=-1, keepdims=True) + EPS)
        normed = (inputs * scale * gain[...]).astype(jnp.bfloat16)
        rows = normed.shape[1] // chunks
        for j in range(chunks):
            out[j, at, :] = normed[:, j * rows : (j + 1) * rows]


def project_kernel(groups, alone, first, last, count, place, own, other, *rest):
    chips_z = own.shape[0] // 2
    y, x, spot = place[0], place[1], place[2]
    rest = list(rest) if alone else list(rest[1:])
    weight, lhs, sems = rest[-3:]
    waits = []
    for g, (k, near) in enumerate(groups):
        i = lax.rem(spot - k + chips_z, chips_z)
        chunk = (i ^ (i >> 1)) * 2 + (y if near else 1 - y)
        pairs = [
            (own.at[chunk], lhs.at[g, pl.ds(0, count)]),
            (other.at[chunk], lhs.at[g, pl.ds(count, count)]),
        ]
        if k == 0:
            pairs.append((rest.pop(0), weight.at[g]))
        else:
            pairs.append((rest.pop(0), weight.at[g, x]))
            pairs.append((rest.pop(0), weight.at[g, 1 - x]))
        copies = [
            pltpu.make_async_copy(source, target, sems.at[g, i])
            for i, (source, target) in enumerate(pairs)
        ]
        for copy in copies:
            copy.start()
        waits.append(copies)
    earlier = None if first else rest.pop(0)
    terms = [None, None]
    for g, copies in enumerate(waits):
        for copy in copies:
            copy.wait()
        for half in range(2):
            part = jnp.dot(lhs[g], weight[g, half], preferred_element_type=jnp.float32)
            terms[half] = part if terms[half] is None else terms[half] + part
    for half in range(2):
        if not first:
            terms[half] += earlier[half]
        if not last:
            rest[0][half] = terms[half]
    if not last:
        return
    cosine, sine, gain = rest[:3]
    outs = rest[3:5]
    for head in range(2):
        columns = slice(head * HD, (head + 1) * HD)
        for part, out in enumerate(outs):
            at = slice(part * count, (part + 1) * count)
            raw = terms[0][at, columns]
            normk = raw * lax.rsqrt(jnp.mean(raw * raw, axis=-1, keepdims=True) + EPS) * gain[...]
            turned = normk * cosine[at, :] + pltpu.roll(normk, HD // 2, 1) * sine[at, :]
            out[:, 2 * head * HD : (2 * head + 1) * HD] = turned.astype(jnp.bfloat16)
            out[:, (2 * head + 1) * HD : (2 * head + 2) * HD] = terms[1][at, columns].astype(
                jnp.bfloat16
            )


def mask_kernel(*refs):
    pieces, (bias, needs) = refs[1:-2], refs[-2:]
    count = bias.shape[0]
    size = count // TILES
    seg_q, pos_q = (
        jnp.transpose(jnp.broadcast_to(pieces[0][i : i + 1, :], (count, count))) for i in range(2)
    )
    width = len(pieces) * size
    for tile in range(TILES):
        for i, piece in enumerate(pieces):
            at = slice(tile * size, (tile + 1) * size)
            allowed = (piece[:1, at] == seg_q[:, at]) & (piece[1:, at] <= pos_q[:, at])
            there = tile * width + i * size
            bias[:, there : there + size] = jnp.where(allowed, 0.0, MASKED)
    for tile in range(TILES - 1):
        rows = slice(tile * size, (tile + 1) * size)
        needs[tile] = (jnp.max(bias[rows, (tile + 1) * width :]) == 0.0).astype(jnp.int32)
    needs[TILES - 1] = 0


def attend_kernel(pieces, count, place, needs, queries, bias, *rest):
    sources, (out, keys, values) = rest[:pieces], rest[-3:]
    step = pl.program_id(0)
    tile_rows = count // TILES
    length = pieces * tile_rows

    for head in range(2):

        @pl.when(step == head)
        def _():
            left = 2 * head * HD
            for i, source in enumerate(sources):
                for tile in range(TILES):
                    here = slice(tile * tile_rows, (tile + 1) * tile_rows)
                    there = tile * length + i * tile_rows
                    keys[there : there + tile_rows, :] = source[here, left : left + HD]
                    values[there : there + tile_rows, :] = source[here, left + HD : left + 2 * HD]

    factor = math.log2(math.e) / math.sqrt(HD)

    def tile_body(tile, high):
        rows = slice(tile * tile_rows, (tile + 1) * tile_rows)
        k, v, b = keys[:high, :], values[:high, :], bias[rows, :high]

        def score(step):
            heads = range(step * WIDE, (step + 1) * WIDE)
            q = jnp.concatenate([queries[rows, g * HD : (g + 1) * HD] for g in heads], axis=0)
            return lax.dot_general(
                q, k, (((1,), (1,)), ((), ())), preferred_element_type=jnp.float32
            )

        ahead = score(0)
        for step in range(G // WIDE):
            scores = ahead.reshape(WIDE, tile_rows, high) + b[None]
            if step + 1 < G // WIDE:
                ahead = score(step + 1)
            top = jnp.max(scores, axis=-1, keepdims=True)
            weights = jnp.exp2((scores - top) * factor)
            total = jnp.sum(weights, axis=-1, keepdims=True)
            summed = jnp.dot(
                weights.astype(jnp.bfloat16).reshape(WIDE * tile_rows, high),
                v,
                preferred_element_type=jnp.float32,
            ).reshape(WIDE, tile_rows, HD)
            result = (summed * (1.0 / total)).astype(jnp.bfloat16)
            for i in range(WIDE):
                g = step * WIDE + i
                out[rows, g * HD : (g + 1) * HD] = result[i]

    for tile in range(TILES):
        for need, high in ((0, tile + 1), (1, TILES)):

            @pl.when(needs[tile] == need)
            def _():
                tile_body(tile, high * length)


def swap(array, axis):
    return lax.ppermute(array, axis, [(0, 1), (1, 0)])


def on_device(
    sizes, hidden, queries, norm_gain, key_gain, k_weight, v_weight, segment, position
):
    chips_z, groups = sizes[0], sizes[3]
    count, width = hidden.shape[1:]
    own_rows = k_weight.shape[0]
    rows = 2 * own_rows
    chunks = 2 * chips_z
    m = 2 * groups
    z, y = lax.axis_index("z"), lax.axis_index("y")
    core, x = lax.axis_index("core"), lax.axis_index("x")
    bf16 = jnp.bfloat16
    whole = pl.BlockSpec(memory_space=pltpu.VMEM)
    params = pltpu.CompilerParams(vmem_limit_bytes=VMEM_LIMIT)

    def along_ctx(array, d, cross=False):
        pairs = []
        for c in range(2):
            for i in range(m):
                pairs.append((c * m + i, (c ^ int(cross)) * m + (i + d) % m))
        return lax.ppermute(array, ("core", "ctx", "x"), pairs)

    def columns(which):
        at = which * 2 * HD
        return jnp.stack(
            [lax.dynamic_slice_in_dim(w, at, 2 * HD, 1) for w in (k_weight, v_weight)]
        )

    taken = swap(columns(1 - core), "core")
    kept = columns(core)
    chip = lax.dynamic_update_slice(
        jnp.zeros((2, rows, 2 * HD), bf16), kept, (0, core * own_rows, 0)
    )
    chip = lax.dynamic_update_slice(chip, taken, (0, (1 - core) * own_rows, 0))
    hidden, segment, position, chip = lax.optimization_barrier((hidden, segment, position, chip))
    normed = pl.pallas_call(
        functools.partial(norm_kernel, chunks),
        out_shape=jax.ShapeDtypeStruct((chunks, count, rows), bf16),
        in_specs=[pl.BlockSpec(memory_space=pltpu.HBM), whole],
        out_specs=whole,
        scratch_shapes=[
            pltpu.VMEM((count, width), bf16),
            pltpu.SemaphoreType.DMA((count // NORM_ROWS,)),
        ],
        compiler_params=params,
        cost_estimate=pl.CostEstimate(
            flops=4 * count * width, bytes_accessed=4 * count * width, transcendentals=0
        ),
        name="norm",
    )(hidden[0], norm_gain[None])
    ints = jnp.concatenate([segment, position])
    ints_all = [ints] + [along_ctx(ints, d) for d in range(1, m)]
    ints_other = swap(ints, "core")

    acc_shape = jax.ShapeDtypeStruct((2, 2 * count, 2 * HD), jnp.float32)
    kv_shape = jax.ShapeDtypeStruct((count, 4 * HD), bf16)

    def project(groups, acc=None, last=False, also=None):
        arrays = [] if also is None else [also]
        for k, near in groups:
            if k == 0:
                arrays.append(chip if near else chip_beside)
            else:
                arrays += [mine[k], across[k]] if near else [beside[k], corner[k]]
        accs = [] if acc is None else [acc]
        outs = pl.pallas_call(
            functools.partial(project_kernel, groups, also is None, acc is None, last, count),
            out_shape=[kv_shape] * 2 if last else [acc_shape],
            in_specs=[pl.BlockSpec(memory_space=pltpu.SMEM)]
            + [pl.BlockSpec(memory_space=pltpu.HBM)] * (2 + len(arrays))
            + [whole] * (len(accs) + (3 if last else 0)),
            out_specs=[whole] * (2 if last else 1),
            scratch_shapes=[
                pltpu.VMEM((len(groups), 2, rows, 2 * HD), bf16),
                pltpu.VMEM((len(groups), 2 * count, rows), bf16),
                pltpu.SemaphoreType.DMA((len(groups), 4)),
            ],
            compiler_params=params,
            cost_estimate=pl.CostEstimate(
                flops=SLOW * 2 * 2 * count * rows * 4 * HD * len(groups),
                bytes_accessed=SLOW * 2 * rows * (4 * HD + 2 * count) * len(groups),
                transcendentals=0,
            ),
            name="project",
        )(
            place, normed, normed_other, *arrays, *accs,
            *((cosine, sine, key_gain[None]) if last else ()),
        )
        return outs if last else outs[0]

    order = [i ^ (i >> 1) for i in range(chips_z)]
    ring = [(order[i], order[(i + 1) % chips_z]) for i in range(chips_z)]
    spot = sum(jnp.where(z == order[i], i, 0) for i in range(chips_z))
    place = jnp.stack([y, x, spot]).astype(jnp.int32)
    tie = lax.optimization_barrier
    end = chips_z - 1
    mine = {0: lax.dynamic_index_in_dim(chip, x, 0, keepdims=False)}
    across, beside, corner = {}, {}, {}
    chip_beside = swap(chip, "y")
    acc = None
    for k in range(1, chips_z):
        mine[k] = lax.ppermute(mine[k - 1], "z", ring)
        if k == 1:
            tied = tie((mine[k], normed, ints_all, ints_other))
            mine[k], normed, ints_all, ints_other = tied
            normed_other = swap(normed, "core")
            bias, needs = pl.pallas_call(
                mask_kernel,
                out_shape=[
                    jax.ShapeDtypeStruct((count, m * count), jnp.float32),
                    jax.ShapeDtypeStruct((TILES,), jnp.int32),
                ],
                in_specs=[pl.BlockSpec(memory_space=pltpu.HBM)] + [whole] * m,
                out_specs=[whole, pl.BlockSpec(memory_space=pltpu.SMEM)],
                compiler_params=params,
                cost_estimate=pl.CostEstimate(
                    flops=MASK_COST, bytes_accessed=MASK_COST // 300, transcendentals=0
                ),
                name="mask",
            )(chip_beside, *ints_all)
        elif k > 2:
            if acc is None:
                acc = project([(0, True), (0, False)])
            acc = project([(k - 2, True)], acc, also=beside[k - 2])
            if k == 3:
                mine[k], acc, bias = tie((mine[k], acc, bias))
            else:
                mine[k], acc = tie((mine[k], acc))
        across[k], beside[k] = swap(mine[k], "x"), swap(mine[k], "y")
    for k in range(1, chips_z):
        if k < end:
            corner[k] = swap(beside[k], "x") if k % 2 else swap(across[k], "y")
    acc = project([(end - 1, True), (1, False)], acc, also=beside[end - 1])
    beside[end], acc = tie((beside[end], acc))
    corner[end] = swap(beside[end], "x")

    where = jnp.concatenate([position[0], ints_other[1]]).astype(jnp.float32)
    half = HD // 2
    freq = np.exp(np.arange(half, dtype=np.float32) * np.float32(-2.0 * math.log(THETA) / HD))
    angle = where[:, None] * freq[None, :]
    cosine, sine = jnp.cos(angle), jnp.sin(angle)
    cosine = jnp.concatenate([cosine, cosine], axis=1)
    sine = jnp.concatenate([-sine, sine], axis=1)

    acc = project([(end, True)] + [(k, False) for k in range(2, end)], acc)
    kv_own, kv_other = project([(end, False)], acc, last=True)

    result = None
    for cross, kv in enumerate((kv_own, kv_other)):
        sources = [kv if d == 0 and not cross else along_ctx(kv, d, cross) for d in range(m)]

        def block(step, place, needs, cross=cross):
            return (0, lax.rem(place[0] + cross, 2) * 2 + step)

        earlier = [] if result is None else [result]
        result = pl.pallas_call(
            functools.partial(attend_kernel, m, count),
            out_shape=jax.ShapeDtypeStruct((count, KVH * G * HD), bf16),
            grid_spec=pltpu.PrefetchScalarGridSpec(
                num_scalar_prefetch=2,
                grid=(2,),
                in_specs=[pl.BlockSpec((count, G * HD), block)]
                + [whole] * (1 + m)
                + [pl.BlockSpec(memory_space=pl.ANY)] * len(earlier),
                out_specs=pl.BlockSpec((count, G * HD), block),
                scratch_shapes=[
                    pltpu.VMEM((m * count, HD), bf16),
                    pltpu.VMEM((m * count, HD), bf16),
                ],
            ),
            input_output_aliases={4 + m: 0} if earlier else {},
            compiler_params=params,
            cost_estimate=pl.CostEstimate(
                flops=2 * count * m * count * KVH * G * HD,
                bytes_accessed=2 * count * KVH * G * HD,
                transcendentals=count * m * count * KVH * G // 2,
            ),
            name="attend",
        )(core.astype(jnp.int32)[None], needs, queries[0], bias, *sources, *earlier)
    return result[None]


def solution(mesh):
    n, m = mesh.shape["fsdp"], mesh.shape["ctx"]
    sizes = (n // 4, 2, 2, m // 2, 2)
    fine = Mesh(mesh.devices.reshape(sizes), ("z", "y", "core", "ctx", "x"))
    fsdp, ctx = ("z", "y", "core"), ("ctx", "x")
    placed = (
        P(fsdp, ctx, None),
        P(fsdp, ctx, None),
        P(),
        P(),
        P(fsdp, None),
        P(fsdp, None),
        P(fsdp, ctx),
        P(fsdp, ctx),
    )
    return jax.shard_map(
        functools.partial(on_device, sizes),
        mesh=fine,
        in_specs=placed,
        out_specs=P(fsdp, ctx, None),
        check_vma=False,
    )
```

```python
import functools
import math

import jax
import jax.numpy as jnp
import numpy as np
from jax import lax
from jax.experimental import pallas as pl
from jax.experimental.pallas import tpu as pltpu
from jax.sharding import Mesh
from jax.sharding import PartitionSpec as P

KVH = 4
HD = 128
G = 8
EPS = 1e-06
THETA = 1000000.0
MASKED = -1e30
VMEM_LIMIT = 24 * 2**20
NORM_ROWS = 64
WIDE = 4
TILES = 2
SLOW = 2
MASK_COST = 30 * 10**9


def norm_kernel(chunks, hidden, gain, out, held, sems):
    steps = held.shape[0] // NORM_ROWS
    copies = []
    for i in range(steps):
        at = pl.ds(i * NORM_ROWS, NORM_ROWS)
        copies.append(pltpu.make_async_copy(hidden.at[at], held.at[at], sems.at[i]))
        copies[-1].start()
    for i, copy in enumerate(copies):
        copy.wait()
        at = pl.ds(i * NORM_ROWS, NORM_ROWS)
        inputs = held[at, :].astype(jnp.float32)
        scale = lax.rsqrt(jnp.mean(inputs * inputs, axis=-1, keepdims=True) + EPS)
        normed = (inputs * scale * gain[...]).astype(jnp.bfloat16)
        rows = normed.shape[1] // chunks
        for j in range(chunks):
            out[j, at, :] = normed[:, j * rows : (j + 1) * rows]


def project_kernel(groups, alone, first, last, count, place, own, other, *rest):
    chips_z = own.shape[0] // 2
    y, x, spot = place[0], place[1], place[2]
    rest = list(rest) if alone else list(rest[1:])
    weight, lhs, sems = rest[-3:]
    waits = []
    for g, (k, near) in enumerate(groups):
        i = lax.rem(spot - k + chips_z, chips_z)
        chunk = (i ^ (i >> 1)) * 2 + (y if near else 1 - y)
        pairs = [
            (own.at[chunk], lhs.at[g, pl.ds(0, count)]),
            (other.at[chunk], lhs.at[g, pl.ds(count, count)]),
        ]
        if k == 0:
            pairs.append((rest.pop(0), weight.at[g]))
        else:
            pairs.append((rest.pop(0), weight.at[g, x]))
            pairs.append((rest.pop(0), weight.at[g, 1 - x]))
        copies = [
            pltpu.make_async_copy(source, target, sems.at[g, i])
            for i, (source, target) in enumerate(pairs)
        ]
        for copy in copies:
            copy.start()
        waits.append(copies)
    earlier = None if first else rest.pop(0)
    terms = [None, None]
    for g, copies in enumerate(waits):
        for copy in copies:
            copy.wait()
        for half in range(2):
            part = jnp.dot(lhs[g], weight[g, half], preferred_element_type=jnp.float32)
            terms[half] = part if terms[half] is None else terms[half] + part
    for half in range(2):
        if not first:
            terms[half] += earlier[half]
        if not last:
            rest[0][half] = terms[half]
    if not last:
        return
    cosine, sine, gain = rest[:3]
    outs = rest[3:5]
    for head in range(2):
        columns = slice(head * HD, (head + 1) * HD)
        for part, out in enumerate(outs):
            at = slice(part * count, (part + 1) * count)
            raw = terms[0][at, columns]
            normk = raw * lax.rsqrt(jnp.mean(raw * raw, axis=-1, keepdims=True) + EPS) * gain[...]
            turned = normk * cosine[at, :] + pltpu.roll(normk, HD // 2, 1) * sine[at, :]
            out[:, 2 * head * HD : (2 * head + 1) * HD] = turned.astype(jnp.bfloat16)
            out[:, (2 * head + 1) * HD : (2 * head + 2) * HD] = terms[1][at, columns].astype(
                jnp.bfloat16
            )


def mask_kernel(*refs):
    pieces, (bias, needs) = refs[1:-2], refs[-2:]
    count = bias.shape[0]
    size = count // TILES
    seg_q, pos_q = (
        jnp.transpose(jnp.broadcast_to(pieces[0][i : i + 1, :], (count, count))) for i in range(2)
    )
    width = len(pieces) * size
    for tile in range(TILES):
        for i, piece in enumerate(pieces):
            at = slice(tile * size, (tile + 1) * size)
            allowed = (piece[:1, at] == seg_q[:, at]) & (piece[1:, at] <= pos_q[:, at])
            there = tile * width + i * size
            bias[:, there : there + size] = jnp.where(allowed, 0.0, MASKED)
    for tile in range(TILES - 1):
        rows = slice(tile * size, (tile + 1) * size)
        needs[tile] = (jnp.max(bias[rows, (tile + 1) * width :]) == 0.0).astype(jnp.int32)
    needs[TILES - 1] = 0


def attend_kernel(pieces, count, place, needs, queries, bias, *rest):
    sources, (out, keys, values) = rest[:pieces], rest[-3:]
    step = pl.program_id(0)
    tile_rows = count // TILES
    length = pieces * tile_rows

    for head in range(2):

        @pl.when(step == head)
        def _():
            left = 2 * head * HD
            for i, source in enumerate(sources):
                for tile in range(TILES):
                    here = slice(tile * tile_rows, (tile + 1) * tile_rows)
                    there = tile * length + i * tile_rows
                    keys[there : there + tile_rows, :] = source[here, left : left + HD]
                    values[there : there + tile_rows, :HD] = source[here, left + HD : left + 2 * HD]

    @pl.when(step == 0)
    def _():
        values[:, HD:] = jnp.ones((pieces * count, HD), jnp.bfloat16)

    factor = math.log2(math.e) / math.sqrt(HD)

    def tile_body(tile, high):
        rows = slice(tile * tile_rows, (tile + 1) * tile_rows)
        k, v, b = keys[:high, :], values[:high, :], bias[rows, :high]

        def score(step):
            heads = range(step * WIDE, (step + 1) * WIDE)
            q = jnp.concatenate([queries[rows, g * HD : (g + 1) * HD] for g in heads], axis=0)
            return lax.dot_general(
                q, k, (((1,), (1,)), ((), ())), preferred_element_type=jnp.float32
            )

        ahead = score(0)
        for step in range(G // WIDE):
            scores = ahead.reshape(WIDE, tile_rows, high) + b[None]
            if step + 1 < G // WIDE:
                ahead = score(step + 1)
            top = jnp.max(scores, axis=-1, keepdims=True)
            weights = jnp.exp2((scores - top) * factor)
            summed = jnp.dot(
                weights.astype(jnp.bfloat16).reshape(WIDE * tile_rows, high),
                v,
                preferred_element_type=jnp.float32,
            )
            result = (summed[:, :HD] / summed[:, HD:]).astype(jnp.bfloat16)
            for i in range(WIDE):
                g = step * WIDE + i
                out[rows, g * HD : (g + 1) * HD] = result[i * tile_rows : (i + 1) * tile_rows]

    for tile in range(TILES):
        for need, high in ((0, tile + 1), (1, TILES)):

            @pl.when(needs[tile] == need)
            def _():
                tile_body(tile, high * length)


def swap(array, axis):
    return lax.ppermute(array, axis, [(0, 1), (1, 0)])


def on_device(
    sizes, hidden, queries, norm_gain, key_gain, k_weight, v_weight, segment, position
):
    chips_z, groups = sizes[0], sizes[3]
    count, width = hidden.shape[1:]
    own_rows = k_weight.shape[0]
    rows = 2 * own_rows
    chunks = 2 * chips_z
    m = 2 * groups
    z, y = lax.axis_index("z"), lax.axis_index("y")
    core, x = lax.axis_index("core"), lax.axis_index("x")
    bf16 = jnp.bfloat16
    whole = pl.BlockSpec(memory_space=pltpu.VMEM)
    params = pltpu.CompilerParams(vmem_limit_bytes=VMEM_LIMIT)

    def along_ctx(array, d, cross=False):
        pairs = []
        for c in range(2):
            for i in range(m):
                pairs.append((c * m + i, (c ^ int(cross)) * m + (i + d) % m))
        return lax.ppermute(array, ("core", "ctx", "x"), pairs)

    def columns(which):
        at = which * 2 * HD
        return jnp.stack(
            [lax.dynamic_slice_in_dim(w, at, 2 * HD, 1) for w in (k_weight, v_weight)]
        )

    taken = swap(columns(1 - core), "core")
    kept = columns(core)
    chip = lax.dynamic_update_slice(
        jnp.zeros((2, rows, 2 * HD), bf16), kept, (0, core * own_rows, 0)
    )
    chip = lax.dynamic_update_slice(chip, taken, (0, (1 - core) * own_rows, 0))
    hidden, segment, position, chip = lax.optimization_barrier((hidden, segment, position, chip))
    normed = pl.pallas_call(
        functools.partial(norm_kernel, chunks),
        out_shape=jax.ShapeDtypeStruct((chunks, count, rows), bf16),
        in_specs=[pl.BlockSpec(memory_space=pltpu.HBM), whole],
        out_specs=whole,
        scratch_shapes=[
            pltpu.VMEM((count, width), bf16),
            pltpu.SemaphoreType.DMA((count // NORM_ROWS,)),
        ],
        compiler_params=params,
        cost_estimate=pl.CostEstimate(
            flops=4 * count * width, bytes_accessed=4 * count * width, transcendentals=0
        ),
        name="norm",
    )(hidden[0], norm_gain[None])
    ints = jnp.concatenate([segment, position])
    ints_all = [ints] + [along_ctx(ints, d) for d in range(1, m)]
    ints_other = swap(ints, "core")

    acc_shape = jax.ShapeDtypeStruct((2, 2 * count, 2 * HD), jnp.float32)
    kv_shape = jax.ShapeDtypeStruct((count, 4 * HD), bf16)

    def project(groups, acc=None, last=False, also=None):
        arrays = [] if also is None else [also]
        for k, near in groups:
            if k == 0:
                arrays.append(chip if near else chip_beside)
            else:
                arrays += [mine[k], across[k]] if near else [beside[k], corner[k]]
        accs = [] if acc is None else [acc]
        outs = pl.pallas_call(
            functools.partial(project_kernel, groups, also is None, acc is None, last, count),
            out_shape=[kv_shape] * 2 if last else [acc_shape],
            in_specs=[pl.BlockSpec(memory_space=pltpu.SMEM)]
            + [pl.BlockSpec(memory_space=pltpu.HBM)] * (2 + len(arrays))
            + [whole] * (len(accs) + (3 if last else 0)),
            out_specs=[whole] * (2 if last else 1),
            scratch_shapes=[
                pltpu.VMEM((len(groups), 2, rows, 2 * HD), bf16),
                pltpu.VMEM((len(groups), 2 * count, rows), bf16),
                pltpu.SemaphoreType.DMA((len(groups), 4)),
            ],
            compiler_params=params,
            cost_estimate=pl.CostEstimate(
                flops=SLOW * 2 * 2 * count * rows * 4 * HD * len(groups),
                bytes_accessed=SLOW * 2 * rows * (4 * HD + 2 * count) * len(groups),
                transcendentals=0,
            ),
            name="project",
        )(
            place, normed, normed_other, *arrays, *accs,
            *((cosine, sine, key_gain[None]) if last else ()),
        )
        return outs if last else outs[0]

    order = [i ^ (i >> 1) for i in range(chips_z)]
    ring = [(order[i], order[(i + 1) % chips_z]) for i in range(chips_z)]
    spot = sum(jnp.where(z == order[i], i, 0) for i in range(chips_z))
    place = jnp.stack([y, x, spot]).astype(jnp.int32)
    tie = lax.optimization_barrier
    end = chips_z - 1
    mine = {0: lax.dynamic_index_in_dim(chip, x, 0, keepdims=False)}
    across, beside, corner = {}, {}, {}
    chip_beside = swap(chip, "y")
    acc = None
    for k in range(1, chips_z):
        mine[k] = lax.ppermute(mine[k - 1], "z", ring)
        if k == 1:
            tied = tie((mine[k], normed, ints_all, ints_other))
            mine[k], normed, ints_all, ints_other = tied
            normed_other = swap(normed, "core")
            bias, needs = pl.pallas_call(
                mask_kernel,
                out_shape=[
                    jax.ShapeDtypeStruct((count, m * count), jnp.float32),
                    jax.ShapeDtypeStruct((TILES,), jnp.int32),
                ],
                in_specs=[pl.BlockSpec(memory_space=pltpu.HBM)] + [whole] * m,
                out_specs=[whole, pl.BlockSpec(memory_space=pltpu.SMEM)],
                compiler_params=params,
                cost_estimate=pl.CostEstimate(
                    flops=MASK_COST, bytes_accessed=MASK_COST // 300, transcendentals=0
                ),
                name="mask",
            )(chip_beside, *ints_all)
        elif k > 2:
            if acc is None:
                acc = project([(0, True), (0, False)])
            acc = project([(k - 2, True)], acc, also=beside[k - 2])
            if k == 3:
                mine[k], acc, bias = tie((mine[k], acc, bias))
            else:
                mine[k], acc = tie((mine[k], acc))
        across[k], beside[k] = swap(mine[k], "x"), swap(mine[k], "y")
    for k in range(1, chips_z):
        if k < end:
            corner[k] = swap(beside[k], "x") if k % 2 else swap(across[k], "y")
    acc = project([(end - 1, True), (1, False)], acc, also=beside[end - 1])
    beside[end], acc = tie((beside[end], acc))
    corner[end] = swap(beside[end], "x")

    where = jnp.concatenate([position[0], ints_other[1]]).astype(jnp.float32)
    half = HD // 2
    freq = np.exp(np.arange(half, dtype=np.float32) * np.float32(-2.0 * math.log(THETA) / HD))
    angle = where[:, None] * freq[None, :]
    cosine, sine = jnp.cos(angle), jnp.sin(angle)
    cosine = jnp.concatenate([cosine, cosine], axis=1)
    sine = jnp.concatenate([-sine, sine], axis=1)

    acc = project([(end, True)] + [(k, False) for k in range(2, end)], acc)
    kv_own, kv_other = project([(end, False)], acc, last=True)

    result = None
    for cross, kv in enumerate((kv_own, kv_other)):
        sources = [kv if d == 0 and not cross else along_ctx(kv, d, cross) for d in range(m)]

        def block(step, place, needs, cross=cross):
            return (0, lax.rem(place[0] + cross, 2) * 2 + step)

        earlier = [] if result is None else [result]
        result = pl.pallas_call(
            functools.partial(attend_kernel, m, count),
            out_shape=jax.ShapeDtypeStruct((count, KVH * G * HD), bf16),
            grid_spec=pltpu.PrefetchScalarGridSpec(
                num_scalar_prefetch=2,
                grid=(2,),
                in_specs=[pl.BlockSpec((count, G * HD), block)]
                + [whole] * (1 + m)
                + [pl.BlockSpec(memory_space=pl.ANY)] * len(earlier),
                out_specs=pl.BlockSpec((count, G * HD), block),
                scratch_shapes=[
                    pltpu.VMEM((m * count, HD), bf16),
                    pltpu.VMEM((m * count, 2 * HD), bf16),
                ],
            ),
            input_output_aliases={4 + m: 0} if earlier else {},
            compiler_params=params,
            cost_estimate=pl.CostEstimate(
                flops=2 * count * m * count * KVH * G * HD,
                bytes_accessed=2 * count * KVH * G * HD,
                transcendentals=count * m * count * KVH * G // 2,
            ),
            name="attend",
        )(core.astype(jnp.int32)[None], needs, queries[0], bias, *sources, *earlier)
    return result[None]


def solution(mesh):
    n, m = mesh.shape["fsdp"], mesh.shape["ctx"]
    sizes = (n // 4, 2, 2, m // 2, 2)
    fine = Mesh(mesh.devices.reshape(sizes), ("z", "y", "core", "ctx", "x"))
    fsdp, ctx = ("z", "y", "core"), ("ctx", "x")
    placed = (
        P(fsdp, ctx, None),
        P(fsdp, ctx, None),
        P(),
        P(),
        P(fsdp, None),
        P(fsdp, None),
        P(fsdp, ctx),
        P(fsdp, ctx),
    )
    return jax.shard_map(
        functools.partial(on_device, sizes),
        mesh=fine,
        in_specs=placed,
        out_specs=P(fsdp, ctx, None),
        check_vma=False,
    )
```

```python
import functools
import math

import jax
import jax.numpy as jnp
import numpy as np
from jax import lax
from jax.experimental import pallas as pl
from jax.experimental.pallas import tpu as pltpu
from jax.sharding import Mesh
from jax.sharding import PartitionSpec as P

KVH = 4
HD = 128
G = 8
EPS = 1e-06
THETA = 1000000.0
MASKED = -1e30
VMEM_LIMIT = 24 * 2**20
NORM_ROWS = 64
WIDE = 4
TILES = 2
HINT = 8
MASK_COST = 1 * 10**9


def norm_kernel(chunks, hidden, gain, out, held, sems):
    steps = held.shape[0] // NORM_ROWS
    copies = []
    for i in range(steps):
        at = pl.ds(i * NORM_ROWS, NORM_ROWS)
        copies.append(pltpu.make_async_copy(hidden.at[at], held.at[at], sems.at[i]))
        copies[-1].start()
    for i, copy in enumerate(copies):
        copy.wait()
        at = pl.ds(i * NORM_ROWS, NORM_ROWS)
        inputs = held[at, :].astype(jnp.float32)
        scale = lax.rsqrt(jnp.mean(inputs * inputs, axis=-1, keepdims=True) + EPS)
        normed = (inputs * scale * gain[...]).astype(jnp.bfloat16)
        rows = normed.shape[1] // chunks
        for j in range(chunks):
            out[j, at, :] = normed[:, j * rows : (j + 1) * rows]


def project_kernel(groups, alone, first, last, count, place, own, other, *rest):
    chips_z = own.shape[0] // 2
    y, x, spot = place[0], place[1], place[2]
    rest = list(rest) if alone else list(rest[1:])
    weight, lhs, sems = rest[-3:]
    waits = []
    for g, (k, near) in enumerate(groups):
        i = lax.rem(spot - k + chips_z, chips_z)
        chunk = (i ^ (i >> 1)) * 2 + (y if near else 1 - y)
        pairs = [
            (own.at[chunk], lhs.at[g, pl.ds(0, count)]),
            (other.at[chunk], lhs.at[g, pl.ds(count, count)]),
        ]
        if k == 0:
            pairs.append((rest.pop(0), weight.at[g]))
        else:
            pairs.append((rest.pop(0), weight.at[g, x]))
            pairs.append((rest.pop(0), weight.at[g, 1 - x]))
        copies = [
            pltpu.make_async_copy(source, target, sems.at[g, i])
            for i, (source, target) in enumerate(pairs)
        ]
        for copy in copies:
            copy.start()
        waits.append(copies)
    earlier = None if first else rest.pop(0)
    terms = [None, None]
    for g, copies in enumerate(waits):
        for copy in copies:
            copy.wait()
        for half in range(2):
            part = jnp.dot(lhs[g], weight[g, half], preferred_element_type=jnp.float32)
            terms[half] = part if terms[half] is None else terms[half] + part
    for half in range(2):
        if not first:
            terms[half] += earlier[half]
        if not last:
            rest[0][half] = terms[half]
    if not last:
        return
    cosine, sine, gain = rest[:3]
    outs = rest[3:5]
    for head in range(2):
        columns = slice(head * HD, (head + 1) * HD)
        for part, out in enumerate(outs):
            at = slice(part * count, (part + 1) * count)
            raw = terms[0][at, columns]
            normk = raw * lax.rsqrt(jnp.mean(raw * raw, axis=-1, keepdims=True) + EPS) * gain[...]
            turned = normk * cosine[at, :] + pltpu.roll(normk, HD // 2, 1) * sine[at, :]
            out[:, 2 * head * HD : (2 * head + 1) * HD] = turned.astype(jnp.bfloat16)
            out[:, (2 * head + 1) * HD : (2 * head + 2) * HD] = terms[1][at, columns].astype(
                jnp.bfloat16
            )


def mask_kernel(*refs):
    pieces, (bias, needs) = refs[1:-2], refs[-2:]
    count = bias.shape[0]
    size = count // TILES
    seg_q, pos_q = (
        jnp.transpose(jnp.broadcast_to(pieces[0][i : i + 1, :], (count, count))) for i in range(2)
    )
    width = len(pieces) * size
    for tile in range(TILES):
        for i, piece in enumerate(pieces):
            at = slice(tile * size, (tile + 1) * size)
            allowed = (piece[:1, at] == seg_q[:, at]) & (piece[1:, at] <= pos_q[:, at])
            there = tile * width + i * size
            bias[:, there : there + size] = jnp.where(allowed, 0.0, MASKED)
    for tile in range(TILES - 1):
        rows = slice(tile * size, (tile + 1) * size)
        needs[tile] = (jnp.max(bias[rows, (tile + 1) * width :]) == 0.0).astype(jnp.int32)
    needs[TILES - 1] = 0


def attend_kernel(pieces, count, place, needs, queries, bias, *rest):
    sources, (out, keys, values) = rest[:pieces], rest[-3:]
    step = pl.program_id(0)
    tile_rows = count // TILES
    length = pieces * tile_rows

    for head in range(2):

        @pl.when(step == head)
        def _():
            left = 2 * head * HD
            for i, source in enumerate(sources):
                for tile in range(TILES):
                    here = slice(tile * tile_rows, (tile + 1) * tile_rows)
                    there = tile * length + i * tile_rows
                    keys[there : there + tile_rows, :] = source[here, left : left + HD]
                    values[there : there + tile_rows, :] = source[here, left + HD : left + 2 * HD]

    factor = math.log2(math.e) / math.sqrt(HD)

    def tile_body(tile, high):
        rows = slice(tile * tile_rows, (tile + 1) * tile_rows)
        k, v, b = keys[:high, :], values[:high, :], bias[rows, :high]

        def score(step):
            heads = range(step * WIDE, (step + 1) * WIDE)
            q = jnp.concatenate([queries[rows, g * HD : (g + 1) * HD] for g in heads], axis=0)
            return lax.dot_general(
                q, k, (((1,), (1,)), ((), ())), preferred_element_type=jnp.float32
            )

        ahead = score(0)
        for step in range(G // WIDE):
            scores = ahead.reshape(WIDE, tile_rows, high) + b[None]
            if step + 1 < G // WIDE:
                ahead = score(step + 1)
            top = jnp.max(scores, axis=-1, keepdims=True)
            weights = jnp.exp2((scores - top) * factor)
            total = jnp.sum(weights, axis=-1, keepdims=True)
            summed = jnp.dot(
                weights.astype(jnp.bfloat16).reshape(WIDE * tile_rows, high),
                v,
                preferred_element_type=jnp.float32,
            ).reshape(WIDE, tile_rows, HD)
            result = (summed * (1.0 / total)).astype(jnp.bfloat16)
            for i in range(WIDE):
                g = step * WIDE + i
                out[rows, g * HD : (g + 1) * HD] = result[i]

    for tile in range(TILES):
        for need, high in ((0, tile + 1), (1, TILES)):

            @pl.when(needs[tile] == need)
            def _():
                tile_body(tile, high * length)


def swap(array, axis):
    return lax.ppermute(array, axis, [(0, 1), (1, 0)])


def on_device(
    sizes, hidden, queries, norm_gain, key_gain, k_weight, v_weight, segment, position
):
    chips_z, groups = sizes[0], sizes[3]
    count, width = hidden.shape[1:]
    own_rows = k_weight.shape[0]
    rows = 2 * own_rows
    chunks = 2 * chips_z
    m = 2 * groups
    z, y = lax.axis_index("z"), lax.axis_index("y")
    core, x = lax.axis_index("core"), lax.axis_index("x")
    bf16 = jnp.bfloat16
    whole = pl.BlockSpec(memory_space=pltpu.VMEM)
    params = pltpu.CompilerParams(vmem_limit_bytes=VMEM_LIMIT)

    def along_ctx(array, d, cross=False):
        pairs = []
        for c in range(2):
            for i in range(m):
                pairs.append((c * m + i, (c ^ int(cross)) * m + (i + d) % m))
        return lax.ppermute(array, ("core", "ctx", "x"), pairs)

    def columns(which):
        at = which * 2 * HD
        return jnp.stack(
            [lax.dynamic_slice_in_dim(w, at, 2 * HD, 1) for w in (k_weight, v_weight)]
        )

    taken = swap(columns(1 - core), "core")
    kept = columns(core)
    chip = lax.dynamic_update_slice(
        jnp.zeros((2, rows, 2 * HD), bf16), kept, (0, core * own_rows, 0)
    )
    chip = lax.dynamic_update_slice(chip, taken, (0, (1 - core) * own_rows, 0))
    hidden, segment, position, chip = lax.optimization_barrier((hidden, segment, position, chip))

    def norm(array):
        return pl.pallas_call(
            functools.partial(norm_kernel, chunks),
            out_shape=jax.ShapeDtypeStruct((chunks, count, rows), bf16),
            in_specs=[pl.BlockSpec(memory_space=pltpu.HBM), whole],
            out_specs=whole,
            scratch_shapes=[
                pltpu.VMEM((count, width), bf16),
                pltpu.SemaphoreType.DMA((count // NORM_ROWS,)),
            ],
            compiler_params=params,
            cost_estimate=pl.CostEstimate(
                flops=4 * count * width, bytes_accessed=4 * count * width, transcendentals=0
            ),
            name="norm",
        )(array[0], norm_gain[None])

    normed, normed_other = norm(hidden), norm(swap(hidden, "core"))
    ints = jnp.concatenate([segment, position])
    ints_all = [ints] + [along_ctx(ints, d) for d in range(1, m)]
    ints_other = swap(ints, "core")

    acc_shape = jax.ShapeDtypeStruct((2, 2 * count, 2 * HD), jnp.float32)
    kv_shape = jax.ShapeDtypeStruct((count, 4 * HD), bf16)

    def project(groups, acc=None, last=False, also=None, hint=1):
        arrays = [] if also is None else [also]
        for k, near in groups:
            if k == 0:
                arrays.append(chip if near else chip_beside)
            else:
                arrays += [mine[k], across[k]] if near else [beside[k], corner[k]]
        accs = [] if acc is None else [acc]
        outs = pl.pallas_call(
            functools.partial(project_kernel, groups, also is None, acc is None, last, count),
            out_shape=[kv_shape] * 2 if last else [acc_shape],
            in_specs=[pl.BlockSpec(memory_space=pltpu.SMEM)]
            + [pl.BlockSpec(memory_space=pltpu.HBM)] * (2 + len(arrays))
            + [whole] * (len(accs) + (3 if last else 0)),
            out_specs=[whole] * (2 if last else 1),
            scratch_shapes=[
                pltpu.VMEM((len(groups), 2, rows, 2 * HD), bf16),
                pltpu.VMEM((len(groups), 2 * count, rows), bf16),
                pltpu.SemaphoreType.DMA((len(groups), 4)),
            ],
            compiler_params=params,
            cost_estimate=pl.CostEstimate(
                flops=hint * 2 * 2 * count * rows * 4 * HD * len(groups),
                bytes_accessed=hint * 2 * rows * (4 * HD + 2 * count) * len(groups),
                transcendentals=0,
            ),
            name="project",
        )(
            place, normed, normed_other, *arrays, *accs,
            *((cosine, sine, key_gain[None]) if last else ()),
        )
        return outs if last else outs[0]

    order = [i ^ (i >> 1) for i in range(chips_z)]
    ring = [(order[i], order[(i + 1) % chips_z]) for i in range(chips_z)]
    spot = sum(jnp.where(z == order[i], i, 0) for i in range(chips_z))
    place = jnp.stack([y, x, spot]).astype(jnp.int32)
    tie = lax.optimization_barrier
    end = chips_z - 1
    mine = {0: lax.dynamic_index_in_dim(chip, x, 0, keepdims=False)}
    across, beside, corner = {}, {}, {}
    chip_beside = swap(chip, "y")
    acc = None
    for k in range(1, chips_z):
        mine[k] = lax.ppermute(mine[k - 1], "z", ring)
        if k == 1:
            tied = tie((mine[k], normed, normed_other, ints_all, ints_other))
            mine[k], normed, normed_other, ints_all, ints_other = tied
            bias, needs = pl.pallas_call(
                mask_kernel,
                out_shape=[
                    jax.ShapeDtypeStruct((count, m * count), jnp.float32),
                    jax.ShapeDtypeStruct((TILES,), jnp.int32),
                ],
                in_specs=[pl.BlockSpec(memory_space=pltpu.HBM)] + [whole] * m,
                out_specs=[whole, pl.BlockSpec(memory_space=pltpu.SMEM)],
                compiler_params=params,
                cost_estimate=pl.CostEstimate(
                    flops=MASK_COST, bytes_accessed=MASK_COST // 300, transcendentals=0
                ),
                name="mask",
            )(chip_beside, *ints_all)
        elif k > 2:
            if acc is None:
                acc = project([(0, True), (0, False)])
            acc = project([(k - 2, True)], acc, also=beside[k - 2])
            if k == 3:
                mine[k], acc, bias = tie((mine[k], acc, bias))
            else:
                mine[k], acc = tie((mine[k], acc))
        across[k], beside[k] = swap(mine[k], "x"), swap(mine[k], "y")
    for k in range(1, chips_z):
        if k < end:
            corner[k] = swap(beside[k], "x") if k % 2 else swap(across[k], "y")
    acc = project([(end - 1, True), (1, False)], acc, also=beside[end - 1], hint=HINT)
    beside[end], acc = tie((beside[end], acc))
    corner[end] = swap(beside[end], "x")

    where = jnp.concatenate([position[0], ints_other[1]]).astype(jnp.float32)
    half = HD // 2
    freq = np.exp(np.arange(half, dtype=np.float32) * np.float32(-2.0 * math.log(THETA) / HD))
    angle = where[:, None] * freq[None, :]
    cosine, sine = jnp.cos(angle), jnp.sin(angle)
    cosine = jnp.concatenate([cosine, cosine], axis=1)
    sine = jnp.concatenate([-sine, sine], axis=1)

    acc = project([(end, True)] + [(k, False) for k in range(2, end)], acc)
    kv_own, kv_other = project([(end, False)], acc, last=True)

    result = None
    for cross, kv in enumerate((kv_own, kv_other)):
        sources = [kv if d == 0 and not cross else along_ctx(kv, d, cross) for d in range(m)]

        def block(step, place, needs, cross=cross):
            return (0, lax.rem(place[0] + cross, 2) * 2 + step)

        earlier = [] if result is None else [result]
        result = pl.pallas_call(
            functools.partial(attend_kernel, m, count),
            out_shape=jax.ShapeDtypeStruct((count, KVH * G * HD), bf16),
            grid_spec=pltpu.PrefetchScalarGridSpec(
                num_scalar_prefetch=2,
                grid=(2,),
                in_specs=[pl.BlockSpec((count, G * HD), block)]
                + [whole] * (1 + m)
                + [pl.BlockSpec(memory_space=pl.ANY)] * len(earlier),
                out_specs=pl.BlockSpec((count, G * HD), block),
                scratch_shapes=[
                    pltpu.VMEM((m * count, HD), bf16),
                    pltpu.VMEM((m * count, HD), bf16),
                ],
            ),
            input_output_aliases={4 + m: 0} if earlier else {},
            compiler_params=params,
            cost_estimate=pl.CostEstimate(
                flops=2 * count * m * count * KVH * G * HD,
                bytes_accessed=2 * count * KVH * G * HD,
                transcendentals=count * m * count * KVH * G // 2,
            ),
            name="attend",
        )(core.astype(jnp.int32)[None], needs, queries[0], bias, *sources, *earlier)
    return result[None]


def solution(mesh):
    n, m = mesh.shape["fsdp"], mesh.shape["ctx"]
    sizes = (n // 4, 2, 2, m // 2, 2)
    fine = Mesh(mesh.devices.reshape(sizes), ("z", "y", "core", "ctx", "x"))
    fsdp, ctx = ("z", "y", "core"), ("ctx", "x")
    placed = (
        P(fsdp, ctx, None),
        P(fsdp, ctx, None),
        P(),
        P(),
        P(fsdp, None),
        P(fsdp, None),
        P(fsdp, ctx),
        P(fsdp, ctx),
    )
    return jax.shard_map(
        functools.partial(on_device, sizes),
        mesh=fine,
        in_specs=placed,
        out_specs=P(fsdp, ctx, None),
        check_vma=False,
    )
```

```python
import functools
import math

import jax
import jax.numpy as jnp
import numpy as np
from jax import lax
from jax.experimental import pallas as pl
from jax.experimental.pallas import tpu as pltpu
from jax.sharding import Mesh
from jax.sharding import PartitionSpec as P

KVH = 4
HD = 128
G = 8
EPS = 1e-06
THETA = 1000000.0
MASKED = -1e30
VMEM_LIMIT = 24 * 2**20
NORM_ROWS = 64
WIDE = 4
TILES = 2
HINT = 8
MASK_COST = 1 * 10**9


def norm_kernel(chunks, hidden, gain, out, held, made, sems):
    steps = held.shape[0] // NORM_ROWS
    reads, writes = [], []
    for i in range(steps):
        at = pl.ds(i * NORM_ROWS, NORM_ROWS)
        reads.append(pltpu.make_async_copy(hidden.at[at], held.at[at], sems.at[0, i]))
        writes.append(pltpu.make_async_copy(made.at[:, at], out.at[:, at], sems.at[1, i]))
        reads[-1].start()
    for i in range(steps):
        reads[i].wait()
        at = pl.ds(i * NORM_ROWS, NORM_ROWS)
        inputs = held[at, :].astype(jnp.float32)
        scale = lax.rsqrt(jnp.mean(inputs * inputs, axis=-1, keepdims=True) + EPS)
        normed = (inputs * scale * gain[...]).astype(jnp.bfloat16)
        rows = normed.shape[1] // chunks
        for j in range(chunks):
            made[j, at, :] = normed[:, j * rows : (j + 1) * rows]
        writes[i].start()
    for write in writes:
        write.wait()


def project_kernel(groups, alone, first, last, count, place, own, other, *rest):
    chips_z = own.shape[0] // 2
    y, x, spot = place[0], place[1], place[2]
    rest = list(rest) if alone else list(rest[1:])
    weight, lhs, sems = rest[-3:]
    waits = []
    for g, (k, near) in enumerate(groups):
        i = lax.rem(spot - k + chips_z, chips_z)
        chunk = (i ^ (i >> 1)) * 2 + (y if near else 1 - y)
        pairs = [
            (own.at[chunk], lhs.at[g, pl.ds(0, count)]),
            (other.at[chunk], lhs.at[g, pl.ds(count, count)]),
        ]
        if k == 0:
            pairs.append((rest.pop(0), weight.at[g]))
        else:
            pairs.append((rest.pop(0), weight.at[g, x]))
            pairs.append((rest.pop(0), weight.at[g, 1 - x]))
        copies = [
            pltpu.make_async_copy(source, target, sems.at[g, i])
            for i, (source, target) in enumerate(pairs)
        ]
        for copy in copies:
            copy.start()
        waits.append(copies)
    earlier = None if first else rest.pop(0)
    terms = [None, None]
    for g, copies in enumerate(waits):
        for copy in copies:
            copy.wait()
        for half in range(2):
            part = jnp.dot(lhs[g], weight[g, half], preferred_element_type=jnp.float32)
            terms[half] = part if terms[half] is None else terms[half] + part
    for half in range(2):
        if not first:
            terms[half] += earlier[half]
        if not last:
            rest[0][half] = terms[half]
    if not last:
        return
    cosine, sine, gain = rest[:3]
    outs = rest[3:5]
    for head in range(2):
        columns = slice(head * HD, (head + 1) * HD)
        for part, out in enumerate(outs):
            at = slice(part * count, (part + 1) * count)
            raw = terms[0][at, columns]
            normk = raw * lax.rsqrt(jnp.mean(raw * raw, axis=-1, keepdims=True) + EPS) * gain[...]
            turned = normk * cosine[at, :] + pltpu.roll(normk, HD // 2, 1) * sine[at, :]
            out[:, 2 * head * HD : (2 * head + 1) * HD] = turned.astype(jnp.bfloat16)
            out[:, (2 * head + 1) * HD : (2 * head + 2) * HD] = terms[1][at, columns].astype(
                jnp.bfloat16
            )


def mask_kernel(*refs):
    pieces, (bias, needs) = refs[1:-2], refs[-2:]
    count = bias.shape[0]
    size = count // TILES
    seg_q, pos_q = (
        jnp.transpose(jnp.broadcast_to(pieces[0][i : i + 1, :], (count, count))) for i in range(2)
    )
    width = len(pieces) * size
    for tile in range(TILES):
        for i, piece in enumerate(pieces):
            at = slice(tile * size, (tile + 1) * size)
            allowed = (piece[:1, at] == seg_q[:, at]) & (piece[1:, at] <= pos_q[:, at])
            there = tile * width + i * size
            bias[:, there : there + size] = jnp.where(allowed, 0.0, MASKED)
    for tile in range(TILES - 1):
        rows = slice(tile * size, (tile + 1) * size)
        needs[tile] = (jnp.max(bias[rows, (tile + 1) * width :]) == 0.0).astype(jnp.int32)
    needs[TILES - 1] = 0


def attend_kernel(pieces, count, place, needs, queries, bias, *rest):
    sources, (out, keys, values) = rest[:pieces], rest[-3:]
    step = pl.program_id(0)
    tile_rows = count // TILES
    length = pieces * tile_rows

    for head in range(2):

        @pl.when(step == head)
        def _():
            left = 2 * head * HD
            for i, source in enumerate(sources):
                for tile in range(TILES):
                    here = slice(tile * tile_rows, (tile + 1) * tile_rows)
                    there = tile * length + i * tile_rows
                    keys[there : there + tile_rows, :] = source[here, left : left + HD]
                    values[there : there + tile_rows, :] = source[here, left + HD : left + 2 * HD]

    factor = math.log2(math.e) / math.sqrt(HD)

    def tile_body(tile, high):
        rows = slice(tile * tile_rows, (tile + 1) * tile_rows)
        k, v, b = keys[:high, :], values[:high, :], bias[rows, :high]

        def score(step):
            heads = range(step * WIDE, (step + 1) * WIDE)
            q = jnp.concatenate([queries[rows, g * HD : (g + 1) * HD] for g in heads], axis=0)
            return lax.dot_general(
                q, k, (((1,), (1,)), ((), ())), preferred_element_type=jnp.float32
            )

        ahead = score(0)
        for step in range(G // WIDE):
            scores = ahead.reshape(WIDE, tile_rows, high) + b[None]
            if step + 1 < G // WIDE:
                ahead = score(step + 1)
            top = jnp.max(scores, axis=-1, keepdims=True)
            weights = jnp.exp2((scores - top) * factor)
            total = jnp.sum(weights, axis=-1, keepdims=True)
            summed = jnp.dot(
                weights.astype(jnp.bfloat16).reshape(WIDE * tile_rows, high),
                v,
                preferred_element_type=jnp.float32,
            ).reshape(WIDE, tile_rows, HD)
            result = (summed * (1.0 / total)).astype(jnp.bfloat16)
            for i in range(WIDE):
                g = step * WIDE + i
                out[rows, g * HD : (g + 1) * HD] = result[i]

    for tile in range(TILES):
        for need, high in ((0, tile + 1), (1, TILES)):

            @pl.when(needs[tile] == need)
            def _():
                tile_body(tile, high * length)


def swap(array, axis):
    return lax.ppermute(array, axis, [(0, 1), (1, 0)])


def on_device(
    sizes, hidden, queries, norm_gain, key_gain, k_weight, v_weight, segment, position
):
    chips_z, groups = sizes[0], sizes[3]
    count, width = hidden.shape[1:]
    own_rows = k_weight.shape[0]
    rows = 2 * own_rows
    chunks = 2 * chips_z
    m = 2 * groups
    z, y = lax.axis_index("z"), lax.axis_index("y")
    core, x = lax.axis_index("core"), lax.axis_index("x")
    bf16 = jnp.bfloat16
    whole = pl.BlockSpec(memory_space=pltpu.VMEM)
    params = pltpu.CompilerParams(vmem_limit_bytes=VMEM_LIMIT)

    def along_ctx(array, d, cross=False):
        pairs = []
        for c in range(2):
            for i in range(m):
                pairs.append((c * m + i, (c ^ int(cross)) * m + (i + d) % m))
        return lax.ppermute(array, ("core", "ctx", "x"), pairs)

    def columns(which):
        at = which * 2 * HD
        return jnp.stack(
            [lax.dynamic_slice_in_dim(w, at, 2 * HD, 1) for w in (k_weight, v_weight)]
        )

    taken = swap(columns(1 - core), "core")
    kept = columns(core)
    chip = lax.dynamic_update_slice(
        jnp.zeros((2, rows, 2 * HD), bf16), kept, (0, core * own_rows, 0)
    )
    chip = lax.dynamic_update_slice(chip, taken, (0, (1 - core) * own_rows, 0))
    hidden, segment, position, chip = lax.optimization_barrier((hidden, segment, position, chip))

    def norm(array):
        return pl.pallas_call(
            functools.partial(norm_kernel, chunks),
            out_shape=jax.ShapeDtypeStruct((chunks, count, rows), bf16),
            in_specs=[pl.BlockSpec(memory_space=pltpu.HBM), whole],
            out_specs=pl.BlockSpec(memory_space=pltpu.HBM),
            scratch_shapes=[
                pltpu.VMEM((count, width), bf16),
                pltpu.VMEM((chunks, count, rows), bf16),
                pltpu.SemaphoreType.DMA((2, count // NORM_ROWS)),
            ],
            compiler_params=params,
            cost_estimate=pl.CostEstimate(
                flops=4 * count * width, bytes_accessed=4 * count * width, transcendentals=0
            ),
            name="norm",
        )(array[0], norm_gain[None])

    normed, normed_other = norm(hidden), norm(swap(hidden, "core"))
    ints = jnp.concatenate([segment, position])
    ints_all = [ints] + [along_ctx(ints, d) for d in range(1, m)]
    ints_other = swap(ints, "core")

    acc_shape = jax.ShapeDtypeStruct((2, 2 * count, 2 * HD), jnp.float32)
    kv_shape = jax.ShapeDtypeStruct((count, 4 * HD), bf16)

    def project(groups, acc=None, last=False, also=None, hint=1):
        arrays = [] if also is None else [also]
        for k, near in groups:
            if k == 0:
                arrays.append(chip if near else chip_beside)
            else:
                arrays += [mine[k], across[k]] if near else [beside[k], corner[k]]
        accs = [] if acc is None else [acc]
        outs = pl.pallas_call(
            functools.partial(project_kernel, groups, also is None, acc is None, last, count),
            out_shape=[kv_shape] * 2 if last else [acc_shape],
            in_specs=[pl.BlockSpec(memory_space=pltpu.SMEM)]
            + [pl.BlockSpec(memory_space=pltpu.HBM)] * (2 + len(arrays))
            + [whole] * (len(accs) + (3 if last else 0)),
            out_specs=[whole] * (2 if last else 1),
            scratch_shapes=[
                pltpu.VMEM((len(groups), 2, rows, 2 * HD), bf16),
                pltpu.VMEM((len(groups), 2 * count, rows), bf16),
                pltpu.SemaphoreType.DMA((len(groups), 4)),
            ],
            compiler_params=params,
            cost_estimate=pl.CostEstimate(
                flops=hint * 2 * 2 * count * rows * 4 * HD * len(groups),
                bytes_accessed=hint * 2 * rows * (4 * HD + 2 * count) * len(groups),
                transcendentals=0,
            ),
            name="project",
        )(
            place, normed, normed_other, *arrays, *accs,
            *((cosine, sine, key_gain[None]) if last else ()),
        )
        return outs if last else outs[0]

    order = [i ^ (i >> 1) for i in range(chips_z)]
    ring = [(order[i], order[(i + 1) % chips_z]) for i in range(chips_z)]
    spot = sum(jnp.where(z == order[i], i, 0) for i in range(chips_z))
    place = jnp.stack([y, x, spot]).astype(jnp.int32)
    tie = lax.optimization_barrier
    end = chips_z - 1
    mine = {0: lax.dynamic_index_in_dim(chip, x, 0, keepdims=False)}
    across, beside, corner = {}, {}, {}
    chip_beside = swap(chip, "y")
    acc = None
    for k in range(1, chips_z):
        mine[k] = lax.ppermute(mine[k - 1], "z", ring)
        if k == 1:
            tied = tie((mine[k], normed, normed_other, ints_all, ints_other))
            mine[k], normed, normed_other, ints_all, ints_other = tied
            bias, needs = pl.pallas_call(
                mask_kernel,
                out_shape=[
                    jax.ShapeDtypeStruct((count, m * count), jnp.float32),
                    jax.ShapeDtypeStruct((TILES,), jnp.int32),
                ],
                in_specs=[pl.BlockSpec(memory_space=pltpu.HBM)] + [whole] * m,
                out_specs=[whole, pl.BlockSpec(memory_space=pltpu.SMEM)],
                compiler_params=params,
                cost_estimate=pl.CostEstimate(
                    flops=MASK_COST, bytes_accessed=MASK_COST // 300, transcendentals=0
                ),
                name="mask",
            )(chip_beside, *ints_all)
        elif k > 2:
            if acc is None:
                acc = project([(0, True), (0, False)])
            acc = project([(k - 2, True)], acc, also=beside[k - 2])
            if k == 3:
                mine[k], acc, bias = tie((mine[k], acc, bias))
            else:
                mine[k], acc = tie((mine[k], acc))
        across[k], beside[k] = swap(mine[k], "x"), swap(mine[k], "y")
    for k in range(1, chips_z):
        if k < end:
            corner[k] = swap(beside[k], "x") if k % 2 else swap(across[k], "y")
    acc = project([(end - 1, True), (1, False)], acc, also=beside[end - 1], hint=HINT)
    beside[end], acc = tie((beside[end], acc))
    corner[end] = swap(beside[end], "x")

    where = jnp.concatenate([position[0], ints_other[1]]).astype(jnp.float32)
    half = HD // 2
    freq = np.exp(np.arange(half, dtype=np.float32) * np.float32(-2.0 * math.log(THETA) / HD))
    angle = where[:, None] * freq[None, :]
    cosine, sine = jnp.cos(angle), jnp.sin(angle)
    cosine = jnp.concatenate([cosine, cosine], axis=1)
    sine = jnp.concatenate([-sine, sine], axis=1)

    acc = project([(end, True)] + [(k, False) for k in range(2, end)], acc)
    kv_own, kv_other = project([(end, False)], acc, last=True)

    result = None
    for cross, kv in enumerate((kv_own, kv_other)):
        sources = [kv if d == 0 and not cross else along_ctx(kv, d, cross) for d in range(m)]

        def block(step, place, needs, cross=cross):
            return (0, lax.rem(place[0] + cross, 2) * 2 + step)

        earlier = [] if result is None else [result]
        result = pl.pallas_call(
            functools.partial(attend_kernel, m, count),
            out_shape=jax.ShapeDtypeStruct((count, KVH * G * HD), bf16),
            grid_spec=pltpu.PrefetchScalarGridSpec(
                num_scalar_prefetch=2,
                grid=(2,),
                in_specs=[pl.BlockSpec((count, G * HD), block)]
                + [whole] * (1 + m)
                + [pl.BlockSpec(memory_space=pl.ANY)] * len(earlier),
                out_specs=pl.BlockSpec((count, G * HD), block),
                scratch_shapes=[
                    pltpu.VMEM((m * count, HD), bf16),
                    pltpu.VMEM((m * count, HD), bf16),
                ],
            ),
            input_output_aliases={4 + m: 0} if earlier else {},
            compiler_params=params,
            cost_estimate=pl.CostEstimate(
                flops=2 * count * m * count * KVH * G * HD,
                bytes_accessed=2 * count * KVH * G * HD,
                transcendentals=count * m * count * KVH * G // 2,
            ),
            name="attend",
        )(core.astype(jnp.int32)[None], needs, queries[0], bias, *sources, *earlier)
    return result[None]


def solution(mesh):
    n, m = mesh.shape["fsdp"], mesh.shape["ctx"]
    sizes = (n // 4, 2, 2, m // 2, 2)
    fine = Mesh(mesh.devices.reshape(sizes), ("z", "y", "core", "ctx", "x"))
    fsdp, ctx = ("z", "y", "core"), ("ctx", "x")
    placed = (
        P(fsdp, ctx, None),
        P(fsdp, ctx, None),
        P(),
        P(),
        P(fsdp, None),
        P(fsdp, None),
        P(fsdp, ctx),
        P(fsdp, ctx),
    )
    return jax.shard_map(
        functools.partial(on_device, sizes),
        mesh=fine,
        in_specs=placed,
        out_specs=P(fsdp, ctx, None),
        check_vma=False,
    )
```

```python
import functools
import math

import jax
import jax.numpy as jnp
import numpy as np
from jax import lax
from jax.experimental import pallas as pl
from jax.experimental.pallas import tpu as pltpu
from jax.sharding import Mesh
from jax.sharding import PartitionSpec as P

KVH = 4
HD = 128
G = 8
EPS = 1e-06
THETA = 1000000.0
MASKED = -1e30
VMEM_LIMIT = 24 * 2**20
NORM_ROWS = 64
WIDE = 4
TILES = 2
HINT = 8
MASK_COST = 1 * 10**9


def norm_kernel(chunks, hidden, gain, out, token, held, sems):
    steps = held.shape[0] // NORM_ROWS
    copies = []
    for i in range(steps):
        at = pl.ds(i * NORM_ROWS, NORM_ROWS)
        copies.append(pltpu.make_async_copy(hidden.at[at], held.at[at], sems.at[i]))
        copies[-1].start()
    for i, copy in enumerate(copies):
        copy.wait()
        at = pl.ds(i * NORM_ROWS, NORM_ROWS)
        inputs = held[at, :].astype(jnp.float32)
        scale = lax.rsqrt(jnp.mean(inputs * inputs, axis=-1, keepdims=True) + EPS)
        normed = (inputs * scale * gain[...]).astype(jnp.bfloat16)
        rows = normed.shape[1] // chunks
        for j in range(chunks):
            out[j, at, :] = normed[:, j * rows : (j + 1) * rows]
    token[...] = jnp.zeros_like(token)


def project_kernel(groups, alone, first, last, count, place, own, other, *rest):
    chips_z = own.shape[0] // 2
    y, x, spot = place[0], place[1], place[2]
    rest = list(rest) if alone else list(rest[1:])
    weight, lhs, sems = rest[-3:]
    waits = []
    for g, (k, near) in enumerate(groups):
        i = lax.rem(spot - k + chips_z, chips_z)
        chunk = (i ^ (i >> 1)) * 2 + (y if near else 1 - y)
        pairs = [
            (own.at[chunk], lhs.at[g, pl.ds(0, count)]),
            (other.at[chunk], lhs.at[g, pl.ds(count, count)]),
        ]
        if k == 0:
            pairs.append((rest.pop(0), weight.at[g]))
        else:
            pairs.append((rest.pop(0), weight.at[g, x]))
            pairs.append((rest.pop(0), weight.at[g, 1 - x]))
        copies = [
            pltpu.make_async_copy(source, target, sems.at[g, i])
            for i, (source, target) in enumerate(pairs)
        ]
        for copy in copies:
            copy.start()
        waits.append(copies)
    earlier = None if first else rest.pop(0)
    terms = [None, None]
    for g, copies in enumerate(waits):
        for copy in copies:
            copy.wait()
        for half in range(2):
            part = jnp.dot(lhs[g], weight[g, half], preferred_element_type=jnp.float32)
            terms[half] = part if terms[half] is None else terms[half] + part
    for half in range(2):
        if not first:
            terms[half] += earlier[half]
        if not last:
            rest[0][half] = terms[half]
    if not last:
        return
    cosine, sine, gain = rest[:3]
    outs = rest[3:5]
    for head in range(2):
        columns = slice(head * HD, (head + 1) * HD)
        for part, out in enumerate(outs):
            at = slice(part * count, (part + 1) * count)
            raw = terms[0][at, columns]
            normk = raw * lax.rsqrt(jnp.mean(raw * raw, axis=-1, keepdims=True) + EPS) * gain[...]
            turned = normk * cosine[at, :] + pltpu.roll(normk, HD // 2, 1) * sine[at, :]
            out[:, 2 * head * HD : (2 * head + 1) * HD] = turned.astype(jnp.bfloat16)
            out[:, (2 * head + 1) * HD : (2 * head + 2) * HD] = terms[1][at, columns].astype(
                jnp.bfloat16
            )


def mask_kernel(*refs):
    pieces, (bias, needs) = refs[3:-2], refs[-2:]
    count = bias.shape[0]
    size = count // TILES
    seg_q, pos_q = (
        jnp.transpose(jnp.broadcast_to(pieces[0][i : i + 1, :], (count, count))) for i in range(2)
    )
    width = len(pieces) * size
    for tile in range(TILES):
        for i, piece in enumerate(pieces):
            at = slice(tile * size, (tile + 1) * size)
            allowed = (piece[:1, at] == seg_q[:, at]) & (piece[1:, at] <= pos_q[:, at])
            there = tile * width + i * size
            bias[:, there : there + size] = jnp.where(allowed, 0.0, MASKED)
    for tile in range(TILES - 1):
        rows = slice(tile * size, (tile + 1) * size)
        needs[tile] = (jnp.max(bias[rows, (tile + 1) * width :]) == 0.0).astype(jnp.int32)
    needs[TILES - 1] = 0


def attend_kernel(pieces, count, place, needs, queries, bias, *rest):
    sources, (out, keys, values) = rest[:pieces], rest[-3:]
    step = pl.program_id(0)
    tile_rows = count // TILES
    length = pieces * tile_rows

    for head in range(2):

        @pl.when(step == head)
        def _():
            left = 2 * head * HD
            for i, source in enumerate(sources):
                for tile in range(TILES):
                    here = slice(tile * tile_rows, (tile + 1) * tile_rows)
                    there = tile * length + i * tile_rows
                    keys[there : there + tile_rows, :] = source[here, left : left + HD]
                    values[there : there + tile_rows, :] = source[here, left + HD : left + 2 * HD]

    factor = math.log2(math.e) / math.sqrt(HD)

    def tile_body(tile, high):
        rows = slice(tile * tile_rows, (tile + 1) * tile_rows)
        k, v, b = keys[:high, :], values[:high, :], bias[rows, :high]

        def score(step):
            heads = range(step * WIDE, (step + 1) * WIDE)
            q = jnp.concatenate([queries[rows, g * HD : (g + 1) * HD] for g in heads], axis=0)
            return lax.dot_general(
                q, k, (((1,), (1,)), ((), ())), preferred_element_type=jnp.float32
            )

        ahead = score(0)
        for step in range(G // WIDE):
            scores = ahead.reshape(WIDE, tile_rows, high) + b[None]
            if step + 1 < G // WIDE:
                ahead = score(step + 1)
            top = jnp.max(scores, axis=-1, keepdims=True)
            weights = jnp.exp2((scores - top) * factor)
            total = jnp.sum(weights, axis=-1, keepdims=True)
            summed = jnp.dot(
                weights.astype(jnp.bfloat16).reshape(WIDE * tile_rows, high),
                v,
                preferred_element_type=jnp.float32,
            ).reshape(WIDE, tile_rows, HD)
            result = (summed * (1.0 / total)).astype(jnp.bfloat16)
            for i in range(WIDE):
                g = step * WIDE + i
                out[rows, g * HD : (g + 1) * HD] = result[i]

    for tile in range(TILES):
        for need, high in ((0, tile + 1), (1, TILES)):

            @pl.when(needs[tile] == need)
            def _():
                tile_body(tile, high * length)


def swap(array, axis):
    return lax.ppermute(array, axis, [(0, 1), (1, 0)])


def on_device(
    sizes, hidden, queries, norm_gain, key_gain, k_weight, v_weight, segment, position
):
    chips_z, groups = sizes[0], sizes[3]
    count, width = hidden.shape[1:]
    own_rows = k_weight.shape[0]
    rows = 2 * own_rows
    chunks = 2 * chips_z
    m = 2 * groups
    z, y = lax.axis_index("z"), lax.axis_index("y")
    core, x = lax.axis_index("core"), lax.axis_index("x")
    bf16 = jnp.bfloat16
    whole = pl.BlockSpec(memory_space=pltpu.VMEM)
    params = pltpu.CompilerParams(vmem_limit_bytes=VMEM_LIMIT)

    def along_ctx(array, d, cross=False):
        pairs = []
        for c in range(2):
            for i in range(m):
                pairs.append((c * m + i, (c ^ int(cross)) * m + (i + d) % m))
        return lax.ppermute(array, ("core", "ctx", "x"), pairs)

    def columns(which):
        at = which * 2 * HD
        return jnp.stack(
            [lax.dynamic_slice_in_dim(w, at, 2 * HD, 1) for w in (k_weight, v_weight)]
        )

    taken = swap(columns(1 - core), "core")
    kept = columns(core)
    chip = lax.dynamic_update_slice(
        jnp.zeros((2, rows, 2 * HD), bf16), kept, (0, core * own_rows, 0)
    )
    chip = lax.dynamic_update_slice(chip, taken, (0, (1 - core) * own_rows, 0))
    hidden, segment, position, chip = lax.optimization_barrier((hidden, segment, position, chip))

    def norm(array):
        return pl.pallas_call(
            functools.partial(norm_kernel, chunks),
            out_shape=[
                jax.ShapeDtypeStruct((chunks, count, rows), bf16),
                jax.ShapeDtypeStruct((8, 128), jnp.float32),
            ],
            in_specs=[pl.BlockSpec(memory_space=pltpu.HBM), whole],
            out_specs=[whole] * 2,
            scratch_shapes=[
                pltpu.VMEM((count, width), bf16),
                pltpu.SemaphoreType.DMA((count // NORM_ROWS,)),
            ],
            compiler_params=params,
            cost_estimate=pl.CostEstimate(
                flops=4 * count * width, bytes_accessed=4 * count * width, transcendentals=0
            ),
            name="norm",
        )(array[0], norm_gain[None])

    normed, token = norm(hidden)
    normed_other, token_other = norm(swap(hidden, "core"))
    ints = jnp.concatenate([segment, position])
    ints_all = [ints] + [along_ctx(ints, d) for d in range(1, m)]
    ints_other = swap(ints, "core")

    acc_shape = jax.ShapeDtypeStruct((2, 2 * count, 2 * HD), jnp.float32)
    kv_shape = jax.ShapeDtypeStruct((count, 4 * HD), bf16)

    def project(groups, acc=None, last=False, also=None, hint=1):
        arrays = [] if also is None else [also]
        for k, near in groups:
            if k == 0:
                arrays.append(chip if near else chip_beside)
            else:
                arrays += [mine[k], across[k]] if near else [beside[k], corner[k]]
        accs = [] if acc is None else [acc]
        outs = pl.pallas_call(
            functools.partial(project_kernel, groups, also is None, acc is None, last, count),
            out_shape=[kv_shape] * 2 if last else [acc_shape],
            in_specs=[pl.BlockSpec(memory_space=pltpu.SMEM)]
            + [pl.BlockSpec(memory_space=pltpu.HBM)] * (2 + len(arrays))
            + [whole] * (len(accs) + (3 if last else 0)),
            out_specs=[whole] * (2 if last else 1),
            scratch_shapes=[
                pltpu.VMEM((len(groups), 2, rows, 2 * HD), bf16),
                pltpu.VMEM((len(groups), 2 * count, rows), bf16),
                pltpu.SemaphoreType.DMA((len(groups), 4)),
            ],
            compiler_params=params,
            cost_estimate=pl.CostEstimate(
                flops=hint * 2 * 2 * count * rows * 4 * HD * len(groups),
                bytes_accessed=hint * 2 * rows * (4 * HD + 2 * count) * len(groups),
                transcendentals=0,
            ),
            name="project",
        )(
            place, normed, normed_other, *arrays, *accs,
            *((cosine, sine, key_gain[None]) if last else ()),
        )
        return outs if last else outs[0]

    order = [i ^ (i >> 1) for i in range(chips_z)]
    ring = [(order[i], order[(i + 1) % chips_z]) for i in range(chips_z)]
    spot = sum(jnp.where(z == order[i], i, 0) for i in range(chips_z))
    place = jnp.stack([y, x, spot]).astype(jnp.int32)
    tie = lax.optimization_barrier
    end = chips_z - 1
    mine = {0: lax.dynamic_index_in_dim(chip, x, 0, keepdims=False)}
    across, beside, corner = {}, {}, {}
    chip_beside = swap(chip, "y")
    acc = None
    for k in range(1, chips_z):
        mine[k] = lax.ppermute(mine[k - 1], "z", ring)
        if k == 1:
            tied = tie((mine[k], token, token_other, ints_all, ints_other))
            mine[k], token, token_other, ints_all, ints_other = tied
            bias, needs = pl.pallas_call(
                mask_kernel,
                out_shape=[
                    jax.ShapeDtypeStruct((count, m * count), jnp.float32),
                    jax.ShapeDtypeStruct((TILES,), jnp.int32),
                ],
                in_specs=[pl.BlockSpec(memory_space=pltpu.HBM)] * 3 + [whole] * m,
                out_specs=[whole, pl.BlockSpec(memory_space=pltpu.SMEM)],
                compiler_params=params,
                cost_estimate=pl.CostEstimate(
                    flops=MASK_COST, bytes_accessed=MASK_COST // 300, transcendentals=0
                ),
                name="mask",
            )(chip_beside, token, token_other, *ints_all)
        elif k > 2:
            if acc is None:
                acc = project([(0, True), (0, False)])
            acc = project([(k - 2, True)], acc, also=beside[k - 2])
            if k == 3:
                mine[k], acc, bias = tie((mine[k], acc, bias))
            else:
                mine[k], acc = tie((mine[k], acc))
        across[k], beside[k] = swap(mine[k], "x"), swap(mine[k], "y")
    for k in range(1, chips_z):
        if k < end:
            corner[k] = swap(beside[k], "x") if k % 2 else swap(across[k], "y")
    acc = project([(end - 1, True), (1, False)], acc, also=beside[end - 1], hint=HINT)
    beside[end], acc = tie((beside[end], acc))
    corner[end] = swap(beside[end], "x")

    where = jnp.concatenate([position[0], ints_other[1]]).astype(jnp.float32)
    half = HD // 2
    freq = np.exp(np.arange(half, dtype=np.float32) * np.float32(-2.0 * math.log(THETA) / HD))
    angle = where[:, None] * freq[None, :]
    cosine, sine = jnp.cos(angle), jnp.sin(angle)
    cosine = jnp.concatenate([cosine, cosine], axis=1)
    sine = jnp.concatenate([-sine, sine], axis=1)

    acc = project([(end, True)] + [(k, False) for k in range(2, end)], acc)
    kv_own, kv_other = project([(end, False)], acc, last=True)

    result = None
    for cross, kv in enumerate((kv_own, kv_other)):
        sources = [kv if d == 0 and not cross else along_ctx(kv, d, cross) for d in range(m)]

        def block(step, place, needs, cross=cross):
            return (0, lax.rem(place[0] + cross, 2) * 2 + step)

        earlier = [] if result is None else [result]
        result = pl.pallas_call(
            functools.partial(attend_kernel, m, count),
            out_shape=jax.ShapeDtypeStruct((count, KVH * G * HD), bf16),
            grid_spec=pltpu.PrefetchScalarGridSpec(
                num_scalar_prefetch=2,
                grid=(2,),
                in_specs=[pl.BlockSpec((count, G * HD), block)]
                + [whole] * (1 + m)
                + [pl.BlockSpec(memory_space=pl.ANY)] * len(earlier),
                out_specs=pl.BlockSpec((count, G * HD), block),
                scratch_shapes=[
                    pltpu.VMEM((m * count, HD), bf16),
                    pltpu.VMEM((m * count, HD), bf16),
                ],
            ),
            input_output_aliases={4 + m: 0} if earlier else {},
            compiler_params=params,
            cost_estimate=pl.CostEstimate(
                flops=2 * count * m * count * KVH * G * HD,
                bytes_accessed=2 * count * KVH * G * HD,
                transcendentals=count * m * count * KVH * G // 2,
            ),
            name="attend",
        )(core.astype(jnp.int32)[None], needs, queries[0], bias, *sources, *earlier)
    return result[None]


def solution(mesh):
    n, m = mesh.shape["fsdp"], mesh.shape["ctx"]
    sizes = (n // 4, 2, 2, m // 2, 2)
    fine = Mesh(mesh.devices.reshape(sizes), ("z", "y", "core", "ctx", "x"))
    fsdp, ctx = ("z", "y", "core"), ("ctx", "x")
    placed = (
        P(fsdp, ctx, None),
        P(fsdp, ctx, None),
        P(),
        P(),
        P(fsdp, None),
        P(fsdp, None),
        P(fsdp, ctx),
        P(fsdp, ctx),
    )
    return jax.shard_map(
        functools.partial(on_device, sizes),
        mesh=fine,
        in_specs=placed,
        out_specs=P(fsdp, ctx, None),
        check_vma=False,
    )
```

```python
import functools
import math

import jax
import jax.numpy as jnp
import numpy as np
from jax import lax
from jax.experimental import pallas as pl
from jax.experimental.pallas import tpu as pltpu
from jax.sharding import Mesh
from jax.sharding import PartitionSpec as P

KVH = 4
HD = 128
G = 8
EPS = 1e-06
THETA = 1000000.0
MASKED = -1e30
VMEM_LIMIT = 16 * 2**20
NORM_ROWS = 64
WIDE = 4
TILES = 2
HINT = 8
MASK_COST = 1 * 10**9


def norm_kernel(chunks, hidden, gain, out, token, held, sems):
    steps = held.shape[0] // NORM_ROWS
    copies = []
    for i in range(steps):
        at = pl.ds(i * NORM_ROWS, NORM_ROWS)
        copies.append(pltpu.make_async_copy(hidden.at[at], held.at[at], sems.at[i]))
        copies[-1].start()
    for i, copy in enumerate(copies):
        copy.wait()
        at = pl.ds(i * NORM_ROWS, NORM_ROWS)
        inputs = held[at, :].astype(jnp.float32)
        scale = lax.rsqrt(jnp.mean(inputs * inputs, axis=-1, keepdims=True) + EPS)
        normed = (inputs * scale * gain[...]).astype(jnp.bfloat16)
        rows = normed.shape[1] // chunks
        for j in range(chunks):
            out[j, at, :] = normed[:, j * rows : (j + 1) * rows]
    token[...] = jnp.zeros_like(token)


def project_kernel(groups, alone, first, last, count, place, own, other, *rest):
    chips_z = own.shape[0] // 2
    y, x, spot = place[0], place[1], place[2]
    rest = list(rest) if alone else list(rest[1:])
    weight, lhs, sems = rest[-3:]
    waits = []
    for g, (k, near) in enumerate(groups):
        i = lax.rem(spot - k + chips_z, chips_z)
        chunk = (i ^ (i >> 1)) * 2 + (y if near else 1 - y)
        pairs = [
            (own.at[chunk], lhs.at[g, pl.ds(0, count)]),
            (other.at[chunk], lhs.at[g, pl.ds(count, count)]),
        ]
        if k == 0:
            pairs.append((rest.pop(0), weight.at[g]))
        else:
            pairs.append((rest.pop(0), weight.at[g, x]))
            pairs.append((rest.pop(0), weight.at[g, 1 - x]))
        copies = [
            pltpu.make_async_copy(source, target, sems.at[g, i])
            for i, (source, target) in enumerate(pairs)
        ]
        for copy in copies:
            copy.start()
        waits.append(copies)
    earlier = None if first else rest.pop(0)
    terms = [None, None]
    for g, copies in enumerate(waits):
        for copy in copies:
            copy.wait()
        for half in range(2):
            part = jnp.dot(lhs[g], weight[g, half], preferred_element_type=jnp.float32)
            terms[half] = part if terms[half] is None else terms[half] + part
    for half in range(2):
        if not first:
            terms[half] += earlier[half]
        if not last:
            rest[0][half] = terms[half]
    if not last:
        return
    cosine, sine, gain = rest[:3]
    outs = rest[3:5]
    for head in range(2):
        columns = slice(head * HD, (head + 1) * HD)
        for part, out in enumerate(outs):
            at = slice(part * count, (part + 1) * count)
            raw = terms[0][at, columns]
            normk = raw * lax.rsqrt(jnp.mean(raw * raw, axis=-1, keepdims=True) + EPS) * gain[...]
            turned = normk * cosine[at, :] + pltpu.roll(normk, HD // 2, 1) * sine[at, :]
            out[:, 2 * head * HD : (2 * head + 1) * HD] = turned.astype(jnp.bfloat16)
            out[:, (2 * head + 1) * HD : (2 * head + 2) * HD] = terms[1][at, columns].astype(
                jnp.bfloat16
            )


def mask_kernel(*refs):
    pieces, (bias, needs) = refs[3:-2], refs[-2:]
    count = bias.shape[0]
    size = count // TILES
    seg_q, pos_q = (
        jnp.transpose(jnp.broadcast_to(pieces[0][i : i + 1, :], (count, count))) for i in range(2)
    )
    width = len(pieces) * size
    for tile in range(TILES):
        for i, piece in enumerate(pieces):
            at = slice(tile * size, (tile + 1) * size)
            allowed = (piece[:1, at] == seg_q[:, at]) & (piece[1:, at] <= pos_q[:, at])
            there = tile * width + i * size
            bias[:, there : there + size] = jnp.where(allowed, 0.0, MASKED)
    for tile in range(TILES - 1):
        rows = slice(tile * size, (tile + 1) * size)
        needs[tile] = (jnp.max(bias[rows, (tile + 1) * width :]) == 0.0).astype(jnp.int32)
    needs[TILES - 1] = 0


def attend_kernel(pieces, count, place, needs, queries, bias, *rest):
    sources, (out, keys, values) = rest[:pieces], rest[-3:]
    step = pl.program_id(0)
    tile_rows = count // TILES
    length = pieces * tile_rows

    for head in range(2):

        @pl.when(step == head)
        def _():
            left = 2 * head * HD
            for i, source in enumerate(sources):
                for tile in range(TILES):
                    here = slice(tile * tile_rows, (tile + 1) * tile_rows)
                    there = tile * length + i * tile_rows
                    keys[there : there + tile_rows, :] = source[here, left : left + HD]
                    values[there : there + tile_rows, :] = source[here, left + HD : left + 2 * HD]

    factor = math.log2(math.e) / math.sqrt(HD)

    def tile_body(tile, high):
        rows = slice(tile * tile_rows, (tile + 1) * tile_rows)
        k, v, b = keys[:high, :], values[:high, :], bias[rows, :high]

        def score(step):
            heads = range(step * WIDE, (step + 1) * WIDE)
            q = jnp.concatenate([queries[rows, g * HD : (g + 1) * HD] for g in heads], axis=0)
            return lax.dot_general(
                q, k, (((1,), (1,)), ((), ())), preferred_element_type=jnp.float32
            )

        ahead = score(0)
        for step in range(G // WIDE):
            scores = ahead.reshape(WIDE, tile_rows, high) + b[None]
            if step + 1 < G // WIDE:
                ahead = score(step + 1)
            top = jnp.max(scores, axis=-1, keepdims=True)
            weights = jnp.exp2((scores - top) * factor)
            total = jnp.sum(weights, axis=-1, keepdims=True)
            summed = jnp.dot(
                weights.astype(jnp.bfloat16).reshape(WIDE * tile_rows, high),
                v,
                preferred_element_type=jnp.float32,
            ).reshape(WIDE, tile_rows, HD)
            result = (summed * (1.0 / total)).astype(jnp.bfloat16)
            for i in range(WIDE):
                g = step * WIDE + i
                out[rows, g * HD : (g + 1) * HD] = result[i]

    for tile in range(TILES):
        for need, high in ((0, tile + 1), (1, TILES)):

            @pl.when(needs[tile] == need)
            def _():
                tile_body(tile, high * length)


def swap(array, axis):
    return lax.ppermute(array, axis, [(0, 1), (1, 0)])


def on_device(
    sizes, hidden, queries, norm_gain, key_gain, k_weight, v_weight, segment, position
):
    chips_z, groups = sizes[0], sizes[3]
    count, width = hidden.shape[1:]
    own_rows = k_weight.shape[0]
    rows = 2 * own_rows
    chunks = 2 * chips_z
    m = 2 * groups
    z, y = lax.axis_index("z"), lax.axis_index("y")
    core, x = lax.axis_index("core"), lax.axis_index("x")
    bf16 = jnp.bfloat16
    whole = pl.BlockSpec(memory_space=pltpu.VMEM)
    params = pltpu.CompilerParams(vmem_limit_bytes=VMEM_LIMIT)

    def along_ctx(array, d, cross=False):
        pairs = []
        for c in range(2):
            for i in range(m):
                pairs.append((c * m + i, (c ^ int(cross)) * m + (i + d) % m))
        return lax.ppermute(array, ("core", "ctx", "x"), pairs)

    def columns(which):
        at = which * 2 * HD
        return jnp.stack(
            [lax.dynamic_slice_in_dim(w, at, 2 * HD, 1) for w in (k_weight, v_weight)]
        )

    taken = swap(columns(1 - core), "core")
    kept = columns(core)
    chip = lax.dynamic_update_slice(
        jnp.zeros((2, rows, 2 * HD), bf16), kept, (0, core * own_rows, 0)
    )
    chip = lax.dynamic_update_slice(chip, taken, (0, (1 - core) * own_rows, 0))
    hidden, segment, position, chip = lax.optimization_barrier((hidden, segment, position, chip))

    def norm(array):
        return pl.pallas_call(
            functools.partial(norm_kernel, chunks),
            out_shape=[
                jax.ShapeDtypeStruct((chunks, count, rows), bf16),
                jax.ShapeDtypeStruct((8, 128), jnp.float32),
            ],
            in_specs=[pl.BlockSpec(memory_space=pltpu.HBM), whole],
            out_specs=[whole] * 2,
            scratch_shapes=[
                pltpu.VMEM((count, width), bf16),
                pltpu.SemaphoreType.DMA((count // NORM_ROWS,)),
            ],
            compiler_params=params,
            cost_estimate=pl.CostEstimate(
                flops=4 * count * width, bytes_accessed=4 * count * width, transcendentals=0
            ),
            name="norm",
        )(array[0], norm_gain[None])

    normed, token = norm(hidden)
    normed_other, token_other = norm(swap(hidden, "core"))
    ints = jnp.concatenate([segment, position])
    ints_other = swap(ints, "core")

    acc_shape = jax.ShapeDtypeStruct((2, 2 * count, 2 * HD), jnp.float32)
    kv_shape = jax.ShapeDtypeStruct((count, 4 * HD), bf16)

    def project(groups, acc=None, last=False, also=None, hint=1):
        arrays = [] if also is None else [also]
        for k, near in groups:
            if k == 0:
                arrays.append(chip if near else chip_beside)
            else:
                arrays += [mine[k], across[k]] if near else [beside[k], corner[k]]
        accs = [] if acc is None else [acc]
        outs = pl.pallas_call(
            functools.partial(project_kernel, groups, also is None, acc is None, last, count),
            out_shape=[kv_shape] * 2 if last else [acc_shape],
            in_specs=[pl.BlockSpec(memory_space=pltpu.SMEM)]
            + [pl.BlockSpec(memory_space=pltpu.HBM)] * (2 + len(arrays))
            + [whole] * (len(accs) + (3 if last else 0)),
            out_specs=[whole] * (2 if last else 1),
            scratch_shapes=[
                pltpu.VMEM((len(groups), 2, rows, 2 * HD), bf16),
                pltpu.VMEM((len(groups), 2 * count, rows), bf16),
                pltpu.SemaphoreType.DMA((len(groups), 4)),
            ],
            compiler_params=params,
            cost_estimate=pl.CostEstimate(
                flops=hint * 2 * 2 * count * rows * 4 * HD * len(groups),
                bytes_accessed=hint * 2 * rows * (4 * HD + 2 * count) * len(groups),
                transcendentals=0,
            ),
            name="project",
        )(
            place, normed, normed_other, *arrays, *accs,
            *((cosine, sine, key_gain[None]) if last else ()),
        )
        return outs if last else outs[0]

    order = [i ^ (i >> 1) for i in range(chips_z)]
    ring = [(order[i], order[(i + 1) % chips_z]) for i in range(chips_z)]
    spot = sum(jnp.where(z == order[i], i, 0) for i in range(chips_z))
    place = jnp.stack([y, x, spot]).astype(jnp.int32)
    tie = lax.optimization_barrier
    end = chips_z - 1
    mine = {0: lax.dynamic_index_in_dim(chip, x, 0, keepdims=False)}
    across, beside, corner = {}, {}, {}
    chip_beside = swap(chip, "y")
    acc = None
    for k in range(1, chips_z):
        mine[k] = lax.ppermute(mine[k - 1], "z", ring)
        if k == 1:
            tied = tie((mine[k], token, token_other, ints, ints_other))
            mine[k], token, token_other, ints, ints_other = tied
            ints_all = [ints] + [along_ctx(ints, d) for d in range(1, m)]
            bias, needs = pl.pallas_call(
                mask_kernel,
                out_shape=[
                    jax.ShapeDtypeStruct((count, m * count), jnp.float32),
                    jax.ShapeDtypeStruct((TILES,), jnp.int32),
                ],
                in_specs=[pl.BlockSpec(memory_space=pltpu.HBM)] * 3 + [whole] * m,
                out_specs=[whole, pl.BlockSpec(memory_space=pltpu.SMEM)],
                compiler_params=params,
                cost_estimate=pl.CostEstimate(
                    flops=MASK_COST, bytes_accessed=MASK_COST // 300, transcendentals=0
                ),
                name="mask",
            )(chip_beside, token, token_other, *ints_all)
        elif k > 2:
            if acc is None:
                acc = project([(0, True), (0, False)])
            acc = project([(k - 2, True)], acc, also=beside[k - 2])
            if k == 3:
                mine[k], acc, bias = tie((mine[k], acc, bias))
            else:
                mine[k], acc = tie((mine[k], acc))
        across[k], beside[k] = swap(mine[k], "x"), swap(mine[k], "y")
    for k in range(1, chips_z):
        if k < end:
            corner[k] = swap(beside[k], "x") if k % 2 else swap(across[k], "y")
    acc = project([(end - 1, True), (1, False)], acc, also=beside[end - 1], hint=HINT)
    beside[end], acc = tie((beside[end], acc))
    corner[end] = swap(beside[end], "x")

    where = jnp.concatenate([position[0], ints_other[1]]).astype(jnp.float32)
    half = HD // 2
    freq = np.exp(np.arange(half, dtype=np.float32) * np.float32(-2.0 * math.log(THETA) / HD))
    angle = where[:, None] * freq[None, :]
    cosine, sine = jnp.cos(angle), jnp.sin(angle)
    cosine = jnp.concatenate([cosine, cosine], axis=1)
    sine = jnp.concatenate([-sine, sine], axis=1)

    acc = project([(end, True)] + [(k, False) for k in range(2, end)], acc)
    kv_own, kv_other = project([(end, False)], acc, last=True)

    result = None
    for cross, kv in enumerate((kv_own, kv_other)):
        sources = [kv if d == 0 and not cross else along_ctx(kv, d, cross) for d in range(m)]

        def block(step, place, needs, cross=cross):
            return (0, lax.rem(place[0] + cross, 2) * 2 + step)

        earlier = [] if result is None else [result]
        result = pl.pallas_call(
            functools.partial(attend_kernel, m, count),
            out_shape=jax.ShapeDtypeStruct((count, KVH * G * HD), bf16),
            grid_spec=pltpu.PrefetchScalarGridSpec(
                num_scalar_prefetch=2,
                grid=(2,),
                in_specs=[pl.BlockSpec((count, G * HD), block)]
                + [whole] * (1 + m)
                + [pl.BlockSpec(memory_space=pl.ANY)] * len(earlier),
                out_specs=pl.BlockSpec((count, G * HD), block),
                scratch_shapes=[
                    pltpu.VMEM((m * count, HD), bf16),
                    pltpu.VMEM((m * count, HD), bf16),
                ],
            ),
            input_output_aliases={4 + m: 0} if earlier else {},
            compiler_params=params,
            cost_estimate=pl.CostEstimate(
                flops=2 * count * m * count * KVH * G * HD,
                bytes_accessed=2 * count * KVH * G * HD,
                transcendentals=count * m * count * KVH * G // 2,
            ),
            name="attend",
        )(core.astype(jnp.int32)[None], needs, queries[0], bias, *sources, *earlier)
    return result[None]


def solution(mesh):
    n, m = mesh.shape["fsdp"], mesh.shape["ctx"]
    sizes = (n // 4, 2, 2, m // 2, 2)
    fine = Mesh(mesh.devices.reshape(sizes), ("z", "y", "core", "ctx", "x"))
    fsdp, ctx = ("z", "y", "core"), ("ctx", "x")
    placed = (
        P(fsdp, ctx, None),
        P(fsdp, ctx, None),
        P(),
        P(),
        P(fsdp, None),
        P(fsdp, None),
        P(fsdp, ctx),
        P(fsdp, ctx),
    )
    return jax.shard_map(
        functools.partial(on_device, sizes),
        mesh=fine,
        in_specs=placed,
        out_specs=P(fsdp, ctx, None),
        check_vma=False,
    )
```

```python
import functools
import math

import jax
import jax.numpy as jnp
import numpy as np
from jax import lax
from jax.experimental import pallas as pl
from jax.experimental.pallas import tpu as pltpu
from jax.sharding import Mesh
from jax.sharding import PartitionSpec as P

KVH = 4
HD = 128
G = 8
EPS = 1e-06
THETA = 1000000.0
MASKED = -1e30
VMEM_LIMIT = 16 * 2**20
NORM_ROWS = 64
WIDE = 4
TILES = 2
HINT = 8
MASK_COST = 1 * 10**9


def norm_kernel(chunks, hidden, gain, out, token, held, sems):
    steps = held.shape[0] // NORM_ROWS
    copies = []
    for i in range(steps):
        at = pl.ds(i * NORM_ROWS, NORM_ROWS)
        copies.append(pltpu.make_async_copy(hidden.at[at], held.at[at], sems.at[i]))
        copies[-1].start()
    for i, copy in enumerate(copies):
        copy.wait()
        at = pl.ds(i * NORM_ROWS, NORM_ROWS)
        inputs = held[at, :].astype(jnp.float32)
        scale = lax.rsqrt(jnp.mean(inputs * inputs, axis=-1, keepdims=True) + EPS)
        normed = (inputs * scale * gain[...]).astype(jnp.bfloat16)
        rows = normed.shape[1] // chunks
        for j in range(chunks):
            out[j, at, :] = normed[:, j * rows : (j + 1) * rows]
    token[...] = jnp.zeros_like(token)


def project_kernel(groups, alone, first, last, count, place, own, other, *rest):
    chips_z = own.shape[0] // 2
    y, x, spot = place[0], place[1], place[2]
    rest = list(rest) if alone else list(rest[1:])
    weight, lhs, sems = rest[-3:]
    waits = []
    for g, (k, near) in enumerate(groups):
        i = lax.rem(spot - k + chips_z, chips_z)
        chunk = (i ^ (i >> 1)) * 2 + (y if near else 1 - y)
        pairs = [
            (own.at[chunk], lhs.at[g, pl.ds(0, count)]),
            (other.at[chunk], lhs.at[g, pl.ds(count, count)]),
        ]
        if k == 0:
            pairs.append((rest.pop(0), weight.at[g]))
        else:
            pairs.append((rest.pop(0), weight.at[g, x]))
            pairs.append((rest.pop(0), weight.at[g, 1 - x]))
        copies = [
            pltpu.make_async_copy(source, target, sems.at[g, i])
            for i, (source, target) in enumerate(pairs)
        ]
        for copy in copies:
            copy.start()
        waits.append(copies)
    earlier = None if first else rest.pop(0)
    terms = [None, None]
    for g, copies in enumerate(waits):
        for copy in copies:
            copy.wait()
        for half in range(2):
            part = jnp.dot(lhs[g], weight[g, half], preferred_element_type=jnp.float32)
            terms[half] = part if terms[half] is None else terms[half] + part
    for half in range(2):
        if not first:
            terms[half] += earlier[half]
        if not last:
            rest[0][half] = terms[half]
    if not last:
        return
    cosine, sine, gain = rest[:3]
    outs = rest[3:5]
    for head in range(2):
        columns = slice(head * HD, (head + 1) * HD)
        for part, out in enumerate(outs):
            at = slice(part * count, (part + 1) * count)
            raw = terms[0][at, columns]
            normk = raw * lax.rsqrt(jnp.mean(raw * raw, axis=-1, keepdims=True) + EPS) * gain[...]
            turned = normk * cosine[at, :] + pltpu.roll(normk, HD // 2, 1) * sine[at, :]
            out[:, 2 * head * HD : (2 * head + 1) * HD] = turned.astype(jnp.bfloat16)
            out[:, (2 * head + 1) * HD : (2 * head + 2) * HD] = terms[1][at, columns].astype(
                jnp.bfloat16
            )


def mask_kernel(*refs):
    pieces, (bias_own, bias_rest, needs) = refs[3:-3], refs[-3:]
    count = bias_own.shape[0]
    size = count // TILES
    seg_q, pos_q = (
        jnp.transpose(jnp.broadcast_to(pieces[0][i : i + 1, :], (count, count))) for i in range(2)
    )
    for bias, some in ((bias_own, pieces[:1]), (bias_rest, pieces[1:])):
        for tile in range(TILES):
            for i, piece in enumerate(some):
                at = slice(tile * size, (tile + 1) * size)
                allowed = (piece[:1, at] == seg_q[:, at]) & (piece[1:, at] <= pos_q[:, at])
                there = (tile * len(some) + i) * size
                bias[:, there : there + size] = jnp.where(allowed, 0.0, MASKED)
    for tile in range(TILES - 1):
        rows = slice(tile * size, (tile + 1) * size)
        later = [
            jnp.max(bias[rows, (tile + 1) * bias.shape[1] // TILES :])
            for bias in (bias_own, bias_rest)
        ]
        needs[tile] = (jnp.maximum(later[0], later[1]) == 0.0).astype(jnp.int32)
    needs[TILES - 1] = 0


def attend_kernel(pieces, count, merge, place, needs, queries, bias, *rest):
    sources, rest = rest[:pieces], rest[pieces:]
    keys, values = rest[-2:]
    if merge:
        top_in, total_in, summed_in, out = *rest[:3], rest[-3]
    else:
        top_out, total_out, summed_out = rest[:3]
    step = pl.program_id(0)
    tile_rows = count // TILES
    length = pieces * tile_rows

    for head in range(2):

        @pl.when(step == head)
        def _():
            left = 2 * head * HD
            for i, source in enumerate(sources):
                for tile in range(TILES):
                    here = slice(tile * tile_rows, (tile + 1) * tile_rows)
                    there = tile * length + i * tile_rows
                    keys[there : there + tile_rows, :] = source[here, left : left + HD]
                    values[there : there + tile_rows, :] = source[here, left + HD : left + 2 * HD]

    factor = math.log2(math.e) / math.sqrt(HD)

    def tile_body(tile, high):
        rows = slice(tile * tile_rows, (tile + 1) * tile_rows)
        k, v, b = keys[:high, :], values[:high, :], bias[rows, :high]

        def score(part):
            heads = range(part * WIDE, (part + 1) * WIDE)
            q = jnp.concatenate([queries[rows, g * HD : (g + 1) * HD] for g in heads], axis=0)
            return lax.dot_general(
                q, k, (((1,), (1,)), ((), ())), preferred_element_type=jnp.float32
            )

        ahead = score(0)
        for part in range(G // WIDE):
            heads = slice(part * WIDE, (part + 1) * WIDE)
            scores = ahead.reshape(WIDE, tile_rows, high) + b[None]
            if part + 1 < G // WIDE:
                ahead = score(part + 1)
            top = jnp.max(scores, axis=-1, keepdims=True)
            if merge:
                before = top_in[0, heads, rows, :]
                top = jnp.maximum(top, before)
            weights = jnp.exp2((scores - top) * factor)
            total = jnp.sum(weights, axis=-1, keepdims=True)
            summed = jnp.dot(
                weights.astype(jnp.bfloat16).reshape(WIDE * tile_rows, high),
                v,
                preferred_element_type=jnp.float32,
            ).reshape(WIDE, tile_rows, HD)
            if merge:
                shrink = jnp.exp2((before - top) * factor)
                over = 1.0 / (total + total_in[0, heads, rows, :] * shrink)
            else:
                top_out[0, heads, rows, :] = top
                total_out[0, heads, rows, :] = total
            for i in range(WIDE):
                g = part * WIDE + i
                at = slice(g * HD, (g + 1) * HD)
                if merge:
                    both = summed[i] + summed_in[rows, at] * shrink[i]
                    out[rows, at] = (both * over[i]).astype(jnp.bfloat16)
                else:
                    summed_out[rows, at] = summed[i]

    for tile in range(TILES):
        for need, high in ((0, tile + 1), (1, TILES)):

            @pl.when(needs[tile] == need)
            def _():
                tile_body(tile, high * length)


def swap(array, axis):
    return lax.ppermute(array, axis, [(0, 1), (1, 0)])


def on_device(
    sizes, hidden, queries, norm_gain, key_gain, k_weight, v_weight, segment, position
):
    chips_z, groups = sizes[0], sizes[3]
    count, width = hidden.shape[1:]
    own_rows = k_weight.shape[0]
    rows = 2 * own_rows
    chunks = 2 * chips_z
    m = 2 * groups
    z, y = lax.axis_index("z"), lax.axis_index("y")
    core, x = lax.axis_index("core"), lax.axis_index("x")
    bf16 = jnp.bfloat16
    whole = pl.BlockSpec(memory_space=pltpu.VMEM)
    params = pltpu.CompilerParams(vmem_limit_bytes=VMEM_LIMIT)

    def along_ctx(array, d, cross=False):
        pairs = []
        for c in range(2):
            for i in range(m):
                pairs.append((c * m + i, (c ^ int(cross)) * m + (i + d) % m))
        return lax.ppermute(array, ("core", "ctx", "x"), pairs)

    def columns(which):
        at = which * 2 * HD
        return jnp.stack(
            [lax.dynamic_slice_in_dim(w, at, 2 * HD, 1) for w in (k_weight, v_weight)]
        )

    taken = swap(columns(1 - core), "core")
    kept = columns(core)
    chip = lax.dynamic_update_slice(
        jnp.zeros((2, rows, 2 * HD), bf16), kept, (0, core * own_rows, 0)
    )
    chip = lax.dynamic_update_slice(chip, taken, (0, (1 - core) * own_rows, 0))
    hidden, segment, position, chip = lax.optimization_barrier((hidden, segment, position, chip))

    def norm(array):
        return pl.pallas_call(
            functools.partial(norm_kernel, chunks),
            out_shape=[
                jax.ShapeDtypeStruct((chunks, count, rows), bf16),
                jax.ShapeDtypeStruct((8, 128), jnp.float32),
            ],
            in_specs=[pl.BlockSpec(memory_space=pltpu.HBM), whole],
            out_specs=[whole] * 2,
            scratch_shapes=[
                pltpu.VMEM((count, width), bf16),
                pltpu.SemaphoreType.DMA((count // NORM_ROWS,)),
            ],
            compiler_params=params,
            cost_estimate=pl.CostEstimate(
                flops=4 * count * width, bytes_accessed=4 * count * width, transcendentals=0
            ),
            name="norm",
        )(array[0], norm_gain[None])

    normed, token = norm(hidden)
    normed_other, token_other = norm(swap(hidden, "core"))
    ints = jnp.concatenate([segment, position])
    ints_other = swap(ints, "core")

    acc_shape = jax.ShapeDtypeStruct((2, 2 * count, 2 * HD), jnp.float32)
    kv_shape = jax.ShapeDtypeStruct((count, 4 * HD), bf16)

    def project(groups, acc=None, last=False, also=None, hint=1):
        arrays = [] if also is None else [also]
        for k, near in groups:
            if k == 0:
                arrays.append(chip if near else chip_beside)
            else:
                arrays += [mine[k], across[k]] if near else [beside[k], corner[k]]
        accs = [] if acc is None else [acc]
        outs = pl.pallas_call(
            functools.partial(project_kernel, groups, also is None, acc is None, last, count),
            out_shape=[kv_shape] * 2 if last else [acc_shape],
            in_specs=[pl.BlockSpec(memory_space=pltpu.SMEM)]
            + [pl.BlockSpec(memory_space=pltpu.HBM)] * (2 + len(arrays))
            + [whole] * (len(accs) + (3 if last else 0)),
            out_specs=[whole] * (2 if last else 1),
            scratch_shapes=[
                pltpu.VMEM((len(groups), 2, rows, 2 * HD), bf16),
                pltpu.VMEM((len(groups), 2 * count, rows), bf16),
                pltpu.SemaphoreType.DMA((len(groups), 4)),
            ],
            compiler_params=params,
            cost_estimate=pl.CostEstimate(
                flops=hint * 2 * 2 * count * rows * 4 * HD * len(groups),
                bytes_accessed=hint * 2 * rows * (4 * HD + 2 * count) * len(groups),
                transcendentals=0,
            ),
            name="project",
        )(
            place, normed, normed_other, *arrays, *accs,
            *((cosine, sine, key_gain[None]) if last else ()),
        )
        return outs if last else outs[0]

    order = [i ^ (i >> 1) for i in range(chips_z)]
    ring = [(order[i], order[(i + 1) % chips_z]) for i in range(chips_z)]
    spot = sum(jnp.where(z == order[i], i, 0) for i in range(chips_z))
    place = jnp.stack([y, x, spot]).astype(jnp.int32)
    tie = lax.optimization_barrier
    end = chips_z - 1
    mine = {0: lax.dynamic_index_in_dim(chip, x, 0, keepdims=False)}
    across, beside, corner = {}, {}, {}
    chip_beside = swap(chip, "y")
    acc = None
    for k in range(1, chips_z):
        mine[k] = lax.ppermute(mine[k - 1], "z", ring)
        if k == 1:
            tied = tie((mine[k], token, token_other, ints, ints_other))
            mine[k], token, token_other, ints, ints_other = tied
            ints_all = [ints] + [along_ctx(ints, d) for d in range(1, m)]
            bias_own, bias_rest, needs = pl.pallas_call(
                mask_kernel,
                out_shape=[
                    jax.ShapeDtypeStruct((count, count), jnp.float32),
                    jax.ShapeDtypeStruct((count, (m - 1) * count), jnp.float32),
                    jax.ShapeDtypeStruct((TILES,), jnp.int32),
                ],
                in_specs=[pl.BlockSpec(memory_space=pltpu.HBM)] * 3 + [whole] * m,
                out_specs=[whole, whole, pl.BlockSpec(memory_space=pltpu.SMEM)],
                compiler_params=params,
                cost_estimate=pl.CostEstimate(
                    flops=MASK_COST, bytes_accessed=MASK_COST // 300, transcendentals=0
                ),
                name="mask",
            )(chip_beside, token, token_other, *ints_all)
        elif k > 2:
            if acc is None:
                acc = project([(0, True), (0, False)])
            acc = project([(k - 2, True)], acc, also=beside[k - 2])
            if k == 3:
                mine[k], acc, bias_own = tie((mine[k], acc, bias_own))
            else:
                mine[k], acc = tie((mine[k], acc))
        across[k], beside[k] = swap(mine[k], "x"), swap(mine[k], "y")
    for k in range(1, chips_z):
        if k < end:
            corner[k] = swap(beside[k], "x") if k % 2 else swap(across[k], "y")
    acc = project([(end - 1, True), (1, False)], acc, also=beside[end - 1], hint=HINT)
    beside[end], acc = tie((beside[end], acc))
    corner[end] = swap(beside[end], "x")

    where = jnp.concatenate([position[0], ints_other[1]]).astype(jnp.float32)
    half = HD // 2
    freq = np.exp(np.arange(half, dtype=np.float32) * np.float32(-2.0 * math.log(THETA) / HD))
    angle = where[:, None] * freq[None, :]
    cosine, sine = jnp.cos(angle), jnp.sin(angle)
    cosine = jnp.concatenate([cosine, cosine], axis=1)
    sine = jnp.concatenate([-sine, sine], axis=1)

    acc = project([(end, True)] + [(k, False) for k in range(2, end)], acc)
    kv_own, kv_other = project([(end, False)], acc, last=True)

    beyond = [[along_ctx(kv_own, d) for d in range(1, m)]]
    local = along_ctx(kv_other, 0, True)
    beyond.append([along_ctx(kv_other, d, True) for d in range(1, m)])
    stat_shape = jax.ShapeDtypeStruct((2, G, count, 1), jnp.float32)
    stat_spec = pl.BlockSpec((1, G, count, 1), lambda step, place, needs: (step, 0, 0, 0))
    half_shape = jax.ShapeDtypeStruct((count, 2 * G * HD), jnp.float32)
    half_spec = pl.BlockSpec((count, G * HD), lambda step, place, needs: (0, step))

    def attend(cross, sources, state=None, result=None):
        def block(step, place, needs):
            return (0, lax.rem(place[0] + cross, 2) * 2 + step)

        block_spec = pl.BlockSpec((count, G * HD), block)
        merge = state is not None
        extra = [] if result is None else [result]
        stats = [stat_spec, stat_spec, half_spec]
        outs = pl.pallas_call(
            functools.partial(attend_kernel, len(sources), count, merge),
            out_shape=[jax.ShapeDtypeStruct((count, KVH * G * HD), bf16)]
            if merge
            else [stat_shape, stat_shape, half_shape],
            grid_spec=pltpu.PrefetchScalarGridSpec(
                num_scalar_prefetch=2,
                grid=(2,),
                in_specs=[block_spec]
                + [whole] * (1 + len(sources))
                + (stats if merge else [])
                + [pl.BlockSpec(memory_space=pl.ANY)] * len(extra),
                out_specs=[block_spec] if merge else stats,
                scratch_shapes=[pltpu.VMEM((len(sources) * count, HD), bf16)] * 2,
            ),
            input_output_aliases={4 + len(sources) + 3: 0} if extra else {},
            compiler_params=params,
            cost_estimate=pl.CostEstimate(
                flops=2 * count * m * count * G * HD * 2,
                bytes_accessed=2 * count * KVH * G * HD,
                transcendentals=count * m * count * G,
            ),
            name="attend",
        )(
            core.astype(jnp.int32)[None], needs, queries[0],
            bias_rest if merge else bias_own, *sources, *(state or ()), *extra,
        )
        return outs[0] if merge else outs

    first = attend(0, [kv_own])
    second = attend(1, [local])
    result = attend(0, beyond[0], first)
    result = attend(1, beyond[1], second, result)
    return result[None]


def solution(mesh):
    n, m = mesh.shape["fsdp"], mesh.shape["ctx"]
    sizes = (n // 4, 2, 2, m // 2, 2)
    fine = Mesh(mesh.devices.reshape(sizes), ("z", "y", "core", "ctx", "x"))
    fsdp, ctx = ("z", "y", "core"), ("ctx", "x")
    placed = (
        P(fsdp, ctx, None),
        P(fsdp, ctx, None),
        P(),
        P(),
        P(fsdp, None),
        P(fsdp, None),
        P(fsdp, ctx),
        P(fsdp, ctx),
    )
    return jax.shard_map(
        functools.partial(on_device, sizes),
        mesh=fine,
        in_specs=placed,
        out_specs=P(fsdp, ctx, None),
        check_vma=False,
    )
```

```python
import functools
import math

import jax
import jax.numpy as jnp
import numpy as np
from jax import lax
from jax.experimental import pallas as pl
from jax.experimental.pallas import tpu as pltpu
from jax.sharding import Mesh
from jax.sharding import PartitionSpec as P

KVH = 4
HD = 128
G = 8
EPS = 1e-06
THETA = 1000000.0
MASKED = -1e30
VMEM_LIMIT = 16 * 2**20
NORM_ROWS = 64
WIDE = 4
TILES = 2
HINT = 8
MASK_COST = 1 * 10**9


def norm_kernel(chunks, hidden, gain, out, token, held, sems):
    steps = held.shape[0] // NORM_ROWS
    copies = []
    for i in range(steps):
        at = pl.ds(i * NORM_ROWS, NORM_ROWS)
        copies.append(pltpu.make_async_copy(hidden.at[at], held.at[at], sems.at[i]))
        copies[-1].start()
    for i, copy in enumerate(copies):
        copy.wait()
        at = pl.ds(i * NORM_ROWS, NORM_ROWS)
        inputs = held[at, :].astype(jnp.float32)
        scale = lax.rsqrt(jnp.mean(inputs * inputs, axis=-1, keepdims=True) + EPS)
        normed = (inputs * scale * gain[...]).astype(jnp.bfloat16)
        rows = normed.shape[1] // chunks
        for j in range(chunks):
            out[j, at, :] = normed[:, j * rows : (j + 1) * rows]
    token[...] = jnp.zeros_like(token)


def project_kernel(groups, alone, first, last, count, place, own, other, *rest):
    chips_z = own.shape[0] // 2
    y, x, spot = place[0], place[1], place[2]
    rest = list(rest) if alone else list(rest[1:])
    weight, lhs, sems = rest[-3:]
    waits = []
    for g, (k, near) in enumerate(groups):
        i = lax.rem(spot - k + chips_z, chips_z)
        chunk = (i ^ (i >> 1)) * 2 + (y if near else 1 - y)
        pairs = [
            (own.at[chunk], lhs.at[g, pl.ds(0, count)]),
            (other.at[chunk], lhs.at[g, pl.ds(count, count)]),
        ]
        if k == 0:
            pairs.append((rest.pop(0), weight.at[g]))
        else:
            pairs.append((rest.pop(0), weight.at[g, x]))
            pairs.append((rest.pop(0), weight.at[g, 1 - x]))
        copies = [
            pltpu.make_async_copy(source, target, sems.at[g, i])
            for i, (source, target) in enumerate(pairs)
        ]
        for copy in copies:
            copy.start()
        waits.append(copies)
    earlier = None if first else rest.pop(0)
    terms = [None, None]
    for g, copies in enumerate(waits):
        for copy in copies:
            copy.wait()
        for half in range(2):
            part = jnp.dot(lhs[g], weight[g, half], preferred_element_type=jnp.float32)
            terms[half] = part if terms[half] is None else terms[half] + part
    for half in range(2):
        if not first:
            terms[half] += earlier[half]
        if not last:
            rest[0][half] = terms[half]
    if not last:
        return
    cosine, sine, gain = rest[:3]
    outs = rest[3:5]
    for head in range(2):
        columns = slice(head * HD, (head + 1) * HD)
        for part, out in enumerate(outs):
            at = slice(part * count, (part + 1) * count)
            raw = terms[0][at, columns]
            normk = raw * lax.rsqrt(jnp.mean(raw * raw, axis=-1, keepdims=True) + EPS) * gain[...]
            turned = normk * cosine[at, :] + pltpu.roll(normk, HD // 2, 1) * sine[at, :]
            out[:, 2 * head * HD : (2 * head + 1) * HD] = turned.astype(jnp.bfloat16)
            out[:, (2 * head + 1) * HD : (2 * head + 2) * HD] = terms[1][at, columns].astype(
                jnp.bfloat16
            )


def mask_kernel(*refs):
    pieces, (bias_own, bias_rest, needs) = refs[3:-3], refs[-3:]
    count = bias_own.shape[0]
    size = count // TILES
    seg_q, pos_q = (
        jnp.transpose(jnp.broadcast_to(pieces[0][i : i + 1, :], (count, count))) for i in range(2)
    )
    for bias, some in ((bias_own, pieces[:1]), (bias_rest, pieces[1:])):
        for tile in range(TILES):
            for i, piece in enumerate(some):
                at = slice(tile * size, (tile + 1) * size)
                allowed = (piece[:1, at] == seg_q[:, at]) & (piece[1:, at] <= pos_q[:, at])
                there = (tile * len(some) + i) * size
                bias[:, there : there + size] = jnp.where(allowed, 0.0, MASKED)
    for tile in range(TILES - 1):
        rows = slice(tile * size, (tile + 1) * size)
        later = [
            jnp.max(bias[rows, (tile + 1) * bias.shape[1] // TILES :])
            for bias in (bias_own, bias_rest)
        ]
        needs[tile] = (jnp.maximum(later[0], later[1]) == 0.0).astype(jnp.int32)
    needs[TILES - 1] = 0


def attend_kernel(pieces, count, merge, place, needs, queries, bias, *rest):
    sources, rest = rest[:pieces], rest[pieces:]
    keys, values = rest[-2:]
    if merge:
        top_in, total_in, summed_in, out = *rest[:3], rest[-3]
    else:
        top_out, total_out, summed_out = rest[:3]
    step = pl.program_id(0)
    tile_rows = count // TILES
    length = pieces * tile_rows

    for head in range(2):

        @pl.when(step == head)
        def _():
            left = 2 * head * HD
            for i, source in enumerate(sources):
                for tile in range(TILES):
                    here = slice(tile * tile_rows, (tile + 1) * tile_rows)
                    there = tile * length + i * tile_rows
                    keys[there : there + tile_rows, :] = source[here, left : left + HD]
                    values[there : there + tile_rows, :] = source[here, left + HD : left + 2 * HD]

    factor = math.log2(math.e) / math.sqrt(HD)

    def tile_body(tile, high):
        rows = slice(tile * tile_rows, (tile + 1) * tile_rows)
        k, v, b = keys[:high, :], values[:high, :], bias[rows, :high]

        def score(part):
            heads = range(part * WIDE, (part + 1) * WIDE)
            q = jnp.concatenate([queries[rows, g * HD : (g + 1) * HD] for g in heads], axis=0)
            return lax.dot_general(
                q, k, (((1,), (1,)), ((), ())), preferred_element_type=jnp.float32
            )

        ahead = score(0)
        for part in range(G // WIDE):
            heads = slice(part * WIDE, (part + 1) * WIDE)
            scores = ahead.reshape(WIDE, tile_rows, high) + b[None]
            if part + 1 < G // WIDE:
                ahead = score(part + 1)
            wide = (WIDE, tile_rows, HD)
            top = jnp.broadcast_to(jnp.max(scores, axis=-1, keepdims=True), wide)
            if merge:
                before = top_in[0, heads, rows, :]
                top = jnp.maximum(top, before)
            tops = jnp.concatenate([top] * (high // HD), axis=-1)
            weights = jnp.exp2((scores - tops) * factor)
            total = jnp.broadcast_to(jnp.sum(weights, axis=-1, keepdims=True), wide)
            summed = jnp.dot(
                weights.astype(jnp.bfloat16).reshape(WIDE * tile_rows, high),
                v,
                preferred_element_type=jnp.float32,
            ).reshape(wide)
            if merge:
                shrink = jnp.exp2((before - top) * factor)
                over = 1.0 / (total + total_in[0, heads, rows, :] * shrink)
            else:
                top_out[0, heads, rows, :] = top
                total_out[0, heads, rows, :] = total
            for i in range(WIDE):
                g = part * WIDE + i
                at = slice(g * HD, (g + 1) * HD)
                if merge:
                    both = summed[i] + summed_in[rows, at] * shrink[i]
                    out[rows, at] = (both * over[i]).astype(jnp.bfloat16)
                else:
                    summed_out[rows, at] = summed[i]

    for tile in range(TILES):
        for need, high in ((0, tile + 1), (1, TILES)):

            @pl.when(needs[tile] == need)
            def _():
                tile_body(tile, high * length)


def swap(array, axis):
    return lax.ppermute(array, axis, [(0, 1), (1, 0)])


def on_device(
    sizes, hidden, queries, norm_gain, key_gain, k_weight, v_weight, segment, position
):
    chips_z, groups = sizes[0], sizes[3]
    count, width = hidden.shape[1:]
    own_rows = k_weight.shape[0]
    rows = 2 * own_rows
    chunks = 2 * chips_z
    m = 2 * groups
    z, y = lax.axis_index("z"), lax.axis_index("y")
    core, x = lax.axis_index("core"), lax.axis_index("x")
    bf16 = jnp.bfloat16
    whole = pl.BlockSpec(memory_space=pltpu.VMEM)
    params = pltpu.CompilerParams(vmem_limit_bytes=VMEM_LIMIT)

    def along_ctx(array, d, cross=False):
        pairs = []
        for c in range(2):
            for i in range(m):
                pairs.append((c * m + i, (c ^ int(cross)) * m + (i + d) % m))
        return lax.ppermute(array, ("core", "ctx", "x"), pairs)

    def columns(which):
        at = which * 2 * HD
        return jnp.stack(
            [lax.dynamic_slice_in_dim(w, at, 2 * HD, 1) for w in (k_weight, v_weight)]
        )

    taken = swap(columns(1 - core), "core")
    kept = columns(core)
    chip = lax.dynamic_update_slice(
        jnp.zeros((2, rows, 2 * HD), bf16), kept, (0, core * own_rows, 0)
    )
    chip = lax.dynamic_update_slice(chip, taken, (0, (1 - core) * own_rows, 0))
    hidden, segment, position, chip = lax.optimization_barrier((hidden, segment, position, chip))

    def norm(array):
        return pl.pallas_call(
            functools.partial(norm_kernel, chunks),
            out_shape=[
                jax.ShapeDtypeStruct((chunks, count, rows), bf16),
                jax.ShapeDtypeStruct((8, 128), jnp.float32),
            ],
            in_specs=[pl.BlockSpec(memory_space=pltpu.HBM), whole],
            out_specs=[whole] * 2,
            scratch_shapes=[
                pltpu.VMEM((count, width), bf16),
                pltpu.SemaphoreType.DMA((count // NORM_ROWS,)),
            ],
            compiler_params=params,
            cost_estimate=pl.CostEstimate(
                flops=4 * count * width, bytes_accessed=4 * count * width, transcendentals=0
            ),
            name="norm",
        )(array[0], norm_gain[None])

    normed, token = norm(hidden)
    normed_other, token_other = norm(swap(hidden, "core"))
    ints = jnp.concatenate([segment, position])
    ints_other = swap(ints, "core")

    acc_shape = jax.ShapeDtypeStruct((2, 2 * count, 2 * HD), jnp.float32)
    kv_shape = jax.ShapeDtypeStruct((count, 4 * HD), bf16)

    def project(groups, acc=None, last=False, also=None, hint=1):
        arrays = [] if also is None else [also]
        for k, near in groups:
            if k == 0:
                arrays.append(chip if near else chip_beside)
            else:
                arrays += [mine[k], across[k]] if near else [beside[k], corner[k]]
        accs = [] if acc is None else [acc]
        outs = pl.pallas_call(
            functools.partial(project_kernel, groups, also is None, acc is None, last, count),
            out_shape=[kv_shape] * 2 if last else [acc_shape],
            in_specs=[pl.BlockSpec(memory_space=pltpu.SMEM)]
            + [pl.BlockSpec(memory_space=pltpu.HBM)] * (2 + len(arrays))
            + [whole] * (len(accs) + (3 if last else 0)),
            out_specs=[whole] * (2 if last else 1),
            scratch_shapes=[
                pltpu.VMEM((len(groups), 2, rows, 2 * HD), bf16),
                pltpu.VMEM((len(groups), 2 * count, rows), bf16),
                pltpu.SemaphoreType.DMA((len(groups), 4)),
            ],
            compiler_params=params,
            cost_estimate=pl.CostEstimate(
                flops=hint * 2 * 2 * count * rows * 4 * HD * len(groups),
                bytes_accessed=hint * 2 * rows * (4 * HD + 2 * count) * len(groups),
                transcendentals=0,
            ),
            name="project",
        )(
            place, normed, normed_other, *arrays, *accs,
            *((cosine, sine, key_gain[None]) if last else ()),
        )
        return outs if last else outs[0]

    order = [i ^ (i >> 1) for i in range(chips_z)]
    ring = [(order[i], order[(i + 1) % chips_z]) for i in range(chips_z)]
    spot = sum(jnp.where(z == order[i], i, 0) for i in range(chips_z))
    place = jnp.stack([y, x, spot]).astype(jnp.int32)
    tie = lax.optimization_barrier
    end = chips_z - 1
    mine = {0: lax.dynamic_index_in_dim(chip, x, 0, keepdims=False)}
    across, beside, corner = {}, {}, {}
    chip_beside = swap(chip, "y")
    acc = None
    for k in range(1, chips_z):
        mine[k] = lax.ppermute(mine[k - 1], "z", ring)
        if k == 1:
            tied = tie((mine[k], token, token_other, ints, ints_other))
            mine[k], token, token_other, ints, ints_other = tied
            ints_all = [ints] + [along_ctx(ints, d) for d in range(1, m)]
            bias_own, bias_rest, needs = pl.pallas_call(
                mask_kernel,
                out_shape=[
                    jax.ShapeDtypeStruct((count, count), jnp.float32),
                    jax.ShapeDtypeStruct((count, (m - 1) * count), jnp.float32),
                    jax.ShapeDtypeStruct((TILES,), jnp.int32),
                ],
                in_specs=[pl.BlockSpec(memory_space=pltpu.HBM)] * 3 + [whole] * m,
                out_specs=[whole, whole, pl.BlockSpec(memory_space=pltpu.SMEM)],
                compiler_params=params,
                cost_estimate=pl.CostEstimate(
                    flops=MASK_COST, bytes_accessed=MASK_COST // 300, transcendentals=0
                ),
                name="mask",
            )(chip_beside, token, token_other, *ints_all)
        elif k > 2:
            if acc is None:
                acc = project([(0, True), (0, False)])
            acc = project([(k - 2, True)], acc, also=beside[k - 2])
            if k == 3:
                mine[k], acc, bias_own = tie((mine[k], acc, bias_own))
            else:
                mine[k], acc = tie((mine[k], acc))
        across[k], beside[k] = swap(mine[k], "x"), swap(mine[k], "y")
    for k in range(1, chips_z):
        if k < end:
            corner[k] = swap(beside[k], "x") if k % 2 else swap(across[k], "y")
    acc = project([(end - 1, True), (1, False)], acc, also=beside[end - 1], hint=HINT)
    beside[end], acc = tie((beside[end], acc))
    corner[end] = swap(beside[end], "x")

    where = jnp.concatenate([position[0], ints_other[1]]).astype(jnp.float32)
    half = HD // 2
    freq = np.exp(np.arange(half, dtype=np.float32) * np.float32(-2.0 * math.log(THETA) / HD))
    angle = where[:, None] * freq[None, :]
    cosine, sine = jnp.cos(angle), jnp.sin(angle)
    cosine = jnp.concatenate([cosine, cosine], axis=1)
    sine = jnp.concatenate([-sine, sine], axis=1)

    acc = project([(end, True)] + [(k, False) for k in range(2, end)], acc)
    kv_own, kv_other = project([(end, False)], acc, last=True)

    beyond = [[along_ctx(kv_own, d) for d in range(1, m)]]
    local = along_ctx(kv_other, 0, True)
    beyond.append([along_ctx(kv_other, d, True) for d in range(1, m)])
    stat_shape = jax.ShapeDtypeStruct((2, G, count, HD), jnp.float32)
    stat_spec = pl.BlockSpec((1, G, count, HD), lambda step, place, needs: (step, 0, 0, 0))
    half_shape = jax.ShapeDtypeStruct((count, 2 * G * HD), jnp.float32)
    half_spec = pl.BlockSpec((count, G * HD), lambda step, place, needs: (0, step))

    def attend(cross, sources, state=None, result=None):
        def block(step, place, needs):
            return (0, lax.rem(place[0] + cross, 2) * 2 + step)

        block_spec = pl.BlockSpec((count, G * HD), block)
        merge = state is not None
        extra = [] if result is None else [result]
        stats = [stat_spec, stat_spec, half_spec]
        outs = pl.pallas_call(
            functools.partial(attend_kernel, len(sources), count, merge),
            out_shape=[jax.ShapeDtypeStruct((count, KVH * G * HD), bf16)]
            if merge
            else [stat_shape, stat_shape, half_shape],
            grid_spec=pltpu.PrefetchScalarGridSpec(
                num_scalar_prefetch=2,
                grid=(2,),
                in_specs=[block_spec]
                + [whole] * (1 + len(sources))
                + (stats if merge else [])
                + [pl.BlockSpec(memory_space=pl.ANY)] * len(extra),
                out_specs=[block_spec] if merge else stats,
                scratch_shapes=[pltpu.VMEM((len(sources) * count, HD), bf16)] * 2,
            ),
            input_output_aliases={4 + len(sources) + 3: 0} if extra else {},
            compiler_params=params,
            cost_estimate=pl.CostEstimate(
                flops=2 * count * m * count * G * HD * 2,
                bytes_accessed=2 * count * KVH * G * HD,
                transcendentals=count * m * count * G,
            ),
            name="attend",
        )(
            core.astype(jnp.int32)[None], needs, queries[0],
            bias_rest if merge else bias_own, *sources, *(state or ()), *extra,
        )
        return outs[0] if merge else outs

    first = attend(0, [kv_own])
    second = attend(1, [local])
    result = attend(0, beyond[0], first)
    result = attend(1, beyond[1], second, result)
    return result[None]


def solution(mesh):
    n, m = mesh.shape["fsdp"], mesh.shape["ctx"]
    sizes = (n // 4, 2, 2, m // 2, 2)
    fine = Mesh(mesh.devices.reshape(sizes), ("z", "y", "core", "ctx", "x"))
    fsdp, ctx = ("z", "y", "core"), ("ctx", "x")
    placed = (
        P(fsdp, ctx, None),
        P(fsdp, ctx, None),
        P(),
        P(),
        P(fsdp, None),
        P(fsdp, None),
        P(fsdp, ctx),
        P(fsdp, ctx),
    )
    return jax.shard_map(
        functools.partial(on_device, sizes),
        mesh=fine,
        in_specs=placed,
        out_specs=P(fsdp, ctx, None),
        check_vma=False,
    )
```

```python
import functools
import math

import jax
import jax.numpy as jnp
import numpy as np
from jax import lax
from jax.experimental import pallas as pl
from jax.experimental.pallas import tpu as pltpu
from jax.sharding import Mesh
from jax.sharding import PartitionSpec as P

KVH = 4
HD = 128
G = 8
EPS = 1e-06
THETA = 1000000.0
MASKED = -1e30
VMEM_LIMIT = 16 * 2**20
NORM_ROWS = 64
WIDE = 4
TILES = 2
HINT = 8
MASK_COST = 1 * 10**9


def norm_kernel(chunks, hidden, gain, out, token, held, sems):
    steps = held.shape[0] // NORM_ROWS
    copies = []
    for i in range(steps):
        at = pl.ds(i * NORM_ROWS, NORM_ROWS)
        copies.append(pltpu.make_async_copy(hidden.at[at], held.at[at], sems.at[i]))
        copies[-1].start()
    for i, copy in enumerate(copies):
        copy.wait()
        at = pl.ds(i * NORM_ROWS, NORM_ROWS)
        inputs = held[at, :].astype(jnp.float32)
        scale = lax.rsqrt(jnp.mean(inputs * inputs, axis=-1, keepdims=True) + EPS)
        normed = (inputs * scale * gain[...]).astype(jnp.bfloat16)
        rows = normed.shape[1] // chunks
        for j in range(chunks):
            out[j, at, :] = normed[:, j * rows : (j + 1) * rows]
    token[...] = jnp.zeros_like(token)


def project_kernel(groups, alone, first, last, count, place, own, other, *rest):
    chips_z = own.shape[0] // 2
    y, x, spot = place[0], place[1], place[2]
    rest = list(rest) if alone else list(rest[1:])
    weight, lhs, sems = rest[-3:]
    waits = []
    for g, (k, near) in enumerate(groups):
        i = lax.rem(spot - k + chips_z, chips_z)
        chunk = (i ^ (i >> 1)) * 2 + (y if near else 1 - y)
        pairs = [
            (own.at[chunk], lhs.at[g, pl.ds(0, count)]),
            (other.at[chunk], lhs.at[g, pl.ds(count, count)]),
        ]
        if k == 0:
            pairs.append((rest.pop(0), weight.at[g]))
        else:
            pairs.append((rest.pop(0), weight.at[g, x]))
            pairs.append((rest.pop(0), weight.at[g, 1 - x]))
        copies = [
            pltpu.make_async_copy(source, target, sems.at[g, i])
            for i, (source, target) in enumerate(pairs)
        ]
        for copy in copies:
            copy.start()
        waits.append(copies)
    earlier = None if first else rest.pop(0)
    terms = [None, None]
    for g, copies in enumerate(waits):
        for copy in copies:
            copy.wait()
        for half in range(2):
            part = jnp.dot(lhs[g], weight[g, half], preferred_element_type=jnp.float32)
            terms[half] = part if terms[half] is None else terms[half] + part
    for half in range(2):
        if not first:
            terms[half] += earlier[half]
        if not last:
            rest[0][half] = terms[half]
    if not last:
        return
    cosine, sine, gain = rest[:3]
    outs = rest[3:5]
    for head in range(2):
        columns = slice(head * HD, (head + 1) * HD)
        for part, out in enumerate(outs):
            at = slice(part * count, (part + 1) * count)
            raw = terms[0][at, columns]
            normk = raw * lax.rsqrt(jnp.mean(raw * raw, axis=-1, keepdims=True) + EPS) * gain[...]
            turned = normk * cosine[at, :] + pltpu.roll(normk, HD // 2, 1) * sine[at, :]
            out[:, 2 * head * HD : (2 * head + 1) * HD] = turned.astype(jnp.bfloat16)
            out[:, (2 * head + 1) * HD : (2 * head + 2) * HD] = terms[1][at, columns].astype(
                jnp.bfloat16
            )


def mask_kernel(*refs):
    pieces, (bias, needs) = refs[3:-2], refs[-2:]
    count = bias.shape[0]
    size = count // TILES
    seg_q, pos_q = (
        jnp.transpose(jnp.broadcast_to(pieces[0][i : i + 1, :], (count, count))) for i in range(2)
    )
    width = len(pieces) * size
    for tile in range(TILES):
        for i, piece in enumerate(pieces):
            at = slice(tile * size, (tile + 1) * size)
            allowed = (piece[:1, at] == seg_q[:, at]) & (piece[1:, at] <= pos_q[:, at])
            there = tile * width + i * size
            bias[:, there : there + size] = jnp.where(allowed, 0.0, MASKED)
    for tile in range(TILES - 1):
        rows = slice(tile * size, (tile + 1) * size)
        needs[tile] = (jnp.max(bias[rows, (tile + 1) * width :]) == 0.0).astype(jnp.int32)
    needs[TILES - 1] = 0


def attend_kernel(pieces, count, cross, place, needs, queries, bias, *rest):
    sources, (out, keys, values) = rest[:pieces], rest[-3:]
    step = pl.program_id(0)
    base = (lax.rem(place[0] + cross, 2) * 2 + step) * G * HD
    tile_rows = count // TILES
    length = pieces * tile_rows

    for head in range(2):

        @pl.when(step == head)
        def _():
            left = 2 * head * HD
            for i, source in enumerate(sources):
                for tile in range(TILES):
                    here = slice(tile * tile_rows, (tile + 1) * tile_rows)
                    there = tile * length + i * tile_rows
                    keys[there : there + tile_rows, :] = source[here, left : left + HD]
                    values[there : there + tile_rows, :] = source[here, left + HD : left + 2 * HD]

    factor = math.log2(math.e) / math.sqrt(HD)

    def tile_body(tile, high):
        rows = slice(tile * tile_rows, (tile + 1) * tile_rows)
        k, v, b = keys[:high, :], values[:high, :], bias[rows, :high]

        def score(part):
            columns = [
                pl.ds(pl.multiple_of(base + g * HD, HD), HD)
                for g in range(part * WIDE, (part + 1) * WIDE)
            ]
            q = jnp.concatenate([queries[rows, at] for at in columns], axis=0)
            return lax.dot_general(
                q, k, (((1,), (1,)), ((), ())), preferred_element_type=jnp.float32
            )

        ahead = score(0)
        for step in range(G // WIDE):
            scores = ahead.reshape(WIDE, tile_rows, high) + b[None]
            if step + 1 < G // WIDE:
                ahead = score(step + 1)
            top = jnp.max(scores, axis=-1, keepdims=True)
            weights = jnp.exp2((scores - top) * factor)
            total = jnp.sum(weights, axis=-1, keepdims=True)
            summed = jnp.dot(
                weights.astype(jnp.bfloat16).reshape(WIDE * tile_rows, high),
                v,
                preferred_element_type=jnp.float32,
            ).reshape(WIDE, tile_rows, HD)
            result = (summed * (1.0 / total)).astype(jnp.bfloat16)
            for i in range(WIDE):
                g = step * WIDE + i
                out[rows, g * HD : (g + 1) * HD] = result[i]

    for tile in range(TILES):
        for need, high in ((0, tile + 1), (1, TILES)):

            @pl.when(needs[tile] == need)
            def _():
                tile_body(tile, high * length)


def swap(array, axis):
    return lax.ppermute(array, axis, [(0, 1), (1, 0)])


def on_device(
    sizes, hidden, queries, norm_gain, key_gain, k_weight, v_weight, segment, position
):
    chips_z, groups = sizes[0], sizes[3]
    count, width = hidden.shape[1:]
    own_rows = k_weight.shape[0]
    rows = 2 * own_rows
    chunks = 2 * chips_z
    m = 2 * groups
    z, y = lax.axis_index("z"), lax.axis_index("y")
    core, x = lax.axis_index("core"), lax.axis_index("x")
    bf16 = jnp.bfloat16
    whole = pl.BlockSpec(memory_space=pltpu.VMEM)
    params = pltpu.CompilerParams(vmem_limit_bytes=VMEM_LIMIT)

    def along_ctx(array, d, cross=False):
        pairs = []
        for c in range(2):
            for i in range(m):
                pairs.append((c * m + i, (c ^ int(cross)) * m + (i + d) % m))
        return lax.ppermute(array, ("core", "ctx", "x"), pairs)

    def columns(which):
        at = which * 2 * HD
        return jnp.stack(
            [lax.dynamic_slice_in_dim(w, at, 2 * HD, 1) for w in (k_weight, v_weight)]
        )

    taken = swap(columns(1 - core), "core")
    kept = columns(core)
    chip = lax.dynamic_update_slice(
        jnp.zeros((2, rows, 2 * HD), bf16), kept, (0, core * own_rows, 0)
    )
    chip = lax.dynamic_update_slice(chip, taken, (0, (1 - core) * own_rows, 0))
    hidden, segment, position, chip = lax.optimization_barrier((hidden, segment, position, chip))

    def norm(array):
        return pl.pallas_call(
            functools.partial(norm_kernel, chunks),
            out_shape=[
                jax.ShapeDtypeStruct((chunks, count, rows), bf16),
                jax.ShapeDtypeStruct((8, 128), jnp.float32),
            ],
            in_specs=[pl.BlockSpec(memory_space=pltpu.HBM), whole],
            out_specs=[whole] * 2,
            scratch_shapes=[
                pltpu.VMEM((count, width), bf16),
                pltpu.SemaphoreType.DMA((count // NORM_ROWS,)),
            ],
            compiler_params=params,
            cost_estimate=pl.CostEstimate(
                flops=4 * count * width, bytes_accessed=4 * count * width, transcendentals=0
            ),
            name="norm",
        )(array[0], norm_gain[None])

    normed, token = norm(hidden)
    normed_other, token_other = norm(swap(hidden, "core"))
    ints = jnp.concatenate([segment, position])
    ints_other = swap(ints, "core")

    acc_shape = jax.ShapeDtypeStruct((2, 2 * count, 2 * HD), jnp.float32)
    kv_shape = jax.ShapeDtypeStruct((count, 4 * HD), bf16)

    def project(groups, acc=None, last=False, also=None, hint=1):
        arrays = [] if also is None else [also]
        for k, near in groups:
            if k == 0:
                arrays.append(chip if near else chip_beside)
            else:
                arrays += [mine[k], across[k]] if near else [beside[k], corner[k]]
        accs = [] if acc is None else [acc]
        outs = pl.pallas_call(
            functools.partial(project_kernel, groups, also is None, acc is None, last, count),
            out_shape=[kv_shape] * 2 if last else [acc_shape],
            in_specs=[pl.BlockSpec(memory_space=pltpu.SMEM)]
            + [pl.BlockSpec(memory_space=pltpu.HBM)] * (2 + len(arrays))
            + [whole] * (len(accs) + (3 if last else 0)),
            out_specs=[whole] * (2 if last else 1),
            scratch_shapes=[
                pltpu.VMEM((len(groups), 2, rows, 2 * HD), bf16),
                pltpu.VMEM((len(groups), 2 * count, rows), bf16),
                pltpu.SemaphoreType.DMA((len(groups), 4)),
            ],
            compiler_params=params,
            cost_estimate=pl.CostEstimate(
                flops=hint * 2 * 2 * count * rows * 4 * HD * len(groups),
                bytes_accessed=hint * 2 * rows * (4 * HD + 2 * count) * len(groups),
                transcendentals=0,
            ),
            name="project",
        )(
            place, normed, normed_other, *arrays, *accs,
            *((cosine, sine, key_gain[None]) if last else ()),
        )
        return outs if last else outs[0]

    order = [i ^ (i >> 1) for i in range(chips_z)]
    ring = [(order[i], order[(i + 1) % chips_z]) for i in range(chips_z)]
    spot = sum(jnp.where(z == order[i], i, 0) for i in range(chips_z))
    place = jnp.stack([y, x, spot]).astype(jnp.int32)
    tie = lax.optimization_barrier
    end = chips_z - 1
    mine = {0: lax.dynamic_index_in_dim(chip, x, 0, keepdims=False)}
    across, beside, corner = {}, {}, {}
    chip_beside = swap(chip, "y")
    acc = None
    for k in range(1, chips_z):
        mine[k] = lax.ppermute(mine[k - 1], "z", ring)
        if k == 1:
            tied = tie((mine[k], token, token_other, ints, ints_other))
            mine[k], token, token_other, ints, ints_other = tied
            ints_all = [ints] + [along_ctx(ints, d) for d in range(1, m)]
            bias, needs = pl.pallas_call(
                mask_kernel,
                out_shape=[
                    jax.ShapeDtypeStruct((count, m * count), jnp.float32),
                    jax.ShapeDtypeStruct((TILES,), jnp.int32),
                ],
                in_specs=[pl.BlockSpec(memory_space=pltpu.HBM)] * 3 + [whole] * m,
                out_specs=[whole, pl.BlockSpec(memory_space=pltpu.SMEM)],
                compiler_params=params,
                cost_estimate=pl.CostEstimate(
                    flops=MASK_COST, bytes_accessed=MASK_COST // 300, transcendentals=0
                ),
                name="mask",
            )(chip_beside, token, token_other, *ints_all)
        elif k > 2:
            if acc is None:
                acc = project([(0, True), (0, False)])
            acc = project([(k - 2, True)], acc, also=beside[k - 2])
            if k == 3:
                mine[k], acc, bias = tie((mine[k], acc, bias))
            else:
                mine[k], acc = tie((mine[k], acc))
        across[k], beside[k] = swap(mine[k], "x"), swap(mine[k], "y")
    for k in range(1, chips_z):
        if k < end:
            corner[k] = swap(beside[k], "x") if k % 2 else swap(across[k], "y")
    acc = project([(end - 1, True), (1, False)], acc, also=beside[end - 1], hint=HINT)
    beside[end], acc = tie((beside[end], acc))
    corner[end] = swap(beside[end], "x")

    where = jnp.concatenate([position[0], ints_other[1]]).astype(jnp.float32)
    half = HD // 2
    freq = np.exp(np.arange(half, dtype=np.float32) * np.float32(-2.0 * math.log(THETA) / HD))
    angle = where[:, None] * freq[None, :]
    cosine, sine = jnp.cos(angle), jnp.sin(angle)
    cosine = jnp.concatenate([cosine, cosine], axis=1)
    sine = jnp.concatenate([-sine, sine], axis=1)

    acc = project([(end, True)] + [(k, False) for k in range(2, end)], acc)
    kv_own, kv_other = project([(end, False)], acc, last=True)

    result = None
    for cross, kv in enumerate((kv_own, kv_other)):
        sources = [kv if d == 0 and not cross else along_ctx(kv, d, cross) for d in range(m)]

        def block(step, place, needs, cross=cross):
            return (0, lax.rem(place[0] + cross, 2) * 2 + step)

        earlier = [] if result is None else [result]
        result = pl.pallas_call(
            functools.partial(attend_kernel, m, count, cross),
            out_shape=jax.ShapeDtypeStruct((count, KVH * G * HD), bf16),
            grid_spec=pltpu.PrefetchScalarGridSpec(
                num_scalar_prefetch=2,
                grid=(2,),
                in_specs=[whole] * (2 + m)
                + [pl.BlockSpec(memory_space=pl.ANY)] * len(earlier),
                out_specs=pl.BlockSpec((count, G * HD), block),
                scratch_shapes=[
                    pltpu.VMEM((m * count, HD), bf16),
                    pltpu.VMEM((m * count, HD), bf16),
                ],
            ),
            input_output_aliases={4 + m: 0} if earlier else {},
            compiler_params=params,
            cost_estimate=pl.CostEstimate(
                flops=2 * count * m * count * KVH * G * HD,
                bytes_accessed=2 * count * KVH * G * HD,
                transcendentals=count * m * count * KVH * G // 2,
            ),
            name="attend",
        )(core.astype(jnp.int32)[None], needs, queries[0], bias, *sources, *earlier)
    return result[None]


def solution(mesh):
    n, m = mesh.shape["fsdp"], mesh.shape["ctx"]
    sizes = (n // 4, 2, 2, m // 2, 2)
    fine = Mesh(mesh.devices.reshape(sizes), ("z", "y", "core", "ctx", "x"))
    fsdp, ctx = ("z", "y", "core"), ("ctx", "x")
    placed = (
        P(fsdp, ctx, None),
        P(fsdp, ctx, None),
        P(),
        P(),
        P(fsdp, None),
        P(fsdp, None),
        P(fsdp, ctx),
        P(fsdp, ctx),
    )
    return jax.shard_map(
        functools.partial(on_device, sizes),
        mesh=fine,
        in_specs=placed,
        out_specs=P(fsdp, ctx, None),
        check_vma=False,
    )
```

```python
import functools
import math

import jax
import jax.numpy as jnp
import numpy as np
from jax import lax
from jax.experimental import pallas as pl
from jax.experimental.pallas import tpu as pltpu
from jax.sharding import Mesh
from jax.sharding import PartitionSpec as P

KVH = 4
HD = 128
G = 8
EPS = 1e-06
THETA = 1000000.0
MASKED = -1e30
VMEM_LIMIT = 16 * 2**20
NORM_ROWS = 64
WIDE = 4
TILES = 2
HINT = 8
MASK_COST = 1 * 10**9


def norm_kernel(chunks, hidden, gain, out, token, held, sems):
    steps = held.shape[0] // NORM_ROWS
    copies = []
    for i in range(steps):
        at = pl.ds(i * NORM_ROWS, NORM_ROWS)
        copies.append(pltpu.make_async_copy(hidden.at[at], held.at[at], sems.at[i]))
        copies[-1].start()
    for i, copy in enumerate(copies):
        copy.wait()
        at = pl.ds(i * NORM_ROWS, NORM_ROWS)
        inputs = held[at, :].astype(jnp.float32)
        scale = lax.rsqrt(jnp.mean(inputs * inputs, axis=-1, keepdims=True) + EPS)
        normed = (inputs * scale * gain[...]).astype(jnp.bfloat16)
        rows = normed.shape[1] // chunks
        for j in range(chunks):
            out[j, at, :] = normed[:, j * rows : (j + 1) * rows]
    token[...] = jnp.zeros_like(token)


def project_kernel(groups, alone, first, last, count, place, own, other, *rest):
    chips_z = own.shape[0] // 2
    y, x, spot = place[0], place[1], place[2]
    rest = list(rest) if alone else list(rest[1:])
    weight, lhs, sems = rest[-3:]
    waits = []
    for g, (k, near) in enumerate(groups):
        i = lax.rem(spot - k + chips_z, chips_z)
        chunk = (i ^ (i >> 1)) * 2 + (y if near else 1 - y)
        pairs = [
            (own.at[chunk], lhs.at[g, pl.ds(0, count)]),
            (other.at[chunk], lhs.at[g, pl.ds(count, count)]),
        ]
        if k == 0:
            pairs.append((rest.pop(0), weight.at[g]))
        else:
            pairs.append((rest.pop(0), weight.at[g, x]))
            pairs.append((rest.pop(0), weight.at[g, 1 - x]))
        copies = [
            pltpu.make_async_copy(source, target, sems.at[g, i])
            for i, (source, target) in enumerate(pairs)
        ]
        for copy in copies:
            copy.start()
        waits.append(copies)
    earlier = None if first else rest.pop(0)
    terms = [None, None]
    for g, copies in enumerate(waits):
        for copy in copies:
            copy.wait()
        for half in range(2):
            part = jnp.dot(lhs[g], weight[g, half], preferred_element_type=jnp.float32)
            terms[half] = part if terms[half] is None else terms[half] + part
    for half in range(2):
        if not first:
            terms[half] += earlier[half]
        if not last:
            rest[0][half] = terms[half]
    if not last:
        return
    cosine, sine, gain = rest[:3]
    outs = rest[3:5]
    for head in range(2):
        columns = slice(head * HD, (head + 1) * HD)
        for part, out in enumerate(outs):
            at = slice(part * count, (part + 1) * count)
            raw = terms[0][at, columns]
            normk = raw * lax.rsqrt(jnp.mean(raw * raw, axis=-1, keepdims=True) + EPS) * gain[...]
            turned = normk * cosine[at, :] + pltpu.roll(normk, HD // 2, 1) * sine[at, :]
            out[:, 2 * head * HD : (2 * head + 1) * HD] = turned.astype(jnp.bfloat16)
            out[:, (2 * head + 1) * HD : (2 * head + 2) * HD] = terms[1][at, columns].astype(
                jnp.bfloat16
            )


def mask_kernel(*refs):
    pieces, (bias, needs) = refs[3:-2], refs[-2:]
    count = bias.shape[0]
    size = count // TILES
    seg_q, pos_q = (
        jnp.transpose(jnp.broadcast_to(pieces[0][i : i + 1, :], (count, count))) for i in range(2)
    )
    width = len(pieces) * size
    for tile in range(TILES):
        for i, piece in enumerate(pieces):
            at = slice(tile * size, (tile + 1) * size)
            allowed = (piece[:1, at] == seg_q[:, at]) & (piece[1:, at] <= pos_q[:, at])
            there = tile * width + i * size
            bias[:, there : there + size] = jnp.where(allowed, 0.0, MASKED)
    for tile in range(TILES - 1):
        rows = slice(tile * size, (tile + 1) * size)
        needs[tile] = (jnp.max(bias[rows, (tile + 1) * width :]) == 0.0).astype(jnp.int32)
    needs[TILES - 1] = 0


def attend_kernel(pieces, count, cross, place, needs, queries, bias, *rest):
    sources, (out, keys, values) = rest[:pieces], rest[-3:]
    step = pl.program_id(0)
    base = (lax.rem(place[0] + cross, 2) * 2 + step) * G * HD
    tile_rows = count // TILES
    length = pieces * tile_rows

    for head in range(2):

        @pl.when(step == head)
        def _():
            left = 2 * head * HD
            for i, source in enumerate(sources):
                for tile in range(TILES):
                    here = slice(tile * tile_rows, (tile + 1) * tile_rows)
                    there = tile * length + i * tile_rows
                    keys[there : there + tile_rows, :] = source[here, left : left + HD]
                    values[there : there + tile_rows, :] = source[here, left + HD : left + 2 * HD]

    factor = math.log2(math.e) / math.sqrt(HD)

    def tile_body(tile, high):
        rows = slice(tile * tile_rows, (tile + 1) * tile_rows)
        k, v, b = keys[:high, :], values[:high, :], bias[rows, :high]

        def score(part):
            columns = [
                pl.ds(pl.multiple_of(base + g * HD, HD), HD)
                for g in range(part * WIDE, (part + 1) * WIDE)
            ]
            q = jnp.concatenate([queries[rows, at] for at in columns], axis=0)
            return lax.dot_general(
                q, k, (((1,), (1,)), ((), ())), preferred_element_type=jnp.float32
            )

        ahead = score(0)
        for step in range(G // WIDE):
            scores = ahead.reshape(WIDE, tile_rows, high) + b[None]
            if step + 1 < G // WIDE:
                ahead = score(step + 1)
            top = jnp.max(scores, axis=-1, keepdims=True)
            weights = jnp.exp2((scores - top) * factor)
            total = jnp.sum(weights, axis=-1, keepdims=True)
            summed = jnp.dot(
                weights.astype(jnp.bfloat16).reshape(WIDE * tile_rows, high),
                v,
                preferred_element_type=jnp.float32,
            ).reshape(WIDE, tile_rows, HD)
            result = (summed * (1.0 / total)).astype(jnp.bfloat16)
            for i in range(WIDE):
                g = step * WIDE + i
                out[rows, g * HD : (g + 1) * HD] = result[i]

    for tile in range(TILES):
        for need, high in ((0, tile + 1), (1, TILES)):

            @pl.when(needs[tile] == need)
            def _():
                tile_body(tile, high * length)


def swap(array, axis):
    return lax.ppermute(array, axis, [(0, 1), (1, 0)])


def on_device(
    sizes, hidden, queries, norm_gain, key_gain, k_weight, v_weight, segment, position
):
    chips_z, groups = sizes[0], sizes[3]
    count, width = hidden.shape[1:]
    own_rows = k_weight.shape[0]
    rows = 2 * own_rows
    chunks = 2 * chips_z
    m = 2 * groups
    z, y = lax.axis_index("z"), lax.axis_index("y")
    core, x = lax.axis_index("core"), lax.axis_index("x")
    bf16 = jnp.bfloat16
    whole = pl.BlockSpec(memory_space=pltpu.VMEM)
    params = pltpu.CompilerParams(vmem_limit_bytes=VMEM_LIMIT)

    def along_ctx(array, d, cross=False):
        pairs = []
        for c in range(2):
            for i in range(m):
                pairs.append((c * m + i, (c ^ int(cross)) * m + (i + d) % m))
        return lax.ppermute(array, ("core", "ctx", "x"), pairs)

    def columns(which):
        at = which * 2 * HD
        return jnp.stack(
            [lax.dynamic_slice_in_dim(w, at, 2 * HD, 1) for w in (k_weight, v_weight)]
        )

    taken = swap(columns(1 - core), "core")
    kept = columns(core)
    chip = lax.dynamic_update_slice(
        jnp.zeros((2, rows, 2 * HD), bf16), kept, (0, core * own_rows, 0)
    )
    chip = lax.dynamic_update_slice(chip, taken, (0, (1 - core) * own_rows, 0))
    hidden, segment, position, chip = lax.optimization_barrier((hidden, segment, position, chip))

    def norm(array):
        return pl.pallas_call(
            functools.partial(norm_kernel, chunks),
            out_shape=[
                jax.ShapeDtypeStruct((chunks, count, rows), bf16),
                jax.ShapeDtypeStruct((8, 128), jnp.float32),
            ],
            in_specs=[pl.BlockSpec(memory_space=pltpu.HBM), whole],
            out_specs=[whole] * 2,
            scratch_shapes=[
                pltpu.VMEM((count, width), bf16),
                pltpu.SemaphoreType.DMA((count // NORM_ROWS,)),
            ],
            compiler_params=params,
            cost_estimate=pl.CostEstimate(
                flops=4 * count * width, bytes_accessed=4 * count * width, transcendentals=0
            ),
            name="norm",
        )(array[0], norm_gain[None])

    normed, token = norm(hidden)
    normed_other, token_other = norm(swap(hidden, "core"))
    ints = jnp.concatenate([segment, position])
    ints_other = swap(ints, "core")

    acc_shape = jax.ShapeDtypeStruct((2, 2 * count, 2 * HD), jnp.float32)
    kv_shape = jax.ShapeDtypeStruct((count, 4 * HD), bf16)

    def project(groups, acc=None, last=False, also=None, hint=1):
        arrays = [] if also is None else [also]
        for k, near in groups:
            if k == 0:
                arrays.append(chip if near else chip_beside)
            else:
                arrays += [mine[k], across[k]] if near else [beside[k], corner[k]]
        accs = [] if acc is None else [acc]
        outs = pl.pallas_call(
            functools.partial(project_kernel, groups, also is None, acc is None, last, count),
            out_shape=[kv_shape] * 2 if last else [acc_shape],
            in_specs=[pl.BlockSpec(memory_space=pltpu.SMEM)]
            + [pl.BlockSpec(memory_space=pltpu.HBM)] * (2 + len(arrays))
            + [whole] * (len(accs) + (3 if last else 0)),
            out_specs=[whole] * (2 if last else 1),
            scratch_shapes=[
                pltpu.VMEM((len(groups), 2, rows, 2 * HD), bf16),
                pltpu.VMEM((len(groups), 2 * count, rows), bf16),
                pltpu.SemaphoreType.DMA((len(groups), 4)),
            ],
            compiler_params=params,
            cost_estimate=pl.CostEstimate(
                flops=hint * 2 * 2 * count * rows * 4 * HD * len(groups),
                bytes_accessed=hint * 2 * rows * (4 * HD + 2 * count) * len(groups),
                transcendentals=0,
            ),
            name="project",
        )(
            place, normed, normed_other, *arrays, *accs,
            *((cosine, sine, key_gain[None]) if last else ()),
        )
        return outs if last else outs[0]

    order = [i ^ (i >> 1) for i in range(chips_z)]
    ring = [(order[i], order[(i + 1) % chips_z]) for i in range(chips_z)]
    spot = sum(jnp.where(z == order[i], i, 0) for i in range(chips_z))
    place = jnp.stack([y, x, spot]).astype(jnp.int32)
    tie = lax.optimization_barrier
    end = chips_z - 1
    mine = {0: lax.dynamic_index_in_dim(chip, x, 0, keepdims=False)}
    across, beside, corner = {}, {}, {}
    chip_beside = swap(chip, "y")
    acc = None
    for k in range(1, chips_z):
        mine[k] = lax.ppermute(mine[k - 1], "z", ring)
        if k == 1:
            tied = tie((mine[k], token, token_other, ints, ints_other))
            mine[k], token, token_other, ints, ints_other = tied
            ints_all = [ints] + [along_ctx(ints, d) for d in range(1, m)]
            bias, needs = pl.pallas_call(
                mask_kernel,
                out_shape=[
                    jax.ShapeDtypeStruct((count, m * count), jnp.float32),
                    jax.ShapeDtypeStruct((TILES,), jnp.int32),
                ],
                in_specs=[pl.BlockSpec(memory_space=pltpu.HBM)] * 3 + [whole] * m,
                out_specs=[whole, pl.BlockSpec(memory_space=pltpu.SMEM)],
                compiler_params=params,
                cost_estimate=pl.CostEstimate(
                    flops=MASK_COST, bytes_accessed=MASK_COST // 300, transcendentals=0
                ),
                name="mask",
            )(chip_beside, token, token_other, *ints_all)
        elif k > 2:
            if acc is None:
                acc = project([(0, True), (0, False)])
            if k == 3:
                mine[k], acc, bias = tie((mine[k], acc, bias))
            else:
                mine[k], acc = tie((mine[k], acc))
            acc = project([(k - 2, True)], acc, also=beside[k - 2])
        across[k], beside[k] = swap(mine[k], "x"), swap(mine[k], "y")
    for k in range(1, chips_z):
        if k < end:
            corner[k] = swap(beside[k], "x") if k % 2 else swap(across[k], "y")
    acc = project([(end - 1, True), (1, False)], acc, also=beside[end - 1], hint=HINT)
    beside[end], acc = tie((beside[end], acc))
    corner[end] = swap(beside[end], "x")

    where = jnp.concatenate([position[0], ints_other[1]]).astype(jnp.float32)
    half = HD // 2
    freq = np.exp(np.arange(half, dtype=np.float32) * np.float32(-2.0 * math.log(THETA) / HD))
    angle = where[:, None] * freq[None, :]
    cosine, sine = jnp.cos(angle), jnp.sin(angle)
    cosine = jnp.concatenate([cosine, cosine], axis=1)
    sine = jnp.concatenate([-sine, sine], axis=1)

    acc = project([(end, True)] + [(k, False) for k in range(2, end)], acc)
    kv_own, kv_other = project([(end, False)], acc, last=True)

    result = None
    for cross, kv in enumerate((kv_own, kv_other)):
        sources = [kv if d == 0 and not cross else along_ctx(kv, d, cross) for d in range(m)]

        def block(step, place, needs, cross=cross):
            return (0, lax.rem(place[0] + cross, 2) * 2 + step)

        earlier = [] if result is None else [result]
        result = pl.pallas_call(
            functools.partial(attend_kernel, m, count, cross),
            out_shape=jax.ShapeDtypeStruct((count, KVH * G * HD), bf16),
            grid_spec=pltpu.PrefetchScalarGridSpec(
                num_scalar_prefetch=2,
                grid=(2,),
                in_specs=[whole] * (2 + m)
                + [pl.BlockSpec(memory_space=pl.ANY)] * len(earlier),
                out_specs=pl.BlockSpec((count, G * HD), block),
                scratch_shapes=[
                    pltpu.VMEM((m * count, HD), bf16),
                    pltpu.VMEM((m * count, HD), bf16),
                ],
            ),
            input_output_aliases={4 + m: 0} if earlier else {},
            compiler_params=params,
            cost_estimate=pl.CostEstimate(
                flops=2 * count * m * count * KVH * G * HD,
                bytes_accessed=2 * count * KVH * G * HD,
                transcendentals=count * m * count * KVH * G // 2,
            ),
            name="attend",
        )(core.astype(jnp.int32)[None], needs, queries[0], bias, *sources, *earlier)
    return result[None]


def solution(mesh):
    n, m = mesh.shape["fsdp"], mesh.shape["ctx"]
    sizes = (n // 4, 2, 2, m // 2, 2)
    fine = Mesh(mesh.devices.reshape(sizes), ("z", "y", "core", "ctx", "x"))
    fsdp, ctx = ("z", "y", "core"), ("ctx", "x")
    placed = (
        P(fsdp, ctx, None),
        P(fsdp, ctx, None),
        P(),
        P(),
        P(fsdp, None),
        P(fsdp, None),
        P(fsdp, ctx),
        P(fsdp, ctx),
    )
    return jax.shard_map(
        functools.partial(on_device, sizes),
        mesh=fine,
        in_specs=placed,
        out_specs=P(fsdp, ctx, None),
        check_vma=False,
    )
```

```python
import functools
import math

import jax
import jax.numpy as jnp
import numpy as np
from jax import lax
from jax.experimental import pallas as pl
from jax.experimental.pallas import tpu as pltpu
from jax.sharding import Mesh
from jax.sharding import PartitionSpec as P

KVH = 4
HD = 128
G = 8
EPS = 1e-06
THETA = 1000000.0
MASKED = -1e30
VMEM_LIMIT = 16 * 2**20
NORM_ROWS = 64
WIDE = 4
TILES = 2
HINT = 8
MASK_COST = 1 * 10**9


def norm_kernel(chunks, hidden, gain, out, token, held, sems):
    steps = held.shape[0] // NORM_ROWS
    copies = []
    for i in range(steps):
        at = pl.ds(i * NORM_ROWS, NORM_ROWS)
        copies.append(pltpu.make_async_copy(hidden.at[at], held.at[at], sems.at[i]))
        copies[-1].start()
    for i, copy in enumerate(copies):
        copy.wait()
        at = pl.ds(i * NORM_ROWS, NORM_ROWS)
        inputs = held[at, :].astype(jnp.float32)
        scale = lax.rsqrt(jnp.mean(inputs * inputs, axis=-1, keepdims=True) + EPS)
        normed = (inputs * scale * gain[...]).astype(jnp.bfloat16)
        rows = normed.shape[1] // chunks
        for j in range(chunks):
            out[j, at, :] = normed[:, j * rows : (j + 1) * rows]
    token[...] = jnp.zeros_like(token)


def project_kernel(groups, alone, first, last, count, place, own, other, *rest):
    chips_z = own.shape[0] // 2
    y, x, spot = place[0], place[1], place[2]
    rest = list(rest) if alone else list(rest[1:])
    weight, lhs, sems = rest[-3:]
    waits = []
    for g, (k, near) in enumerate(groups):
        i = lax.rem(spot - k + chips_z, chips_z)
        chunk = (i ^ (i >> 1)) * 2 + (y if near else 1 - y)
        pairs = [
            (own.at[chunk], lhs.at[g, pl.ds(0, count)]),
            (other.at[chunk], lhs.at[g, pl.ds(count, count)]),
        ]
        if k == 0:
            pairs.append((rest.pop(0), weight.at[g]))
        else:
            pairs.append((rest.pop(0), weight.at[g, x]))
            pairs.append((rest.pop(0), weight.at[g, 1 - x]))
        copies = [
            pltpu.make_async_copy(source, target, sems.at[g, i])
            for i, (source, target) in enumerate(pairs)
        ]
        for copy in copies:
            copy.start()
        waits.append(copies)
    earlier = None if first else rest.pop(0)
    terms = [None, None]
    for g, copies in enumerate(waits):
        for copy in copies:
            copy.wait()
        for half in range(2):
            part = jnp.dot(lhs[g], weight[g, half], preferred_element_type=jnp.float32)
            terms[half] = part if terms[half] is None else terms[half] + part
    for half in range(2):
        if not first:
            terms[half] += earlier[half]
        if not last:
            rest[0][half] = terms[half]
    if not last:
        return
    cosine, sine, gain = rest[:3]
    outs = rest[3:5]
    for head in range(2):
        columns = slice(head * HD, (head + 1) * HD)
        for part, out in enumerate(outs):
            at = slice(part * count, (part + 1) * count)
            raw = terms[0][at, columns]
            normk = raw * lax.rsqrt(jnp.mean(raw * raw, axis=-1, keepdims=True) + EPS) * gain[...]
            turned = normk * cosine[at, :] + pltpu.roll(normk, HD // 2, 1) * sine[at, :]
            out[:, 2 * head * HD : (2 * head + 1) * HD] = turned.astype(jnp.bfloat16)
            out[:, (2 * head + 1) * HD : (2 * head + 2) * HD] = terms[1][at, columns].astype(
                jnp.bfloat16
            )


def mask_kernel(*refs):
    pieces, (bias, needs) = refs[3:-2], refs[-2:]
    count = bias.shape[0]
    size = count // TILES
    seg_q, pos_q = (
        jnp.transpose(jnp.broadcast_to(pieces[0][i : i + 1, :], (count, count))) for i in range(2)
    )
    width = len(pieces) * size
    for tile in range(TILES):
        for i, piece in enumerate(pieces):
            at = slice(tile * size, (tile + 1) * size)
            allowed = (piece[:1, at] == seg_q[:, at]) & (piece[1:, at] <= pos_q[:, at])
            there = tile * width + i * size
            bias[:, there : there + size] = jnp.where(allowed, 0.0, MASKED)
    for tile in range(TILES - 1):
        rows = slice(tile * size, (tile + 1) * size)
        needs[tile] = (jnp.max(bias[rows, (tile + 1) * width :]) == 0.0).astype(jnp.int32)
    needs[TILES - 1] = 0


def attend_kernel(pieces, count, cross, place, needs, queries, bias, *rest):
    sources, (out, keys, values) = rest[:pieces], rest[-3:]
    step = pl.program_id(0)
    base = (lax.rem(place[0] + cross, 2) * 2 + step) * G * HD
    tile_rows = count // TILES
    length = pieces * tile_rows

    for head in range(2):

        @pl.when(step == head)
        def _():
            left = 2 * head * HD
            for i, source in enumerate(sources):
                for tile in range(TILES):
                    here = slice(tile * tile_rows, (tile + 1) * tile_rows)
                    there = tile * length + i * tile_rows
                    keys[there : there + tile_rows, :] = source[here, left : left + HD]
                    values[there : there + tile_rows, :HD] = source[here, left + HD : left + 2 * HD]

    @pl.when(step == 0)
    def _():
        values[:, HD:] = jnp.ones((pieces * count, HD), jnp.bfloat16)

    factor = math.log2(math.e) / math.sqrt(HD)

    def tile_body(tile, high):
        rows = slice(tile * tile_rows, (tile + 1) * tile_rows)
        k, v, b = keys[:high, :], values[:high, :], bias[rows, :high]

        def score(part):
            columns = [
                pl.ds(pl.multiple_of(base + g * HD, HD), HD)
                for g in range(part * WIDE, (part + 1) * WIDE)
            ]
            q = jnp.concatenate([queries[rows, at] for at in columns], axis=0)
            return lax.dot_general(
                q, k, (((1,), (1,)), ((), ())), preferred_element_type=jnp.float32
            )

        ahead = score(0)
        for step in range(G // WIDE):
            scores = ahead.reshape(WIDE, tile_rows, high) + b[None]
            if step + 1 < G // WIDE:
                ahead = score(step + 1)
            top = jnp.max(scores, axis=-1, keepdims=True)
            weights = jnp.exp2((scores - top) * factor)
            summed = jnp.dot(
                weights.astype(jnp.bfloat16).reshape(WIDE * tile_rows, high),
                v,
                preferred_element_type=jnp.float32,
            )
            result = (summed[:, :HD] / summed[:, HD:]).astype(jnp.bfloat16)
            for i in range(WIDE):
                g = step * WIDE + i
                out[rows, g * HD : (g + 1) * HD] = result[i * tile_rows : (i + 1) * tile_rows]

    for tile in range(TILES):
        for need, high in ((0, tile + 1), (1, TILES)):

            @pl.when(needs[tile] == need)
            def _():
                tile_body(tile, high * length)


def swap(array, axis):
    return lax.ppermute(array, axis, [(0, 1), (1, 0)])


def on_device(
    sizes, hidden, queries, norm_gain, key_gain, k_weight, v_weight, segment, position
):
    chips_z, groups = sizes[0], sizes[3]
    count, width = hidden.shape[1:]
    own_rows = k_weight.shape[0]
    rows = 2 * own_rows
    chunks = 2 * chips_z
    m = 2 * groups
    z, y = lax.axis_index("z"), lax.axis_index("y")
    core, x = lax.axis_index("core"), lax.axis_index("x")
    bf16 = jnp.bfloat16
    whole = pl.BlockSpec(memory_space=pltpu.VMEM)
    params = pltpu.CompilerParams(vmem_limit_bytes=VMEM_LIMIT)

    def along_ctx(array, d, cross=False):
        pairs = []
        for c in range(2):
            for i in range(m):
                pairs.append((c * m + i, (c ^ int(cross)) * m + (i + d) % m))
        return lax.ppermute(array, ("core", "ctx", "x"), pairs)

    def columns(which):
        at = which * 2 * HD
        return jnp.stack(
            [lax.dynamic_slice_in_dim(w, at, 2 * HD, 1) for w in (k_weight, v_weight)]
        )

    taken = swap(columns(1 - core), "core")
    kept = columns(core)
    chip = lax.dynamic_update_slice(
        jnp.zeros((2, rows, 2 * HD), bf16), kept, (0, core * own_rows, 0)
    )
    chip = lax.dynamic_update_slice(chip, taken, (0, (1 - core) * own_rows, 0))
    hidden, segment, position, chip = lax.optimization_barrier((hidden, segment, position, chip))

    def norm(array):
        return pl.pallas_call(
            functools.partial(norm_kernel, chunks),
            out_shape=[
                jax.ShapeDtypeStruct((chunks, count, rows), bf16),
                jax.ShapeDtypeStruct((8, 128), jnp.float32),
            ],
            in_specs=[pl.BlockSpec(memory_space=pltpu.HBM), whole],
            out_specs=[whole] * 2,
            scratch_shapes=[
                pltpu.VMEM((count, width), bf16),
                pltpu.SemaphoreType.DMA((count // NORM_ROWS,)),
            ],
            compiler_params=params,
            cost_estimate=pl.CostEstimate(
                flops=4 * count * width, bytes_accessed=4 * count * width, transcendentals=0
            ),
            name="norm",
        )(array[0], norm_gain[None])

    normed, token = norm(hidden)
    normed_other, token_other = norm(swap(hidden, "core"))
    ints = jnp.concatenate([segment, position])
    ints_other = swap(ints, "core")

    acc_shape = jax.ShapeDtypeStruct((2, 2 * count, 2 * HD), jnp.float32)
    kv_shape = jax.ShapeDtypeStruct((count, 4 * HD), bf16)

    def project(groups, acc=None, last=False, also=None, hint=1):
        arrays = [] if also is None else [also]
        for k, near in groups:
            if k == 0:
                arrays.append(chip if near else chip_beside)
            else:
                arrays += [mine[k], across[k]] if near else [beside[k], corner[k]]
        accs = [] if acc is None else [acc]
        outs = pl.pallas_call(
            functools.partial(project_kernel, groups, also is None, acc is None, last, count),
            out_shape=[kv_shape] * 2 if last else [acc_shape],
            in_specs=[pl.BlockSpec(memory_space=pltpu.SMEM)]
            + [pl.BlockSpec(memory_space=pltpu.HBM)] * (2 + len(arrays))
            + [whole] * (len(accs) + (3 if last else 0)),
            out_specs=[whole] * (2 if last else 1),
            scratch_shapes=[
                pltpu.VMEM((len(groups), 2, rows, 2 * HD), bf16),
                pltpu.VMEM((len(groups), 2 * count, rows), bf16),
                pltpu.SemaphoreType.DMA((len(groups), 4)),
            ],
            compiler_params=params,
            cost_estimate=pl.CostEstimate(
                flops=hint * 2 * 2 * count * rows * 4 * HD * len(groups),
                bytes_accessed=hint * 2 * rows * (4 * HD + 2 * count) * len(groups),
                transcendentals=0,
            ),
            name="project",
        )(
            place, normed, normed_other, *arrays, *accs,
            *((cosine, sine, key_gain[None]) if last else ()),
        )
        return outs if last else outs[0]

    order = [i ^ (i >> 1) for i in range(chips_z)]
    ring = [(order[i], order[(i + 1) % chips_z]) for i in range(chips_z)]
    spot = sum(jnp.where(z == order[i], i, 0) for i in range(chips_z))
    place = jnp.stack([y, x, spot]).astype(jnp.int32)
    tie = lax.optimization_barrier
    end = chips_z - 1
    mine = {0: lax.dynamic_index_in_dim(chip, x, 0, keepdims=False)}
    across, beside, corner = {}, {}, {}
    chip_beside = swap(chip, "y")
    acc = None
    for k in range(1, chips_z):
        mine[k] = lax.ppermute(mine[k - 1], "z", ring)
        if k == 1:
            tied = tie((mine[k], token, token_other, ints, ints_other))
            mine[k], token, token_other, ints, ints_other = tied
            ints_all = [ints] + [along_ctx(ints, d) for d in range(1, m)]
            bias, needs = pl.pallas_call(
                mask_kernel,
                out_shape=[
                    jax.ShapeDtypeStruct((count, m * count), jnp.float32),
                    jax.ShapeDtypeStruct((TILES,), jnp.int32),
                ],
                in_specs=[pl.BlockSpec(memory_space=pltpu.HBM)] * 3 + [whole] * m,
                out_specs=[whole, pl.BlockSpec(memory_space=pltpu.SMEM)],
                compiler_params=params,
                cost_estimate=pl.CostEstimate(
                    flops=MASK_COST, bytes_accessed=MASK_COST // 300, transcendentals=0
                ),
                name="mask",
            )(chip_beside, token, token_other, *ints_all)
        elif k > 2:
            if acc is None:
                acc = project([(0, True), (0, False)])
            if k == 3:
                mine[k], acc, bias = tie((mine[k], acc, bias))
            else:
                mine[k], acc = tie((mine[k], acc))
            acc = project([(k - 2, True)], acc, also=beside[k - 2])
        across[k], beside[k] = swap(mine[k], "x"), swap(mine[k], "y")
    for k in range(1, chips_z):
        if k < end:
            corner[k] = swap(beside[k], "x") if k % 2 else swap(across[k], "y")
    acc = project([(end - 1, True), (1, False)], acc, also=beside[end - 1], hint=HINT)
    beside[end], acc = tie((beside[end], acc))
    corner[end] = swap(beside[end], "x")

    where = jnp.concatenate([position[0], ints_other[1]]).astype(jnp.float32)
    half = HD // 2
    freq = np.exp(np.arange(half, dtype=np.float32) * np.float32(-2.0 * math.log(THETA) / HD))
    angle = where[:, None] * freq[None, :]
    cosine, sine = jnp.cos(angle), jnp.sin(angle)
    cosine = jnp.concatenate([cosine, cosine], axis=1)
    sine = jnp.concatenate([-sine, sine], axis=1)

    acc = project([(end, True)] + [(k, False) for k in range(2, end)], acc)
    kv_own, kv_other = project([(end, False)], acc, last=True)

    result = None
    for cross, kv in enumerate((kv_own, kv_other)):
        sources = [kv if d == 0 and not cross else along_ctx(kv, d, cross) for d in range(m)]

        def block(step, place, needs, cross=cross):
            return (0, lax.rem(place[0] + cross, 2) * 2 + step)

        earlier = [] if result is None else [result]
        result = pl.pallas_call(
            functools.partial(attend_kernel, m, count, cross),
            out_shape=jax.ShapeDtypeStruct((count, KVH * G * HD), bf16),
            grid_spec=pltpu.PrefetchScalarGridSpec(
                num_scalar_prefetch=2,
                grid=(2,),
                in_specs=[whole] * (2 + m)
                + [pl.BlockSpec(memory_space=pl.ANY)] * len(earlier),
                out_specs=pl.BlockSpec((count, G * HD), block),
                scratch_shapes=[
                    pltpu.VMEM((m * count, HD), bf16),
                    pltpu.VMEM((m * count, 2 * HD), bf16),
                ],
            ),
            input_output_aliases={4 + m: 0} if earlier else {},
            compiler_params=params,
            cost_estimate=pl.CostEstimate(
                flops=2 * count * m * count * KVH * G * HD,
                bytes_accessed=2 * count * KVH * G * HD,
                transcendentals=count * m * count * KVH * G // 2,
            ),
            name="attend",
        )(core.astype(jnp.int32)[None], needs, queries[0], bias, *sources, *earlier)
    return result[None]


def solution(mesh):
    n, m = mesh.shape["fsdp"], mesh.shape["ctx"]
    sizes = (n // 4, 2, 2, m // 2, 2)
    fine = Mesh(mesh.devices.reshape(sizes), ("z", "y", "core", "ctx", "x"))
    fsdp, ctx = ("z", "y", "core"), ("ctx", "x")
    placed = (
        P(fsdp, ctx, None),
        P(fsdp, ctx, None),
        P(),
        P(),
        P(fsdp, None),
        P(fsdp, None),
        P(fsdp, ctx),
        P(fsdp, ctx),
    )
    return jax.shard_map(
        functools.partial(on_device, sizes),
        mesh=fine,
        in_specs=placed,
        out_specs=P(fsdp, ctx, None),
        check_vma=False,
    )
```
